32 devices in a mesh: ctx: 8 (over y, x, core), fsdp: 4 (over z).
Axes of the slice: x: 2, y: 2, z: 4, core: 2. Of those that a mesh axis runs over, the one named last changes fastest.
Arguments:
- block_in: bfloat16 [4, 2048, 1024], P('fsdp', 'ctx'), may hold values from -6 to 6
- out_grad: bfloat16 [4, 2048, 1024], P('fsdp', 'ctx'), may hold values from -6 to 6
- ln1_gain: bfloat16 [1024], P('fsdp'), may hold values from 0.25 to 1.75
- ln1_shift: bfloat16 [1024], P('fsdp'), may hold values from -4 to 4
- qkv_weight: bfloat16 [1024, 3072], P('fsdp'), may hold values from -0.1875 to 0.1875
- query_bias: bfloat16 [1024], P('fsdp'), may hold values from -4 to 4
- value_bias: bfloat16 [1024], P('fsdp'), may hold values from -4 to 4
- proj_weight: bfloat16 [1024, 1024], P('fsdp'), may hold values from -0.75 to 0.75
- proj_bias: bfloat16 [1024], P('fsdp'), may hold values from -4 to 4
- ln2_gain: bfloat16 [1024], P('fsdp'), may hold values from 0.25 to 1.75
- ln2_shift: bfloat16 [1024], P('fsdp'), may hold values from -4 to 4
- up_weight: bfloat16 [1024, 4096], P('fsdp'), may hold values from -0.1875 to 0.1875
- up_bias: bfloat16 [4096], P('fsdp'), may hold values from -4 to 4
- down_weight: bfloat16 [4096, 1024], P('fsdp'), may hold values from -0.09375 to 0.09375
- down_bias: bfloat16 [1024], P('fsdp'), may hold values from -4 to 4
Outputs:
- block_out: bfloat16 [4, 2048, 1024], P('fsdp', 'ctx')
- d_input: float32 [4, 2048, 1024], P('fsdp', 'ctx')
- d_ln1_gain: float32 [1024], P('fsdp')
- d_ln1_shift: float32 [1024], P('fsdp')
- d_qkv_weight: float32 [1024, 3072], P('fsdp')
- d_query_bias: float32 [1024], P('fsdp')
- d_value_bias: float32 [1024], P('fsdp')
- d_proj_weight: float32 [1024, 1024], P('fsdp')
- d_proj_bias: float32 [1024], P('fsdp')
- d_ln2_gain: float32 [1024], P('fsdp')
- d_ln2_shift: float32 [1024], P('fsdp')
- d_up_weight: float32 [1024, 4096], P('fsdp')
- d_up_bias: float32 [4096], P('fsdp')
- d_down_weight: float32 [4096, 1024], P('fsdp')
- d_down_bias: float32 [1024], P('fsdp')
The draws below stay inside these ranges and needn't reach their ends.
All inputs are finite; a program needn't handle non-finite values.
Results may differ from the reference program's by a relative error of at most 0.02.
Values may be sent and summed in bfloat16 or wider, within the bound.
No kernel may reach another device: no remote copies, remote signals or barrier semaphores. Data moves between devices by JAX's collectives and lax.ppermute only.
A program may use at most 256 MiB of HBM per device.

```python
import jax
import jax.numpy as jnp
from jax import lax

D = 1024
HEADS = 16
HEAD_DIM = 64
FF = 4096
SEQS = 4
LEN = 2048


def block_levels(key, shape, pieces, least, largest):
    def one(axis_at, blocks):
        heights = jax.random.uniform(jax.random.fold_in(jax.random.fold_in(key, 6), axis_at), (blocks,), jnp.float32, least / len(pieces), largest / len(pieces))
        return jnp.repeat(jnp.exp(heights), shape[axis_at] // blocks).reshape((-1,) + (1,) * (len(shape) - axis_at - 1))

    loudness = one(*pieces[0])
    for cut in pieces[1:]:
        loudness = loudness * one(*cut)
    return loudness


def normal_values(key, shape, scale, most, split=(), kind=jnp.bfloat16):
    values = scale * jax.random.normal(key, shape, jnp.float32)
    if split:
        values = values * block_levels(key, shape, split, -0.22, 0.18)
    return jnp.clip(values, -most, most).astype(kind)


def setup_inputs(seed: int = 0) -> dict:
    keys = jax.random.split(jax.random.key(seed), 16)
    return {
        "block_in": normal_values(keys[0], (SEQS, LEN, D), 1.0, 6.0, ((0, 4), (1, 8))),
        "out_grad": normal_values(keys[1], (SEQS, LEN, D), 1.0, 6.0, ((0, 4), (1, 8))),
        "ln1_gain": jnp.clip(1.0 + 0.15 * jax.random.normal(keys[2], (D,), jnp.float32), 0.25, 1.75).astype(jnp.bfloat16),
        "ln1_shift": normal_values(keys[3], (D,), 0.3, 4.0, ((0, 4),)),
        "qkv_weight": normal_values(keys[4], (D, 3 * D), D ** -0.5, 0.1875, ((0, 4),)),
        "query_bias": normal_values(keys[5], (D,), 0.3, 4.0, ((0, 4),)),
        "value_bias": normal_values(keys[6], (D,), 0.3, 4.0, ((0, 4),)),
        "proj_weight": normal_values(keys[7], (D, D), (D // 16) ** -0.5, 0.75, ((0, 4),)),
        "proj_bias": normal_values(keys[8], (D,), 0.3, 4.0, ((0, 4),)),
        "ln2_gain": jnp.clip(1.0 + 0.15 * jax.random.normal(keys[9], (D,), jnp.float32), 0.25, 1.75).astype(jnp.bfloat16),
        "ln2_shift": normal_values(keys[10], (D,), 0.3, 4.0, ((0, 4),)),
        "up_weight": normal_values(keys[11], (D, FF), D ** -0.5, 0.1875, ((0, 4),)),
        "up_bias": normal_values(keys[12], (FF,), 0.3, 4.0, ((0, 4),)),
        "down_weight": normal_values(keys[13], (FF, D), FF ** -0.5, 0.09375, ((0, 4),)),
        "down_bias": normal_values(keys[14], (D,), 0.3, 4.0, ((0, 4),)),
    }


EPSILON = 1e-05
GELU_COEF = 0.7978845608028654
MASKED = -1e+30

@jax.custom_vjp
def low(v):
    return lax.optimization_barrier(v.astype(jnp.bfloat16)).astype(jnp.float32)

@jax.custom_vjp
def low_back(v):
    return v

def low_keep(v):
    return (low(v), None)

def low_pass(kept, grad):
    return (grad,)

def back_keep(v):
    return (v, None)

def back_low(kept, grad):
    return (low(grad),)
low.defvjp(low_keep, low_pass)
low_back.defvjp(back_keep, back_low)

def matmul(left, right):
    return jnp.dot(left, right, precision=lax.Precision.HIGHEST, preferred_element_type=jnp.float32)

def layer_norm(values, gain_vec, shift_vec):
    center = values - lax.optimization_barrier(jnp.mean(values, -1, keepdims=True))
    spread = lax.optimization_barrier(jnp.mean(center * center, -1, keepdims=True))
    return center * lax.rsqrt(spread + EPSILON) * gain_vec + shift_vec

def gelu_tanh(values):
    return 0.5 * values * (1.0 + jnp.tanh(GELU_COEF * (values + 0.044715 * values * values * values)))

def seq_layer(sequence, weights):
    gain_one, shift_one, qkv_full, qbias_full, vbias_full, proj_full, pbias_full, gain_two, shift_two, up_full, ubias_full, down_full, dbias_full = weights
    seq_len = sequence.shape[0]
    attn_scale = HEAD_DIM ** (-0.5)
    normed = low(layer_norm(sequence, gain_one, shift_one))
    projected = matmul(normed, qkv_full)
    queries = low(low_back(projected[:, :D] + qbias_full))
    keys_all = low(low_back(projected[:, D:2 * D]))
    values_all = low(low_back(projected[:, 2 * D:] + vbias_full))
    block_rows = min(512, seq_len)
    block_count = seq_len // block_rows
    query_blocks = queries.reshape(block_count, block_rows, HEADS, HEAD_DIM)
    key_heads = keys_all.reshape(seq_len, HEADS, HEAD_DIM)
    value_heads = values_all.reshape(seq_len, HEADS, HEAD_DIM)
    key_pos = jnp.arange(seq_len, dtype=jnp.int32)

    def query_block(pair):
        query_blk, start = pair
        scores = jnp.einsum('qhd,khd->hqk', query_blk, key_heads, precision=lax.Precision.HIGHEST)
        scores = low_back(scores * attn_scale)
        query_pos = start + jnp.arange(block_rows, dtype=jnp.int32)
        allowed = key_pos[None, :] <= query_pos[:, None]
        scores = jnp.where(allowed[None], scores, MASKED)
        probs = low(jax.nn.softmax(scores, axis=-1))
        result = jnp.einsum('hqk,khd->qhd', probs, value_heads, precision=lax.Precision.HIGHEST)
        return low(low_back(result))
    starts = (jnp.arange(block_count, dtype=jnp.int32) * block_rows).astype(jnp.int32)
    attn_out = lax.map(jax.checkpoint(query_block), (query_blocks, starts)).reshape(seq_len, D)
    resid_one = sequence + low_back(matmul(attn_out, proj_full) + pbias_full)
    normed_two = low(layer_norm(resid_one, gain_two, shift_two))
    pre_act = low_back(matmul(normed_two, up_full) + ubias_full)
    hidden = low(gelu_tanh(pre_act))
    return resid_one + low_back(matmul(hidden, down_full) + dbias_full)

def reference(block_in, out_grad, ln1_gain, ln1_shift, qkv_weight, query_bias, value_bias, proj_weight, proj_bias, ln2_gain, ln2_shift, up_weight, up_bias, down_weight, down_bias):
    params = tuple((item.astype(jnp.float32) for item in (ln1_gain, ln1_shift, qkv_weight, query_bias, value_bias, proj_weight, proj_bias, ln2_gain, ln2_shift, up_weight, up_bias, down_weight, down_bias)))

    def forward(inputs, weights):

        def one_seq(sequence):
            return seq_layer(sequence, weights)
        return lax.map(jax.checkpoint(one_seq), inputs)
    outputs, pull = jax.vjp(forward, block_in.astype(jnp.float32), params)
    d_inputs, grads = pull(out_grad.astype(jnp.float32))
    return (outputs.astype(jnp.bfloat16), d_inputs, grads[0], grads[1], grads[2], grads[3], grads[4], grads[5], grads[6], grads[7], grads[8], grads[9], grads[10], grads[11], grads[12])
```

```python
import functools
import math

import jax
import jax.numpy as jnp
from jax import lax
from jax.experimental import pallas as pl
from jax.experimental.pallas import tpu as pltpu
from jax.sharding import PartitionSpec as P

HEADS = 16
HEAD_DIM = 64

EPSILON = 1e-05
GELU_COEF = 0.7978845608028654
MASKED = -1e30
SCORE_SCALE = HEAD_DIM ** (-0.5)
EXP2_SCALE = SCORE_SCALE / math.log(2.0)
F32 = jnp.float32
BF16 = jnp.bfloat16


def layer_norm(values, gain_vec, shift_vec):
    center = values - jnp.mean(values, -1, keepdims=True)
    spread = jnp.mean(center * center, -1, keepdims=True)
    return center * lax.rsqrt(spread + EPSILON) * gain_vec + shift_vec


def gelu_tanh(values):
    return (
        0.5 * values * (1.0 + jnp.tanh(GELU_COEF * (values + 0.044715 * values * values * values)))
    )


def contract_rows(left, right):
    return lax.dot_general(left, right, (((0,), (0,)), ((), ())), preferred_element_type=F32)


def times_trans(left, right):
    return lax.dot_general(left, right, (((1,), (1,)), ((), ())), preferred_element_type=F32)


def times(left, right):
    return jnp.dot(left, right, preferred_element_type=F32)


def ctx_swap(value, bits):
    size = lax.axis_size("ctx")
    return lax.ppermute(value, "ctx", [(at, at ^ bits) for at in range(size)])


def ctx_base():
    return lax.axis_index("ctx") if lax.axis_size("ctx") == 8 else jnp.int32(0)


def ctx_gather(block):
    if lax.axis_size("ctx") != 8:
        return lax.all_gather(block, "ctx", axis=0)
    half = block.shape[0] // 2
    by_x = ctx_swap(block, 2)
    by_y = ctx_swap(block, 4)
    own_pair = ctx_swap(block, 1)
    diag = jnp.concatenate([ctx_swap(by_y[:half], 2), ctx_swap(by_x[half:], 4)])
    pair_x = ctx_swap(by_x, 1)
    pair_y = ctx_swap(by_y, 1)
    pair_diag = ctx_swap(diag, 1)
    return jnp.stack([block, own_pair, by_x, pair_x, by_y, pair_y, diag, pair_diag])


def ctx_scatter(blocks):
    if lax.axis_size("ctx") != 8:
        return lax.psum_scatter(blocks, "ctx", scatter_dimension=0, tiled=False).astype(F32)
    kept = blocks[0::2]
    pairs = kept + ctx_swap(blocks[1::2], 1)
    parts = [pairs[0]] + [ctx_swap(pairs[m], 2 * m) for m in (1, 2, 3)]
    return sum(part.astype(F32) for part in parts)


def depth_gather(block):
    size = lax.axis_size("fsdp")
    if size != 4:
        return lax.all_gather(block, "fsdp", axis=0)
    here = lax.axis_index("fsdp")
    out = jnp.zeros((size,) + block.shape, block.dtype)
    for step in range(size):
        part = block
        if step:
            part = lax.ppermute(block, "fsdp", [(at, (at + step) % size) for at in range(size)])
        out = lax.dynamic_update_index_in_dim(out, part, lax.rem(here - step + size, size), 0)
    return out


def depth_scatter(blocks):
    size = lax.axis_size("fsdp")
    if size != 4:
        return lax.psum_scatter(blocks, "fsdp", scatter_dimension=0, tiled=False).astype(F32)
    here = lax.axis_index("fsdp")
    total = lax.dynamic_index_in_dim(blocks, here, 0, False).astype(F32)
    for step in range(1, size):
        part = lax.dynamic_index_in_dim(blocks, lax.rem(here + step, size), 0, False)
        part = lax.ppermute(part, "fsdp", [(at, (at + step) % size) for at in range(size)])
        total = total + part.astype(F32)
    return total


def swap_place(base_ref, block):
    return jnp.bitwise_xor(base_ref[0], block)


def causal(rows, columns):
    keys = lax.broadcasted_iota(jnp.int32, (rows, columns), 0)
    queries = lax.broadcasted_iota(jnp.int32, (rows, columns), 1)
    return keys <= queries


def attend_kernel(
    blocks, tile, base_ref, qkv_ref, out_ref, out_t_ref, log_ref, q_ref, k_ref, v_t_ref
):
    length, width = out_ref.shape
    heads = width // HEAD_DIM
    rows = length // blocks
    for block in range(blocks):
        place = pl.multiple_of(swap_place(base_ref, block) * rows, rows)
        part = qkv_ref[block * rows : (block + 1) * rows, :]
        for head in range(heads):
            low, high = head * HEAD_DIM, (head + 1) * HEAD_DIM
            q_ref[head, pl.ds(place, rows), :] = part[:, low:high]
            k_ref[head, pl.ds(place, rows), :] = part[:, width + low : width + high]
        v_t_ref[:, pl.ds(place, rows)] = part[:, 2 * width :].T
    for q_tile in range(length // tile):
        columns = slice(q_tile * tile, (q_tile + 1) * tile)
        queries = [q_ref[head, columns, :] for head in range(heads)]

        def visit(k_tile, state, masked):
            start = pl.multiple_of(k_tile * tile, tile)
            result = []
            for head in range(heads):
                run_max, run_sum, run_acc = state[head]
                scores = times_trans(k_ref[head, pl.ds(start, tile), :], queries[head])
                if masked:
                    scores = jnp.where(causal(tile, tile), scores, MASKED)
                new_max = jnp.maximum(run_max, jnp.max(scores, 0, keepdims=True))
                weights = jnp.exp2(scores * EXP2_SCALE - new_max * EXP2_SCALE)
                factor = jnp.exp2((run_max - new_max) * EXP2_SCALE)
                new_sum = run_sum * factor + jnp.sum(weights, 0, keepdims=True)
                low, high = head * HEAD_DIM, (head + 1) * HEAD_DIM
                values = v_t_ref[low:high, pl.ds(start, tile)]
                new_acc = run_acc * factor + times(values, weights.astype(BF16))
                result.append((new_max, new_sum, new_acc))
            return result

        state = [
            (
                jnp.full((1, tile), MASKED, F32),
                jnp.zeros((1, tile), F32),
                jnp.zeros((HEAD_DIM, tile), F32),
            )
        ] * heads
        if q_tile:
            state = lax.fori_loop(0, q_tile, lambda at, st: visit(at, st, False), state)
        state = visit(q_tile, state, True)
        result = []
        for head in range(heads):
            run_max, run_sum, run_acc = state[head]
            result.append(run_acc / run_sum)
            log_ref[head : head + 1, columns] = run_max * EXP2_SCALE + jnp.log2(run_sum)
        result = jnp.concatenate(result, 0) if heads > 1 else result[0]
        out_t_ref[:, columns] = result
        out_ref[columns, :] = result.T.astype(BF16)


def attend_grad_kernel(
    blocks,
    tile,
    base_ref,
    qkv_ref,
    d_out_ref,
    out_t_ref,
    log_ref,
    d_qkv_ref,
    q_ref,
    k_ref,
    v_ref,
    k_t_ref,
    do_ref,
    delta_ref,
    dq_t_ref,
    dk_ref,
    dv_ref,
):
    length, width = d_out_ref.shape
    heads = width // HEAD_DIM
    rows = length // blocks
    for block in range(blocks):
        place = pl.multiple_of(swap_place(base_ref, block) * rows, rows)
        part = qkv_ref[block * rows : (block + 1) * rows, :]
        for head in range(heads):
            low, high = head * HEAD_DIM, (head + 1) * HEAD_DIM
            q_ref[head, pl.ds(place, rows), :] = part[:, low:high]
            k_ref[head, pl.ds(place, rows), :] = part[:, width + low : width + high]
            v_ref[head, pl.ds(place, rows), :] = part[:, 2 * width + low : 2 * width + high]
        k_t_ref[:, pl.ds(place, rows)] = part[:, width : 2 * width].T
        here = slice(block * rows, (block + 1) * rows)
        d_out = d_out_ref[here, :]
        product = d_out.astype(F32).T * out_t_ref[:, here]
        for head in range(heads):
            low, high = head * HEAD_DIM, (head + 1) * HEAD_DIM
            do_ref[head, here, :] = d_out[:, low:high]
            delta_ref[head : head + 1, here] = jnp.sum(product[low:high], 0, keepdims=True)
    dq_t_ref[...] = jnp.zeros_like(dq_t_ref)
    tiles = length // tile
    for k_tile in range(tiles):
        key_rows = slice(k_tile * tile, (k_tile + 1) * tile)

        def visit(q_tile, state, masked):
            start = pl.multiple_of(q_tile * tile, tile)
            query_rows = pl.ds(start, tile)
            result = []
            for head in range(heads):
                d_key, d_value = state[head]
                low, high = head * HEAD_DIM, (head + 1) * HEAD_DIM
                queries = q_ref[head, query_rows, :]
                d_out = do_ref[head, query_rows, :]
                scores = times_trans(k_ref[head, key_rows, :], queries)
                log_row = log_ref[head : head + 1, query_rows]
                probs = jnp.exp2(scores * EXP2_SCALE - log_row)
                if masked:
                    probs = jnp.where(causal(tile, tile), probs, 0.0)
                d_probs = times_trans(v_ref[head, key_rows, :], d_out)
                d_scores = (probs * (d_probs - delta_ref[head : head + 1, query_rows])).astype(BF16)
                d_value = d_value + times(probs.astype(BF16), d_out)
                d_key = d_key + times(d_scores, queries)
                dq_t_ref[low:high, query_rows] += times(k_t_ref[low:high, key_rows], d_scores)
                result.append((d_key, d_value))
            return result

        state = [(jnp.zeros((tile, HEAD_DIM), F32), jnp.zeros((tile, HEAD_DIM), F32))] * heads
        state = visit(k_tile, state, True)
        if k_tile + 1 < tiles:
            state = lax.fori_loop(k_tile + 1, tiles, lambda at, st: visit(at, st, False), state)
        for head in range(heads):
            dk_ref[head, key_rows, :] = state[head][0]
            dv_ref[head, key_rows, :] = state[head][1]
    for block in range(blocks):
        here = slice(block * rows, (block + 1) * rows)
        place = pl.ds(pl.multiple_of(swap_place(base_ref, block) * rows, rows), rows)
        d_key = [dk_ref[head, here, :] * SCORE_SCALE for head in range(heads)]
        d_value = [dv_ref[head, here, :] for head in range(heads)]
        parts = [dq_t_ref[:, here].T * SCORE_SCALE] + d_key + d_value
        d_qkv_ref[place, :] = jnp.concatenate(parts, 1).astype(BF16)


def attend(base, qkv, blocks):
    length, width = qkv.shape[0], qkv.shape[1] // 3
    heads = width // HEAD_DIM
    tile = min(512, length)
    return pl.pallas_call(
        functools.partial(attend_kernel, blocks, tile),
        out_shape=(
            jax.ShapeDtypeStruct((length, width), BF16),
            jax.ShapeDtypeStruct((width, length), F32),
            jax.ShapeDtypeStruct((heads, length), F32),
        ),
        in_specs=[
            pl.BlockSpec(memory_space=pltpu.SMEM),
            pl.BlockSpec(memory_space=pltpu.VMEM),
        ],
        out_specs=(pl.BlockSpec(memory_space=pltpu.VMEM),) * 3,
        scratch_shapes=[
            pltpu.VMEM((heads, length, HEAD_DIM), BF16),
            pltpu.VMEM((heads, length, HEAD_DIM), BF16),
            pltpu.VMEM((width, length), BF16),
        ],
        compiler_params=pltpu.CompilerParams(vmem_limit_bytes=40 << 20),
        cost_estimate=pl.CostEstimate(
            flops=2 * length * length * width,
            bytes_accessed=length * width * 12,
            transcendentals=heads * length * length // 2,
        ),
        name="attend",
    )(base, qkv)


def attend_grad(base, qkv, d_out, out_t, log_total, blocks):
    length, width = d_out.shape
    heads = width // HEAD_DIM
    tile = min(512, length)
    per_head = pltpu.VMEM((heads, length, HEAD_DIM), BF16)
    return pl.pallas_call(
        functools.partial(attend_grad_kernel, blocks, tile),
        out_shape=jax.ShapeDtypeStruct((length, 3 * width), BF16),
        in_specs=[pl.BlockSpec(memory_space=pltpu.SMEM)]
        + [pl.BlockSpec(memory_space=pltpu.VMEM)] * 4,
        out_specs=pl.BlockSpec(memory_space=pltpu.VMEM),
        scratch_shapes=[
            per_head,
            per_head,
            per_head,
            pltpu.VMEM((width, length), BF16),
            per_head,
            pltpu.VMEM((heads, length), F32),
            pltpu.VMEM((width, length), F32),
            pltpu.VMEM((heads, length, HEAD_DIM), F32),
            pltpu.VMEM((heads, length, HEAD_DIM), F32),
        ],
        compiler_params=pltpu.CompilerParams(vmem_limit_bytes=40 << 20),
        cost_estimate=pl.CostEstimate(
            flops=5 * length * length * width,
            bytes_accessed=length * width * 20,
            transcendentals=heads * length * length // 2,
        ),
        name="attend_grad",
    )(base, qkv, d_out, out_t, log_total)


def shards(
    block_in,
    out_grad,
    ln1_gain,
    ln1_shift,
    qkv_weight,
    query_bias,
    value_bias,
    proj_weight,
    proj_bias,
    ln2_gain,
    ln2_shift,
    up_weight,
    up_bias,
    down_weight,
    down_bias,
):
    seq_count, blk_len, model_dim = block_in.shape
    ctx_size, depth = lax.axis_size("ctx"), lax.axis_size("fsdp")
    ctx_index = lax.axis_index("ctx")
    base = ctx_base().reshape(1)
    seq_len = ctx_size * blk_len
    width = model_dim // ctx_size
    part = model_dim // depth
    hidden_part = up_bias.shape[0] // ctx_size
    hidden = hidden_part * depth

    own_in = block_in.reshape(blk_len, model_dim)
    own_dy = out_grad.reshape(blk_len, model_dim)

    def ctx_columns(value, columns, axis):
        return lax.dynamic_slice_in_dim(value, ctx_index * columns, columns, axis)

    qkv_slice = ctx_columns(qkv_weight.reshape(part, 3, model_dim), width, 2)
    vectors = [
        ln1_gain,
        ln1_shift,
        query_bias,
        value_bias,
        proj_bias,
        ln2_gain,
        ln2_shift,
        down_bias,
    ]
    first = jnp.concatenate(
        [qkv_slice.reshape(-1, 3 * width)]
        + [jnp.concatenate(vectors + [up_bias]).reshape(-1, 3 * width)]
    )
    first = depth_gather(first)
    qkv_full = first[:, :part].reshape(model_dim, 3 * width)
    vectors_full = first[:, part:].reshape(depth, -1).astype(F32)
    vectors_full, ubias_full = vectors_full[:, : 8 * part], vectors_full[:, 8 * part :]
    vectors_full = vectors_full.reshape(depth, 8, part).transpose(1, 0, 2).reshape(8, model_dim)
    gain_one, shift_one, qbias, vbias, pbias, gain_two, shift_two, dbias = vectors_full
    ubias = ctx_columns(ubias_full, hidden_part, 1).reshape(hidden)
    qkv_bias = jnp.concatenate(
        [ctx_columns(qbias, width, 0), jnp.zeros((width,), F32), ctx_columns(vbias, width, 0)]
    )

    all_in = ctx_gather(own_in).reshape(seq_len, model_dim)
    up_slice = lax.dynamic_index_in_dim(
        up_weight.reshape(part, depth, ctx_size, hidden_part), ctx_index, 2, False
    ).reshape(part, hidden)
    down_slice = ctx_columns(down_weight, hidden_part, 0)
    second = depth_gather(jnp.concatenate([up_slice, down_slice.reshape(-1, hidden)]))
    up_full = second[:, :part].reshape(model_dim, hidden)
    down_full = second[:, part:].reshape(hidden, model_dim)
    proj_rows = part // ctx_size
    proj_full = lax.all_gather(
        ctx_columns(proj_weight, proj_rows, 0), ("fsdp", "ctx"), axis=0, tiled=True
    )
    all_dy = ctx_gather(own_dy).reshape(seq_len, model_dim)

    normed = layer_norm(all_in.astype(F32), gain_one, shift_one).astype(BF16)
    qkv = (times(normed, qkv_full) + qkv_bias).astype(BF16)
    attn_heads, attn_trans, log_total = attend(base, qkv, ctx_size)
    attn_low = lax.all_to_all(
        attn_heads.reshape(ctx_size, blk_len, width), "ctx", 0, 0, tiled=False
    )
    attn_low = attn_low.transpose(1, 0, 2).reshape(blk_len, model_dim)

    own_f = own_in.astype(F32)
    resid_one = own_f + times(attn_low, proj_full) + pbias
    normed_two = layer_norm(resid_one, gain_two, shift_two).astype(BF16)

    all_two = ctx_gather(normed_two).reshape(seq_len, model_dim)
    pre_act = times(all_two, up_full) + ubias
    gelu_out, gelu_pull = jax.vjp(gelu_tanh, pre_act)
    hidden_low = gelu_out.astype(BF16)
    d_hidden = times_trans(all_dy, down_full)
    d_pre = gelu_pull(d_hidden)[0].astype(BF16)
    d_normed_two = times_trans(d_pre, up_full).astype(BF16)
    d_normed_two = ctx_scatter(d_normed_two.reshape(ctx_size, blk_len, model_dim))
    final_part = times(hidden_low, down_full).astype(BF16)
    final_sum = ctx_scatter(final_part.reshape(ctx_size, blk_len, model_dim))
    block_out = (resid_one + final_sum + dbias).astype(BF16).reshape(block_in.shape)
    d_up = contract_rows(all_two, d_pre).astype(BF16).reshape(depth, part, hidden)
    d_down = contract_rows(hidden_low, all_dy).astype(BF16).reshape(depth, hidden_part, model_dim)
    d_ubias = jnp.sum(d_pre.astype(F32), 0)

    norm_two_out, norm_two_pull = jax.vjp(layer_norm, resid_one, gain_two, shift_two)
    d_resid_part, d_gain_two, d_shift_two = norm_two_pull(d_normed_two)
    grad_f = own_dy.astype(F32)
    d_resid = grad_f + d_resid_part
    d_branch = d_resid.astype(BF16)
    d_attn = times_trans(d_branch, proj_full).astype(BF16)
    d_attn = d_attn.reshape(blk_len, ctx_size, width).transpose(1, 0, 2)
    d_attn = lax.all_to_all(d_attn, "ctx", 0, 0, tiled=False).reshape(seq_len, width)
    d_proj = contract_rows(attn_low, d_branch).astype(BF16)
    d_proj = d_proj.reshape(depth, ctx_size, proj_rows, model_dim)
    swapped = jnp.bitwise_xor(jnp.arange(ctx_size, dtype=jnp.int32), base)
    d_proj = jnp.take(d_proj, swapped, axis=1).transpose(1, 0, 2, 3)
    d_proj = ctx_scatter(d_proj).astype(BF16)

    d_qkv = attend_grad(base, qkv, d_attn, attn_trans, log_total, ctx_size)
    d_qkv_sum = jnp.sum(d_qkv.astype(F32), 0)
    d_normed = times_trans(d_qkv, qkv_full).astype(BF16)
    d_normed_own = ctx_scatter(d_normed.reshape(ctx_size, blk_len, model_dim))
    d_weight_qkv = contract_rows(normed, d_qkv).astype(BF16).reshape(depth, part, 3 * width)

    norm_all, norm_all_pull = jax.vjp(
        lambda gain, shift: layer_norm(all_in.astype(F32), gain, shift), gain_one, shift_one
    )
    d_gain_one, d_shift_one = norm_all_pull(d_normed.astype(F32))
    norm_one, norm_one_pull = jax.vjp(lambda value: layer_norm(value, gain_one, shift_one), own_f)
    d_input = (d_resid + norm_one_pull(d_normed_own)[0]).reshape(block_in.shape)

    def spread(value):
        return lax.all_gather(value.astype(BF16), "ctx", axis=0)

    d_up = spread(depth_scatter(d_up)).astype(F32)
    d_up = d_up.reshape(ctx_size, part, depth, hidden_part).transpose(1, 2, 0, 3)
    d_up = d_up.reshape(part, -1)
    d_down = spread(depth_scatter(d_down)).astype(F32).reshape(-1, model_dim)
    d_proj = spread(depth_scatter(d_proj)).astype(F32).reshape(part, model_dim)
    d_weight_qkv = spread(depth_scatter(d_weight_qkv)).astype(F32)
    d_weight_qkv = d_weight_qkv.reshape(ctx_size, part, 3, width).transpose(1, 2, 0, 3)
    d_weight_qkv = d_weight_qkv.reshape(part, -1)

    def widen(value, total):
        start = jnp.zeros(value.shape[:-1] + (total,), F32)
        return lax.dynamic_update_slice_in_dim(
            start, value, ctx_index * value.shape[-1], value.ndim - 1
        )

    small = [
        d_gain_one,
        d_shift_one,
        widen(d_qkv_sum[:width], model_dim),
        widen(d_qkv_sum[2 * width :], model_dim),
        jnp.sum(d_branch.astype(F32), 0),
        d_gain_two,
        d_shift_two,
        jnp.sum(grad_f, 0),
    ]
    small = jnp.stack(small).reshape(8, depth, part).transpose(1, 0, 2).reshape(depth, 8 * part)
    small = jnp.concatenate(
        [small, widen(d_ubias.reshape(depth, hidden_part), up_bias.shape[0])], 1
    )
    small = lax.psum(depth_scatter(small), "ctx")
    vec = small[: 8 * part].reshape(8, part)
    return (
        block_out,
        d_input,
        vec[0],
        vec[1],
        d_weight_qkv,
        vec[2],
        vec[3],
        d_proj,
        vec[4],
        vec[5],
        vec[6],
        d_up,
        small[8 * part :],
        d_down,
        vec[7],
    )


def solution(mesh):
    rows, matrix, vector = P("fsdp", "ctx", None), P("fsdp", None), P("fsdp")
    in_specs = (
        rows,
        rows,
        vector,
        vector,
        matrix,
        vector,
        vector,
        matrix,
        vector,
        vector,
        vector,
        matrix,
        vector,
        matrix,
        vector,
    )
    out_specs = (rows, rows) + in_specs[2:]
    return jax.shard_map(shards, mesh=mesh, in_specs=in_specs, out_specs=out_specs, check_vma=False)
```

```python
import functools
import math

import jax
import jax.numpy as jnp
from jax import lax
from jax.experimental import pallas as pl
from jax.experimental.pallas import tpu as pltpu
from jax.sharding import PartitionSpec as P

HEADS = 16
HEAD_DIM = 64

EPSILON = 1e-05
GELU_COEF = 0.7978845608028654
MASKED = -1e30
SCORE_SCALE = HEAD_DIM ** (-0.5)
EXP2_SCALE = SCORE_SCALE / math.log(2.0)
F32 = jnp.float32
BF16 = jnp.bfloat16
SMEM = pl.BlockSpec(memory_space=pltpu.SMEM)
VMEM = pl.BlockSpec(memory_space=pltpu.VMEM)


def layer_norm(values, gain_vec, shift_vec):
    center = values - jnp.mean(values, -1, keepdims=True)
    spread = jnp.mean(center * center, -1, keepdims=True)
    return center * lax.rsqrt(spread + EPSILON) * gain_vec + shift_vec


def contract_rows(left, right):
    return lax.dot_general(left, right, (((0,), (0,)), ((), ())), preferred_element_type=F32)


def times_trans(left, right):
    return lax.dot_general(left, right, (((1,), (1,)), ((), ())), preferred_element_type=F32)


def times(left, right):
    return jnp.dot(left, right, preferred_element_type=F32)


def ctx_swap(value, bits):
    size = lax.axis_size("ctx")
    return lax.ppermute(value, "ctx", [(at, at ^ bits) for at in range(size)])


def ctx_places():
    size = lax.axis_size("ctx")
    order = jnp.arange(size, dtype=jnp.int32)
    return jnp.bitwise_xor(order, lax.axis_index("ctx")) if size == 8 else order


def ctx_gather(block):
    size = lax.axis_size("ctx")
    if size != 8:
        whole = lax.all_gather(block, "ctx", axis=0)
        return [whole[at] for at in range(size)]
    half = block.shape[0] // 2
    by_x = ctx_swap(block, 2)
    by_y = ctx_swap(block, 4)
    own_pair = ctx_swap(block, 1)
    diag = jnp.concatenate([ctx_swap(by_y[:half], 2), ctx_swap(by_x[half:], 4)])
    pair_x = ctx_swap(by_x, 1)
    pair_y = ctx_swap(by_y, 1)
    pair_diag = ctx_swap(diag, 1)
    return [block, own_pair, by_x, pair_x, by_y, pair_y, diag, pair_diag]


def ctx_scatter(kept, sent):
    if lax.axis_size("ctx") != 8:
        blocks = jnp.stack([kept, sent], 1).reshape((-1,) + kept.shape[1:])
        return lax.psum_scatter(blocks, "ctx", scatter_dimension=0, tiled=False).astype(F32)
    swapped = ctx_swap(sent, 1)
    total = kept[0].astype(F32) + swapped[0].astype(F32)
    for step in (1, 2, 3):
        pair = kept[step] + swapped[step]
        total = total + ctx_swap(pair, 2 * step).astype(F32)
    return total


def depth_shift(value, step):
    size = lax.axis_size("fsdp")
    return lax.ppermute(value, "fsdp", [(at, (at + step) % size) for at in range(size)])


def depth_swap(value, bits):
    size = lax.axis_size("fsdp")
    return lax.ppermute(value, "fsdp", [(at, at ^ bits) for at in range(size)])


def depth_places():
    size = lax.axis_size("fsdp")
    order = jnp.arange(size, dtype=jnp.int32)
    return lax.rem(lax.axis_index("fsdp") - order + size, size) if size == 4 else order


def depth_gather(block):
    size = lax.axis_size("fsdp")
    if size != 4:
        whole = lax.all_gather(block, "fsdp", axis=0)
        return [whole[at] for at in range(size)]
    return [block] + [depth_shift(block, step) for step in range(1, size)]


def depth_scatter(blocks):
    size = lax.axis_size("fsdp")
    if size != 4:
        return lax.psum_scatter(blocks, "fsdp", scatter_dimension=0, tiled=False).astype(F32)
    here = lax.axis_index("fsdp")
    total = lax.dynamic_index_in_dim(blocks, here, 0, False).astype(F32)
    for step in range(1, size):
        part = lax.dynamic_index_in_dim(blocks, lax.rem(here + step, size), 0, False)
        total = total + depth_shift(part, step).astype(F32)
    return total


def cost_of(microseconds):
    return pl.CostEstimate(flops=microseconds * 10**9, bytes_accessed=0, transcendentals=0)


def causal(rows, columns):
    keys = lax.broadcasted_iota(jnp.int32, (rows, columns), 0)
    queries = lax.broadcasted_iota(jnp.int32, (rows, columns), 1)
    return keys <= queries


def rows_at(place, rows):
    return pl.ds(pl.multiple_of(place * rows, rows), rows)


def normalize(values):
    center = values - jnp.mean(values, -1, keepdims=True)
    spread = jnp.mean(center * center, -1, keepdims=True)
    return center * lax.rsqrt(spread + EPSILON)


def attend_kernel(blocks, depth, tile, places_ref, depths_ref, *refs):
    x_refs, w_refs = refs[:blocks], refs[blocks : blocks + depth]
    (
        vec_ref,
        bias_ref,
        normed_ref,
        w_ref,
        qkv_ref,
        out_ref,
        out_t_ref,
        log_ref,
        q_ref,
        k_ref,
        v_t_ref,
    ) = refs[blocks + depth :]
    length, width = out_ref.shape
    heads = width // HEAD_DIM
    rows = length // blocks
    part = w_ref.shape[0] // depth
    for at in range(depth):
        place = rows_at(depths_ref[at], part)
        for column in range(3):
            w_ref[place, column * width : (column + 1) * width] = w_refs[at][
                column * part : (column + 1) * part, :
            ]
    for block in range(blocks):
        place = rows_at(places_ref[block], rows)
        normed = normalize(x_refs[block][...].astype(F32)) * vec_ref[0:1, :] + vec_ref[1:2, :]
        normed = normed.astype(BF16)
        normed_ref[place, :] = normed
        qkv = (times(normed, w_ref[...]) + bias_ref[...]).astype(BF16)
        qkv_ref[place, :] = qkv
        for head in range(heads):
            low, high = head * HEAD_DIM, (head + 1) * HEAD_DIM
            q_ref[head, place, :] = qkv[:, low:high]
            k_ref[head, place, :] = qkv[:, width + low : width + high]
        v_t_ref[:, place] = qkv[:, 2 * width :].T
    for q_tile in range(length // tile):
        columns = slice(q_tile * tile, (q_tile + 1) * tile)
        queries = [q_ref[head, columns, :] for head in range(heads)]

        def visit(k_tile, state, masked):
            start = pl.multiple_of(k_tile * tile, tile)
            result = []
            for head in range(heads):
                run_max, run_sum, run_acc = state[head]
                scores = times_trans(k_ref[head, pl.ds(start, tile), :], queries[head])
                if masked:
                    scores = jnp.where(causal(tile, tile), scores, MASKED)
                new_max = jnp.maximum(run_max, jnp.max(scores, 0, keepdims=True))
                weights = jnp.exp2(scores * EXP2_SCALE - new_max * EXP2_SCALE)
                factor = jnp.exp2((run_max - new_max) * EXP2_SCALE)
                new_sum = run_sum * factor + jnp.sum(weights, 0, keepdims=True)
                low, high = head * HEAD_DIM, (head + 1) * HEAD_DIM
                values = v_t_ref[low:high, pl.ds(start, tile)]
                new_acc = run_acc * factor + times(values, weights.astype(BF16))
                result.append((new_max, new_sum, new_acc))
            return result

        state = [
            (
                jnp.full((1, tile), MASKED, F32),
                jnp.zeros((1, tile), F32),
                jnp.zeros((HEAD_DIM, tile), F32),
            )
        ] * heads
        if q_tile:
            state = lax.fori_loop(0, q_tile, lambda at, st: visit(at, st, False), state)
        state = visit(q_tile, state, True)
        result = []
        for head in range(heads):
            run_max, run_sum, run_acc = state[head]
            result.append(run_acc / run_sum)
            log_ref[head : head + 1, columns] = run_max * EXP2_SCALE + jnp.log2(run_sum)
        result = jnp.concatenate(result, 0) if heads > 1 else result[0]
        out_t_ref[:, columns] = result
        out_ref[columns, :] = result.T.astype(BF16)


def attend_grad_kernel(
    blocks, tile, places_ref, qkv_ref, out_t_ref, log_ref, w_ref, d_out_ref, *refs
):
    d_qkv_ref, kept_ref, sent_ref, sum_ref = refs[:4]
    q_ref, k_ref, v_ref, k_t_ref, do_ref, delta_ref, dq_t_ref, dk_ref, dv_ref = refs[4:]
    width, length = out_t_ref.shape
    heads = width // HEAD_DIM
    rows = length // blocks
    for block in range(blocks):
        here = slice(block * rows, (block + 1) * rows)
        part = qkv_ref[here, :]
        for head in range(heads):
            low, high = head * HEAD_DIM, (head + 1) * HEAD_DIM
            q_ref[head, here, :] = part[:, low:high]
            k_ref[head, here, :] = part[:, width + low : width + high]
            v_ref[head, here, :] = part[:, 2 * width + low : 2 * width + high]
        k_t_ref[:, here] = part[:, width : 2 * width].T
        d_out = d_out_ref[block]
        product = d_out.astype(F32).T * out_t_ref[:, here]
        for head in range(heads):
            low, high = head * HEAD_DIM, (head + 1) * HEAD_DIM
            do_ref[head, here, :] = d_out[:, low:high]
            delta_ref[head : head + 1, here] = jnp.sum(product[low:high], 0, keepdims=True)
    dq_t_ref[...] = jnp.zeros_like(dq_t_ref)
    tiles = length // tile
    for k_tile in range(tiles):
        key_rows = slice(k_tile * tile, (k_tile + 1) * tile)

        def visit(q_tile, state, masked):
            query_rows = pl.ds(pl.multiple_of(q_tile * tile, tile), tile)
            result = []
            for head in range(heads):
                d_key, d_value = state[head]
                low, high = head * HEAD_DIM, (head + 1) * HEAD_DIM
                queries = q_ref[head, query_rows, :]
                d_out = do_ref[head, query_rows, :]
                scores = times_trans(k_ref[head, key_rows, :], queries)
                log_row = log_ref[head : head + 1, query_rows]
                probs = jnp.exp2(scores * EXP2_SCALE - log_row)
                if masked:
                    probs = jnp.where(causal(tile, tile), probs, 0.0)
                d_probs = times_trans(v_ref[head, key_rows, :], d_out)
                d_scores = (probs * (d_probs - delta_ref[head : head + 1, query_rows])).astype(BF16)
                d_value = d_value + times(probs.astype(BF16), d_out)
                d_key = d_key + times(d_scores, queries)
                dq_t_ref[low:high, query_rows] += times(k_t_ref[low:high, key_rows], d_scores)
                result.append((d_key, d_value))
            return result

        state = [(jnp.zeros((tile, HEAD_DIM), F32), jnp.zeros((tile, HEAD_DIM), F32))] * heads
        state = visit(k_tile, state, True)
        if k_tile + 1 < tiles:
            state = lax.fori_loop(k_tile + 1, tiles, lambda at, st: visit(at, st, False), state)
        for head in range(heads):
            dk_ref[head, key_rows, :] = state[head][0]
            dv_ref[head, key_rows, :] = state[head][1]
    total = jnp.zeros((1, 3 * width), F32)
    for block in range(blocks):
        place = rows_at(places_ref[block], rows)
        d_key = [dk_ref[head, place, :] * SCORE_SCALE for head in range(heads)]
        d_value = [dv_ref[head, place, :] for head in range(heads)]
        parts = [dq_t_ref[:, place].T * SCORE_SCALE] + d_key + d_value
        d_qkv = jnp.concatenate(parts, 1).astype(BF16)
        d_qkv_ref[place, :] = d_qkv
        total = total + jnp.sum(d_qkv.astype(F32), 0, keepdims=True)
        out = sent_ref if block % 2 else kept_ref
        out[block // 2] = times_trans(d_qkv, w_ref[...]).astype(BF16)
    sum_ref[...] = total


def attend(places, depths, x_parts, w_parts, vectors, bias):
    blocks, depth = len(x_parts), len(w_parts)
    rows, model_dim = x_parts[0].shape
    width = bias.shape[1] // 3
    length = rows * blocks
    heads = width // HEAD_DIM
    tile = min(512, length)
    return pl.pallas_call(
        functools.partial(attend_kernel, blocks, depth, tile),
        out_shape=(
            jax.ShapeDtypeStruct((length, model_dim), BF16),
            jax.ShapeDtypeStruct((model_dim, 3 * width), BF16),
            jax.ShapeDtypeStruct((length, 3 * width), BF16),
            jax.ShapeDtypeStruct((length, width), BF16),
            jax.ShapeDtypeStruct((width, length), F32),
            jax.ShapeDtypeStruct((heads, length), F32),
        ),
        in_specs=[SMEM] * 2 + [VMEM] * (blocks + depth + 2),
        out_specs=(VMEM,) * 6,
        scratch_shapes=[
            pltpu.VMEM((heads, length, HEAD_DIM), BF16),
            pltpu.VMEM((heads, length, HEAD_DIM), BF16),
            pltpu.VMEM((width, length), BF16),
        ],
        compiler_params=pltpu.CompilerParams(vmem_limit_bytes=32 << 20),
        cost_estimate=cost_of(10),
        name="attend",
    )(places, depths, *x_parts, *w_parts, vectors, bias)


def attend_grad(places, qkv, d_out, out_t, log_total, w_full):
    length, width = qkv.shape[0], qkv.shape[1] // 3
    model_dim = w_full.shape[0]
    blocks = places.shape[0]
    heads = width // HEAD_DIM
    tile = min(512, length)
    per_head = pltpu.VMEM((heads, length, HEAD_DIM), BF16)
    half = jax.ShapeDtypeStruct((blocks // 2, length // blocks, model_dim), BF16)
    return pl.pallas_call(
        functools.partial(attend_grad_kernel, blocks, tile),
        out_shape=(
            jax.ShapeDtypeStruct((length, 3 * width), BF16),
            half,
            half,
            jax.ShapeDtypeStruct((1, 3 * width), F32),
        ),
        in_specs=[SMEM] + [VMEM] * 5,
        out_specs=(VMEM,) * 4,
        scratch_shapes=[
            per_head,
            per_head,
            per_head,
            pltpu.VMEM((width, length), BF16),
            per_head,
            pltpu.VMEM((heads, length), F32),
            pltpu.VMEM((width, length), F32),
            pltpu.VMEM((heads, length, HEAD_DIM), F32),
            pltpu.VMEM((heads, length, HEAD_DIM), F32),
        ],
        compiler_params=pltpu.CompilerParams(vmem_limit_bytes=32 << 20),
        cost_estimate=cost_of(20),
        name="attend_grad",
    )(places, qkv, out_t, log_total, w_full, d_out)


def feed_kernel(blocks, depth, depths_ref, *refs):
    m_refs, dy_refs = refs[:blocks], refs[blocks : 2 * blocks]
    w_refs = refs[2 * blocks : 2 * blocks + depth]
    (
        bias_ref,
        kept_ref,
        sent_ref,
        m_ref,
        dy_ref,
        hidden_ref,
        d_pre_ref,
        sum_ref,
        down_ref,
        up_ref,
    ) = refs[2 * blocks + depth :]
    rows = m_refs[0].shape[0]
    model_dim, hidden = up_ref.shape
    part, share = model_dim // depth, hidden // depth
    for at in range(depth):
        up_ref[rows_at(depths_ref[at], part), :] = w_refs[at][:part, :]
        place = rows_at(depths_ref[at], share)
        for cut in range(model_dim // hidden):
            first = part + cut * share
            down_ref[place, cut * hidden : (cut + 1) * hidden] = w_refs[at][
                first : first + share, :
            ]
    total = jnp.zeros((1, hidden), F32)
    for block in range(blocks):
        here = slice(block * rows, (block + 1) * rows)
        m_ref[here, :] = m_refs[block][...]
        dy_ref[here, :] = dy_refs[block][...]
        pre_act = times(m_refs[block][...], up_ref[...]) + bias_ref[...]
        d_hidden = times_trans(dy_refs[block][...], down_ref[...])
        square = pre_act * pre_act
        bent = jnp.tanh(GELU_COEF * (pre_act + 0.044715 * (square * pre_act)))
        half_one = 0.5 + 0.5 * bent
        hidden_ref[here, :] = (pre_act * half_one).astype(BF16)
        slope = half_one + (0.5 * pre_act) * (1.0 - bent * bent) * (
            GELU_COEF + (3.0 * 0.044715 * GELU_COEF) * square
        )
        d_pre = (d_hidden * slope).astype(BF16)
        d_pre_ref[here, :] = d_pre
        total = total + jnp.sum(d_pre.astype(F32), 0, keepdims=True)
        out = sent_ref if block % 2 else kept_ref
        out[block // 2] = times_trans(d_pre, up_ref[...]).astype(BF16)
    sum_ref[...] = total


def feed(depths, m_parts, dy_parts, w_parts, bias):
    blocks, depth = len(m_parts), len(w_parts)
    rows, model_dim = m_parts[0].shape
    hidden = bias.shape[1]
    length = rows * blocks
    half = jax.ShapeDtypeStruct((blocks // 2, rows, model_dim), BF16)
    whole = jax.ShapeDtypeStruct((length, model_dim), BF16)
    units = jax.ShapeDtypeStruct((length, hidden), BF16)
    return pl.pallas_call(
        functools.partial(feed_kernel, blocks, depth),
        out_shape=(
            half,
            half,
            whole,
            whole,
            units,
            units,
            jax.ShapeDtypeStruct((1, hidden), F32),
            jax.ShapeDtypeStruct((hidden, model_dim), BF16),
        ),
        in_specs=[SMEM] + [VMEM] * (2 * blocks + depth + 1),
        out_specs=(VMEM,) * 8,
        scratch_shapes=[pltpu.VMEM((model_dim, hidden), BF16)],
        compiler_params=pltpu.CompilerParams(vmem_limit_bytes=32 << 20),
        cost_estimate=cost_of(10),
        name="feed",
    )(depths, *m_parts, *dy_parts, *w_parts, bias)


def first_sums_kernel(blocks, *refs):
    x_refs = refs[:blocks]
    kept_ref, sent_ref, out_ref = refs[blocks:]
    gain = jnp.zeros((1, out_ref.shape[1]), F32)
    shift = gain
    for block in range(blocks):
        grad = (sent_ref if block % 2 else kept_ref)[block // 2].astype(F32)
        values = normalize(x_refs[block][...].astype(F32))
        gain = gain + jnp.sum(grad * values, 0, keepdims=True)
        shift = shift + jnp.sum(grad, 0, keepdims=True)
    out_ref[...] = jnp.concatenate([gain, shift], 0)


def first_sums(x_parts, kept, sent):
    blocks = len(x_parts)
    rows, model_dim = x_parts[0].shape
    return pl.pallas_call(
        functools.partial(first_sums_kernel, blocks),
        out_shape=jax.ShapeDtypeStruct((2, model_dim), F32),
        in_specs=[VMEM] * (blocks + 2),
        out_specs=VMEM,
        compiler_params=pltpu.CompilerParams(vmem_limit_bytes=32 << 20),
        cost_estimate=cost_of(0),
        name="first_sums",
    )(*x_parts, kept, sent)


def place_feed_kernel(blocks, depth, places_ref, *refs):
    piece_refs, (up_ref, down_ref) = refs[:blocks], refs[blocks:]
    part, share = up_ref.shape[0], up_ref.shape[1] // depth // blocks
    hidden = share * depth
    for at in range(blocks):
        place = places_ref[at]
        for cut in range(depth):
            start = pl.multiple_of(cut * share * blocks + place * share, share)
            up_ref[:, pl.ds(start, share)] = piece_refs[at][
                :part, cut * share : (cut + 1) * share
            ].astype(F32)
        for cut in range(down_ref.shape[1] // hidden):
            first = part + cut * share
            down_ref[rows_at(place, share), cut * hidden : (cut + 1) * hidden] = piece_refs[at][
                first : first + share, :
            ].astype(F32)


def place_feed(places, pieces, part, model_dim, units, depth):
    blocks = len(pieces)
    share = units // blocks
    if share % 128 == 0:
        return pl.pallas_call(
            functools.partial(place_feed_kernel, blocks, depth),
            out_shape=(
                jax.ShapeDtypeStruct((part, units * depth), F32),
                jax.ShapeDtypeStruct((units, model_dim), F32),
            ),
            in_specs=[SMEM] + [VMEM] * blocks,
            out_specs=(VMEM,) * 2,
            compiler_params=pltpu.CompilerParams(vmem_limit_bytes=32 << 20),
            name="place_feed",
        )(places, *pieces)
    pieces = jnp.stack(pieces).astype(F32)
    up = pieces[:, :part].reshape(blocks, part, depth, share).transpose(1, 2, 0, 3)
    down = pieces[:, part:].reshape(blocks, -1, share, share * depth).transpose(0, 2, 1, 3)
    return up.reshape(part, -1), down.reshape(units, model_dim)


def place_heads_kernel(blocks, places_ref, *refs):
    piece_refs, (qkv_ref, proj_ref, vec_ref) = refs[:blocks], refs[blocks:]
    part, width = qkv_ref.shape[0], qkv_ref.shape[1] // 3 // blocks
    share = part // blocks
    for at in range(blocks):
        place = places_ref[at]
        for cut in range(3):
            start = pl.multiple_of(cut * width * blocks + place * width, width)
            qkv_ref[:, pl.ds(start, width)] = piece_refs[at][
                :part, cut * width : (cut + 1) * width
            ].astype(F32)
        for cut in range(blocks):
            proj_ref[rows_at(place, share), cut * width : (cut + 1) * width] = piece_refs[at][
                cut * share : (cut + 1) * share, 3 * width :
            ].astype(F32)
    vec = piece_refs[0][part:, :].astype(F32)
    for at in range(1, blocks):
        vec = vec + piece_refs[at][part:, :].astype(F32)
    vec_ref[...] = vec


def place_heads(places, pieces, part, model_dim):
    blocks = len(pieces)
    width, extra = model_dim // blocks, pieces[0].shape[0] - part
    if width % 128 == 0:
        return pl.pallas_call(
            functools.partial(place_heads_kernel, blocks),
            out_shape=(
                jax.ShapeDtypeStruct((part, 3 * model_dim), F32),
                jax.ShapeDtypeStruct((part, model_dim), F32),
                jax.ShapeDtypeStruct((extra, 4 * width), F32),
            ),
            in_specs=[SMEM] + [VMEM] * blocks,
            out_specs=(VMEM,) * 3,
            compiler_params=pltpu.CompilerParams(vmem_limit_bytes=32 << 20),
            name="place_heads",
        )(places, *pieces)
    pieces = jnp.stack(pieces).astype(F32)
    qkv = pieces[:, :part, : 3 * width].reshape(blocks, part, 3, width).transpose(1, 2, 0, 3)
    proj = pieces[:, :part, 3 * width :].reshape(blocks, blocks, part // blocks, width)
    proj = proj.transpose(0, 2, 1, 3).reshape(part, model_dim)
    return qkv.reshape(part, -1), proj, jnp.sum(pieces[:, part:], 0)


def shards_any(
    block_in,
    out_grad,
    ln1_gain,
    ln1_shift,
    qkv_weight,
    query_bias,
    value_bias,
    proj_weight,
    proj_bias,
    ln2_gain,
    ln2_shift,
    up_weight,
    up_bias,
    down_weight,
    down_bias,
):
    seq_count, blk_len, model_dim = block_in.shape
    ctx_size, depth = lax.axis_size("ctx"), lax.axis_size("fsdp")
    ctx_index, depth_index = lax.axis_index("ctx"), lax.axis_index("fsdp")
    places, depths = ctx_places(), depth_places()
    seq_len = ctx_size * blk_len
    width = model_dim // ctx_size
    part = model_dim // depth
    units = up_bias.shape[0]
    share = units // ctx_size
    hidden = share * depth
    cuts = model_dim // hidden

    own_in = block_in.reshape(blk_len, model_dim)
    own_dy = out_grad.reshape(blk_len, model_dim)

    def ctx_columns(value, columns, axis):
        return lax.dynamic_slice_in_dim(value, ctx_index * columns, columns, axis)

    x_parts = ctx_gather(own_in)
    vectors = jnp.concatenate(
        [
            ln1_gain,
            ln1_shift,
            query_bias,
            value_bias,
            proj_bias,
            ln2_gain,
            ln2_shift,
            down_bias,
            up_bias,
        ]
    )
    slices = [
        lax.dynamic_slice_in_dim(qkv_weight, at * model_dim + ctx_index * width, width, 1)
        for at in range(3)
    ]
    first = depth_gather(jnp.concatenate(slices + [vectors.reshape(-1, width)]))
    vec = jnp.stack([piece[3 * part :] for piece in first]).reshape(depth, -1)
    vec = jnp.take(vec, depths, axis=0).astype(F32)
    ubias = ctx_columns(vec[:, 8 * part :], share, 1).reshape(1, hidden)
    vec = vec[:, : 8 * part].reshape(depth, 8, part).transpose(1, 0, 2).reshape(8, model_dim)
    gain_two, shift_two = vec[5], vec[6]
    qkv_bias = jnp.concatenate(
        [ctx_columns(vec[2], width, 0), jnp.zeros((width,), F32), ctx_columns(vec[3], width, 0)]
    ).reshape(1, 3 * width)

    normed, qkv_full, qkv, attn_heads, attn_trans, log_total = attend(
        places, depths, x_parts, first, vec, qkv_bias
    )
    attn_low = lax.all_to_all(
        attn_heads.reshape(ctx_size, blk_len, width), "ctx", 0, 0, tiled=False
    )
    attn_low = attn_low.transpose(1, 0, 2).reshape(blk_len, model_dim)

    up_slice = lax.dynamic_index_in_dim(
        up_weight.reshape(part, depth, ctx_size, share), ctx_index, 2, False
    ).reshape(part, hidden)
    down_slice = ctx_columns(down_weight, share, 0)
    down_cuts = [down_slice[:, at * hidden : (at + 1) * hidden] for at in range(cuts)]
    second = depth_gather(jnp.concatenate([up_slice] + down_cuts))
    proj_rows = part // ctx_size
    proj_full = lax.all_gather(
        ctx_columns(proj_weight, proj_rows, 0), ("fsdp", "ctx"), axis=0, tiled=True
    )
    dy_parts = ctx_gather(own_dy)

    own_f = own_in.astype(F32)
    resid_one = own_f + times(attn_low, proj_full) + vec[4]
    normed_two = layer_norm(resid_one, gain_two, shift_two).astype(BF16)

    m_parts = ctx_gather(normed_two)
    kept, sent, all_two, all_dy, hidden_low, d_pre, d_ubias, down_full = feed(
        depths, m_parts, dy_parts, second, ubias
    )
    d_normed_two = ctx_scatter(kept, sent)
    final_part = times(hidden_low, down_full).astype(BF16)
    final_part = final_part.reshape(ctx_size // 2, 2, blk_len, model_dim)
    final_sum = ctx_scatter(final_part[:, 0], final_part[:, 1])
    block_out = (resid_one + final_sum + vec[7]).astype(BF16).reshape(block_in.shape)
    d_up = contract_rows(all_two, d_pre).astype(BF16).reshape(depth, part, hidden)
    d_down = contract_rows(hidden_low, all_dy).astype(BF16).reshape(depth, share, cuts, hidden)
    d_down = d_down.transpose(0, 2, 1, 3).reshape(depth, cuts * share, hidden)
    d_feed = depth_scatter(jnp.concatenate([d_up, d_down], 1)).astype(BF16)
    d_up, d_down = place_feed(places, ctx_gather(d_feed), part, model_dim, units, depth)

    norm_two_out, norm_two_pull = jax.vjp(layer_norm, resid_one, gain_two, shift_two)
    d_resid_part, d_gain_two, d_shift_two = norm_two_pull(d_normed_two)
    grad_f = own_dy.astype(F32)
    d_resid = grad_f + d_resid_part
    d_branch = d_resid.astype(BF16)
    d_attn = times_trans(d_branch, proj_full).astype(BF16)
    d_attn = d_attn.reshape(blk_len, ctx_size, width).transpose(1, 0, 2)
    d_attn = lax.all_to_all(d_attn, "ctx", 0, 0, tiled=False)
    d_proj = contract_rows(attn_low, d_branch).astype(BF16)
    d_proj = d_proj.reshape(depth, ctx_size, proj_rows, model_dim)
    d_proj = jnp.take(d_proj, places, axis=1).transpose(1, 0, 2, 3)
    d_proj = d_proj.reshape(ctx_size // 2, 2, part // ctx_size * depth, model_dim)
    d_proj = ctx_scatter(d_proj[:, 0], d_proj[:, 1]).astype(BF16)
    d_proj = d_proj.reshape(depth, proj_rows, ctx_size, width).transpose(0, 2, 1, 3)
    d_proj = d_proj.reshape(depth, part, width)

    d_qkv, kept, sent, d_qkv_sum = attend_grad(
        places, qkv, d_attn, attn_trans, log_total, qkv_full
    )
    d_normed_own = ctx_scatter(kept, sent)
    d_weight_qkv = contract_rows(normed, d_qkv).astype(BF16).reshape(depth, part, 3 * width)
    d_first = first_sums(x_parts, kept, sent)
    norm_one, norm_one_pull = jax.vjp(lambda value: layer_norm(value, vec[0], vec[1]), own_f)
    d_input = (d_resid + norm_one_pull(d_normed_own)[0]).reshape(block_in.shape)

    def widen(value, total):
        start = jnp.zeros(value.shape[:-1] + (total,), F32)
        return lax.dynamic_update_slice_in_dim(
            start, value, ctx_index * value.shape[-1], value.ndim - 1
        )

    small = [
        d_first[0],
        d_first[1],
        widen(d_qkv_sum[0, :width], model_dim),
        widen(d_qkv_sum[0, 2 * width :], model_dim),
        jnp.sum(d_branch.astype(F32), 0),
        d_gain_two,
        d_shift_two,
        jnp.sum(grad_f, 0),
    ]
    small = jnp.stack(small).reshape(8, depth, part).transpose(1, 0, 2).reshape(depth, 8 * part)
    small = jnp.concatenate([small, widen(d_ubias.reshape(depth, share), units)], 1)
    count = small.shape[1]
    small = small.astype(BF16).reshape(depth, -1, 4 * width)
    small = jnp.pad(small, ((0, 0), (0, -small.shape[1] % 16), (0, 0)))
    last = jnp.concatenate([jnp.concatenate([d_weight_qkv, d_proj], 2), small], 1)
    last = ctx_gather(depth_scatter(last).astype(BF16))
    d_weight_qkv, d_proj, small = place_heads(places, last, part, model_dim)
    small = small.reshape(-1)[:count]
    d_vec = small[: 8 * part].reshape(8, part)
    return (
        block_out,
        d_input,
        d_vec[0],
        d_vec[1],
        d_weight_qkv,
        d_vec[2],
        d_vec[3],
        d_proj,
        d_vec[4],
        d_vec[5],
        d_vec[6],
        d_up,
        small[8 * part :],
        d_down,
        d_vec[7],
    )


ANY = pl.BlockSpec(memory_space=pl.ANY)
HBM = pl.BlockSpec(memory_space=pltpu.HBM)


SPOT_OWN, SPOT_CTX, SPOT_FROM, SPOT_SWAP = 0, 1, 9, 13


def tie(value, *others):
    return lax.optimization_barrier((value,) + others)[0]


def call(kernel, name, outs, in_specs, scratch=(), out_specs=None, limit=16, after=(), cost=3):
    count = len(in_specs)

    def body(*refs):
        return kernel(*refs[:count], *refs[count + len(after) :])

    run = pl.pallas_call(
        body if after else kernel,
        out_shape=tuple(jax.ShapeDtypeStruct(shape, kind) for shape, kind in outs),
        in_specs=list(in_specs) + [ANY] * len(after),
        out_specs=tuple(out_specs or [VMEM] * len(outs)),
        scratch_shapes=list(scratch),
        compiler_params=pltpu.CompilerParams(vmem_limit_bytes=limit << 20),
        cost_estimate=cost_of(cost),
        name=name,
    )
    return lambda *args: run(*args, *after)


def lanes_at(place, size):
    return pl.ds(pl.multiple_of(place * size, size), size)


def run_copies(copies):
    for copy in copies:
        copy.start()
    for copy in copies:
        copy.wait()


def pack_first_kernel(spots_ref, qkv_ref, proj_ref, vec_ref, out_ref, proj_buf, sems):
    own = spots_ref[SPOT_OWN]
    part, model_dim = proj_ref.shape
    width = out_ref.shape[1]
    blocks = model_dim // width
    share = part // blocks
    copies = [
        pltpu.make_async_copy(
            qkv_ref.at[:, lanes_at(at * blocks + own, width)],
            out_ref.at[at * part : (at + 1) * part, :],
            sems.at[at],
        )
        for at in range(3)
    ]
    copies.append(pltpu.make_async_copy(proj_ref.at[rows_at(own, share), :], proj_buf, sems.at[3]))
    run_copies(copies)
    vec = vec_ref[...].reshape(1, 16 * part)
    vec = [vec[:, at * part : (at + 1) * part] for at in range(16)]
    vec = jnp.concatenate(vec, 0).astype(BF16)
    first = 3 * part
    out_ref[first : first + 16, :] = vec[:, :width]
    out_ref[first + 16 : first + 32, :] = vec[:, width:]
    first = first + 32
    for at in range(blocks):
        out_ref[first + at * share : first + (at + 1) * share, :] = proj_buf[
            :, at * width : (at + 1) * width
        ]


def pack_second_kernel(spots_ref, up_ref, down_ref, out_ref, sems):
    own = spots_ref[SPOT_OWN]
    part, hidden = up_ref.shape[0], out_ref.shape[1]
    share = hidden // 4
    blocks = up_ref.shape[1] // hidden
    copies = []
    for at in range(4):
        copies.append(
            pltpu.make_async_copy(
                up_ref.at[:, lanes_at(at * blocks + own, share)],
                out_ref.at[:part, at * share : (at + 1) * share],
                sems.at[at],
            )
        )
    for at in range(down_ref.shape[1] // hidden):
        first = part + at * share
        copies.append(
            pltpu.make_async_copy(
                down_ref.at[rows_at(own, share), at * hidden : (at + 1) * hidden],
                out_ref.at[first : first + share, :],
                sems.at[4 + at],
            )
        )
    run_copies(copies)


def attend_fast_kernel(tile, spots_ref, *refs):
    x_refs, w_refs = refs[:8], refs[8:10]
    (
        normed_ref,
        w_ref,
        qkv_ref,
        out_ref,
        out_t_ref,
        log_ref,
        vec_ref,
        ubias_ref,
        q_ref,
        k_ref,
        v_t_ref,
        normed_buf,
        sems,
    ) = refs[10:]
    blocks, rows, width = out_ref.shape
    length = blocks * rows
    heads = width // HEAD_DIM
    part = w_ref.shape[0] // 4
    own = spots_ref[SPOT_OWN]
    for at in range(4):
        source = spots_ref[SPOT_SWAP + at]
        piece = w_refs[at % 2].at[at // 2]
        place = rows_at(source, part)
        for column in range(3):
            w_ref[place, column * width : (column + 1) * width] = piece[
                column * part : (column + 1) * part, :
            ]
        for half in range(2):
            first = 3 * part + 16 * half
            vec_ref[:, lanes_at(source * 2 + half, width)] = piece[
                first : first + 16, :
            ].astype(F32)
    for at in range(4):
        rows_here = vec_ref[8:16, lanes_at(at * 2 + lax.rem(own, 2), width)]
        chosen = lax.broadcasted_iota(jnp.int32, (8, width), 0) == own // 2
        ubias_ref[:, at * width : (at + 1) * width] = jnp.sum(
            jnp.where(chosen, rows_here, 0.0), 0, keepdims=True
        )
    qbias, vbias = (vec_ref[at : at + 1, lanes_at(own, width)] for at in (2, 3))
    bias = jnp.concatenate([qbias, jnp.zeros((1, width), F32), vbias], 1)
    gain, shift = vec_ref[0:1, :], vec_ref[1:2, :]
    copies = []
    for block in range(blocks):
        place = rows_at(spots_ref[SPOT_CTX + block], rows)
        normed = (normalize(x_refs[block][...].astype(F32)) * gain + shift).astype(BF16)
        normed_buf[block] = normed
        copies.append(
            pltpu.make_async_copy(normed_buf.at[block], normed_ref.at[place, :], sems.at[block])
        )
        copies[-1].start()
        qkv = (times(normed, w_ref[...]) + bias).astype(BF16)
        qkv_ref[place, :] = qkv
        for head in range(heads):
            low, high = head * HEAD_DIM, (head + 1) * HEAD_DIM
            q_ref[head, place, :] = qkv[:, low:high]
            k_ref[head, place, :] = qkv[:, width + low : width + high]
        v_t_ref[:, place] = qkv[:, 2 * width :].T
    for q_tile in range(length // tile):
        columns = slice(q_tile * tile, (q_tile + 1) * tile)
        queries = [q_ref[head, columns, :] for head in range(heads)]

        def visit(k_tile, state, masked):
            start = pl.multiple_of(k_tile * tile, tile)
            result = []
            for head in range(heads):
                run_max, run_sum, run_acc = state[head]
                scores = times_trans(k_ref[head, pl.ds(start, tile), :], queries[head])
                if masked:
                    scores = jnp.where(causal(tile, tile), scores, MASKED)
                new_max = jnp.maximum(run_max, jnp.max(scores, 0, keepdims=True))
                weights = jnp.exp2(scores * EXP2_SCALE - new_max * EXP2_SCALE)
                factor = jnp.exp2((run_max - new_max) * EXP2_SCALE)
                new_sum = run_sum * factor + jnp.sum(weights, 0, keepdims=True)
                low, high = head * HEAD_DIM, (head + 1) * HEAD_DIM
                values = v_t_ref[low:high, pl.ds(start, tile)]
                new_acc = run_acc * factor + times(values, weights.astype(BF16))
                result.append((new_max, new_sum, new_acc))
            return result

        state = [
            (
                jnp.full((1, tile), MASKED, F32),
                jnp.zeros((1, tile), F32),
                jnp.zeros((HEAD_DIM, tile), F32),
            )
        ] * heads
        if q_tile:
            state = lax.fori_loop(0, q_tile, lambda at, st: visit(at, st, False), state)
        state = visit(q_tile, state, True)
        result = []
        for head in range(heads):
            run_max, run_sum, run_acc = state[head]
            result.append(run_acc / run_sum)
            log_ref[head : head + 1, columns] = run_max * EXP2_SCALE + jnp.log2(run_sum)
        result = jnp.concatenate(result, 0)
        out_t_ref[:, columns] = result
        result = result.T.astype(BF16)
        for at in range(tile // rows):
            out_ref[q_tile * (tile // rows) + at] = result[at * rows : (at + 1) * rows]
    for copy in copies:
        copy.wait()


def mix_kernel(spots_ref, x_ref, vec_ref, attn_ref, *refs):
    joined_refs, (resid_ref, m_ref, proj_ref, attn_low_ref, sems) = refs[:8], refs[8:]
    blocks, rows, width = attn_ref.shape
    share = proj_ref.shape[0] // 4 // blocks
    copies = []
    for at in range(blocks):
        for source in range(4):
            place = spots_ref[SPOT_SWAP + source] * blocks + spots_ref[SPOT_CTX + at]
            first = rows + source * share
            copies.append(
                pltpu.make_async_copy(
                    joined_refs[at].at[first : first + share, :],
                    proj_ref.at[rows_at(place, share), :],
                    sems.at[at * 4 + source],
                )
            )
            copies[-1].start()
        attn_low_ref[:, at * width : (at + 1) * width] = attn_ref[at]
    for copy in copies:
        copy.wait()
    resid = x_ref[...].astype(F32) + times(attn_low_ref[...], proj_ref[...]) + vec_ref[4:5, :]
    resid_ref[...] = resid
    m_ref[...] = (normalize(resid) * vec_ref[5:6, :] + vec_ref[6:7, :]).astype(BF16)


def norm_back(values, grad, gain):
    center = values - jnp.mean(values, -1, keepdims=True)
    scale = lax.rsqrt(jnp.mean(center * center, -1, keepdims=True) + EPSILON)
    unit = center * scale
    grad_unit = grad * gain
    inner = jnp.mean(grad_unit * unit, -1, keepdims=True)
    return unit, scale * (grad_unit - jnp.mean(grad_unit, -1, keepdims=True) - unit * inner)


def add_parts(refs):
    total = refs[0][...].astype(F32)
    for ref in refs[1:]:
        total = total + ref[...].astype(F32)
    return total


def mix_back_kernel(spots_ref, dy_ref, resid_ref, vec_ref, proj_ref, attn_ref, *refs):
    part_refs, (d_resid_ref, d_attn_ref, sum_ref, kept_ref, sent_ref, full_ref) = refs[:5], refs[5:]
    blocks, rows, width = d_attn_ref.shape
    grad = add_parts(part_refs)
    dy = dy_ref[...].astype(F32)
    unit, d_values = norm_back(resid_ref[...], grad, vec_ref[5:6, :])
    d_resid = dy + d_values
    d_resid_ref[...] = d_resid
    d_branch = d_resid.astype(BF16)
    for at in range(blocks):
        d_attn_ref[at] = times_trans(
            d_branch, proj_ref[at * width : (at + 1) * width, :]
        ).astype(BF16)
    sums = [d_branch.astype(F32), grad * unit, grad, dy]
    sums = [jnp.sum(item, 0, keepdims=True) for item in sums]
    sum_ref[...] = jnp.concatenate(sums + [jnp.zeros((4, sum_ref.shape[1]), F32)], 0)
    full_ref[...] = contract_rows(attn_ref[...], d_branch).astype(BF16)
    share = full_ref.shape[0] // 4 // blocks
    for block in range(blocks):
        out = sent_ref if block % 2 else kept_ref
        for at in range(4):
            place = at * blocks + spots_ref[SPOT_CTX + block]
            out[block // 2, at * share : (at + 1) * share, :] = full_ref[rows_at(place, share), :]


def feed_fast_kernel(spots_ref, *refs):
    m_refs, dy_refs, w_refs, bias_ref = refs[:8], refs[8:16], refs[16:18], refs[18]
    kept_ref, sent_ref, y_kept_ref, y_sent_ref, w_kept_ref, w_sent_ref, sum_ref = refs[19:26]
    (
        down_ref,
        up_ref,
        m_buf,
        dy_buf,
        out_buf,
        hidden_ref,
        d_pre_ref,
        in_sems,
        out_sems,
    ) = refs[26:]
    length, model_dim = m_buf.shape
    rows = length // 8
    hidden = up_ref.shape[1]
    part, share = model_dim // 4, hidden // 4
    for block in range(8):
        here = slice(block * rows, (block + 1) * rows)
        pltpu.make_async_copy(m_refs[block], m_buf.at[here, :], in_sems.at[2 * block]).start()
        pltpu.make_async_copy(
            dy_refs[block].at[:rows, :], dy_buf.at[here, :], in_sems.at[2 * block + 1]
        ).start()
    for at in range(4):
        source = spots_ref[SPOT_SWAP + at]
        piece = w_refs[at % 2].at[at // 2]
        up_ref[rows_at(source, part), :] = piece[:part, :]
        for cut in range(model_dim // hidden):
            first = part + cut * share
            down_ref[rows_at(source, share), cut * hidden : (cut + 1) * hidden] = piece[
                first : first + share, :
            ]
    sum_ref[...] = jnp.zeros_like(sum_ref)
    outs = ((kept_ref, y_kept_ref), (sent_ref, y_sent_ref))

    def send(pair, side):
        block = 2 * pair + side
        return pltpu.make_async_copy(out_buf.at[block], outs[side][0].at[pair], out_sems.at[block])

    @pl.loop(0, 4)
    def _(pair):
        for side in range(2):
            block = 2 * pair + side
            here = rows_at(block, rows)
            for at, buf in enumerate((m_buf, dy_buf)):
                pltpu.make_async_copy(
                    buf.at[here, :], buf.at[here, :], in_sems.at[2 * block + at]
                ).wait()
            pre_act = times(m_buf[here, :], up_ref[...]) + bias_ref[...]
            d_hidden = times_trans(dy_buf[here, :], down_ref[...])
            square = pre_act * pre_act
            bent = jnp.tanh(GELU_COEF * (pre_act + 0.044715 * (square * pre_act)))
            half_one = 0.5 + 0.5 * bent
            hidden_low = (pre_act * half_one).astype(BF16)
            hidden_ref[here, :] = hidden_low
            slope = half_one + (0.5 * pre_act) * (1.0 - bent * bent) * (
                GELU_COEF + (3.0 * 0.044715 * GELU_COEF) * square
            )
            d_pre = (d_hidden * slope).astype(BF16)
            d_pre_ref[here, :] = d_pre
            sum_ref[...] += jnp.sum(d_pre.astype(F32), 0, keepdims=True)
            out_buf[block] = times_trans(d_pre, up_ref[...]).astype(BF16)
            send(pair, side).start()
            outs[side][1][pair] = times(hidden_low, down_ref[...]).astype(BF16)

    @pl.loop(0, 2)
    def _(pair):
        for side, out in enumerate((w_kept_ref, w_sent_ref)):
            place = spots_ref[SPOT_SWAP + 2 * pair + side]
            columns = lanes_at(place, part)
            out[pair, :part, :] = contract_rows(m_buf[:, columns], d_pre_ref[...]).astype(BF16)
            d_down = contract_rows(hidden_ref[:, lanes_at(place, share)], dy_buf[...]).astype(BF16)
            for cut in range(model_dim // hidden):
                first = part + cut * share
                out[pair, first : first + share, :] = d_down[:, cut * hidden : (cut + 1) * hidden]

    for pair in range(4):
        for side in range(2):
            send(pair, side).wait()


def pack_last_kernel(
    spots_ref,
    normed_ref,
    d_qkv_ref,
    d_first_ref,
    d_qkv_sum_ref,
    sum_ref,
    d_ubias_ref,
    *refs,
):
    part_refs, out_refs, (vec_ref, units_ref, proj_ref) = refs[:4], refs[4:6], refs[6:]
    own = spots_ref[SPOT_OWN]
    width = d_qkv_ref.shape[1] // 3
    model_dim = normed_ref.shape[1]
    part = model_dim // 4
    blocks = model_dim // width
    share = part // blocks
    proj_ref[...] = add_parts(part_refs)
    vec_ref[...] = jnp.zeros_like(vec_ref)
    vec_ref[0:2, :] = d_first_ref[...]
    vec_ref[2:3, lanes_at(own, width)] = d_qkv_sum_ref[:, :width]
    vec_ref[3:4, lanes_at(own, width)] = d_qkv_sum_ref[:, 2 * width :]
    vec_ref[4:8, :] = sum_ref[0:4, :]
    for at in range(4):
        place = spots_ref[SPOT_SWAP + at]
        out = out_refs[at % 2].at[at // 2]
        columns = lanes_at(place, part)
        out[:part, : 3 * width] = contract_rows(normed_ref[:, columns], d_qkv_ref[...]).astype(BF16)
        for cut in range(blocks):
            out[cut * share : (cut + 1) * share, 3 * width :] = proj_ref[
                rows_at(place, share), cut * width : (cut + 1) * width
            ].astype(BF16)
        units_ref[...] = jnp.zeros_like(units_ref)
        units_ref[:, lanes_at(own, width)] = d_ubias_ref[:, lanes_at(place, width)]
        vec = [
            jnp.concatenate([vec_ref[2 * row : 2 * row + 1, columns], vec_ref[2 * row + 1 : 2 * row + 2, columns]], 1)
            for row in range(4)
        ]
        vec = vec + [units_ref[:, : 2 * part], units_ref[:, 2 * part :]]
        vec = jnp.concatenate(vec + [jnp.zeros((10, 4 * width), F32)], 0)
        out[part:, :] = vec.astype(BF16)


def place_last_kernel(spots_ref, *refs):
    piece_refs, (qkv_ref, proj_ref), vec_refs = refs[:8], refs[8:10], refs[10:]
    part, width = qkv_ref.shape[0], qkv_ref.shape[1] // 24
    share = part // 8
    for at in range(8):
        place = spots_ref[SPOT_CTX + at]
        for cut in range(3):
            qkv_ref[:, lanes_at(cut * 8 + place, width)] = piece_refs[at][
                :part, cut * width : (cut + 1) * width
            ].astype(F32)
        for cut in range(8):
            proj_ref[rows_at(place, share), cut * width : (cut + 1) * width] = piece_refs[at][
                cut * share : (cut + 1) * share, 3 * width :
            ].astype(F32)
    vec = piece_refs[0][part:, :].astype(F32)
    for at in range(1, 8):
        vec = vec + piece_refs[at][part:, :].astype(F32)
    for at in range(8):
        vec_refs[at][...] = vec[at // 2 : at // 2 + 1, (at % 2) * part : (at % 2 + 1) * part]
    vec_refs[8][...] = jnp.concatenate([vec[4:5], vec[5:6]], 1)


def input_grad_kernel(x_ref, d_resid_ref, vec_ref, *refs):
    unit, d_values = norm_back(x_ref[...].astype(F32), add_parts(refs[:-1]), vec_ref[0:1, :])
    refs[-1][...] = d_resid_ref[...] + d_values


def scatter_pairs(kept, sent):
    swapped = ctx_swap(sent, 1)
    return [kept[0], swapped[0]], [kept[step] + swapped[step] for step in (1, 2, 3)]


def scatter_half(pairs):
    by_x, by_y, diag = pairs
    half = by_x.shape[0] // 2
    sent_x = ctx_swap(jnp.concatenate([by_x[:half], diag[:half]]), 2)
    return sent_x, ctx_swap(jnp.concatenate([by_y[half:], diag[half:]]), 4)


def scatter_other(own, pairs, from_x, from_y):
    by_x, by_y, _ = pairs
    half = by_x.shape[0] // 2
    rest = ctx_swap(by_y[:half] + from_x[half:], 4), ctx_swap(by_x[half:] + from_y[half:], 2)
    return own + [jnp.concatenate([from_x[:half], from_y[:half]]), jnp.concatenate(rest)]


def scatter_rest(own, pairs):
    return own + [ctx_swap(pair, 2 * (at + 1)) for at, pair in enumerate(pairs)]


def gather_direct(block):
    return ctx_swap(block, 2), ctx_swap(block, 4), ctx_swap(block, 6)


def gather_pairs(block, near):
    parts = [block] + list(near)
    return [item for part in parts for item in (part, ctx_swap(part, 1))]


def gather_near(block):
    return ctx_swap(block, 2), ctx_swap(block, 4), ctx_swap(block, 1)


def gather_far(block, near, ready=()):
    by_x, by_y, own_pair = near
    half = block.shape[0] // 2
    diag = jnp.concatenate([ctx_swap(by_y[:half], 2), ctx_swap(by_x[half:], 4)])
    pair_x = ctx_swap(by_x, 1)
    pair_y = ctx_swap(by_y, 1)
    return [block, own_pair, by_x, pair_x, by_y, pair_y, diag, ctx_swap(tie(diag, *ready), 1)]


def shards_fast(
    block_in,
    out_grad,
    ln1_gain,
    ln1_shift,
    qkv_weight,
    query_bias,
    value_bias,
    proj_weight,
    proj_bias,
    ln2_gain,
    ln2_shift,
    up_weight,
    up_bias,
    down_weight,
    down_bias,
):
    seq_count, rows, model_dim = block_in.shape
    length = 8 * rows
    width, part = model_dim // 8, model_dim // 4
    units = up_bias.shape[0]
    hidden = units // 2
    heads = width // HEAD_DIM
    own, here = lax.axis_index("ctx"), lax.axis_index("fsdp")
    eight, four = jnp.arange(8, dtype=jnp.int32), jnp.arange(4, dtype=jnp.int32)
    spots = jnp.concatenate(
        [own[None], eight ^ own, lax.rem(here - four + 4, 4), four ^ here]
    ).astype(jnp.int32)
    x = block_in.reshape(rows, model_dim)
    dy = out_grad.reshape(rows, model_dim)
    token = (rows, model_dim)
    half = ((4,) + token, BF16)

    x_near = gather_direct(x)
    vectors = [ln1_gain, ln1_shift, query_bias, value_bias, proj_bias, ln2_gain, ln2_shift]
    vectors = sum(
        jnp.pad(item.astype(F32), (at * part, 16 * part - at * part - item.shape[0]))
        for at, item in enumerate(vectors + [down_bias, up_bias])
    )
    (first,) = call(
        pack_first_kernel,
        "pack_first",
        [((4 * part + 32, width), BF16)],
        [SMEM] + [ANY] * 2 + [VMEM],
        [pltpu.VMEM((part // 8, model_dim), BF16), pltpu.SemaphoreType.DMA((4,))],
        cost=1,
    )(spots, qkv_weight, proj_weight, vectors)
    (second,) = call(
        pack_second_kernel,
        "pack_second",
        [((2 * part, hidden), BF16)],
        [SMEM] + [ANY] * 2,
        [pltpu.SemaphoreType.DMA((6,))],
        cost=1,
    )(spots, up_weight, tie(down_weight, first))
    first = jnp.stack([first, depth_swap(first, 2)])
    first = (first, depth_swap(first, 1))
    x_parts = gather_pairs(x, x_near)
    proj_slices = [first[at % 2][at // 2, 3 * part + 32 :] for at in range(4)]
    proj_slices = jnp.stack(proj_slices).reshape(4, 8, part // 8, width).transpose(0, 2, 1, 3)
    joined = jnp.concatenate([dy, proj_slices.reshape(part // 2, model_dim)])
    joined_near = gather_direct(joined)
    second_far = depth_swap(tie(second, first[1]), 2)

    normed, qkv_full, qkv, attn, attn_trans, log_total, vec, ubias = call(
        functools.partial(attend_fast_kernel, 512),
        "attend",
        [
            ((length, model_dim), BF16),
            ((model_dim, 3 * width), BF16),
            ((length, 3 * width), BF16),
            ((8, rows, width), BF16),
            ((width, length), F32),
            ((heads, length), F32),
            ((16, model_dim), F32),
            ((1, hidden), F32),
        ],
        [SMEM] + [VMEM] * 10,
        [
            pltpu.VMEM((heads, length, HEAD_DIM), BF16),
            pltpu.VMEM((heads, length, HEAD_DIM), BF16),
            pltpu.VMEM((width, length), BF16),
            pltpu.VMEM((8,) + token, BF16),
            pltpu.SemaphoreType.DMA((8,)),
        ],
        [ANY] + [VMEM] * 7,
        limit=58,
        cost=20,
    )(spots, *x_parts, *first)
    attn, second_far = lax.optimization_barrier((attn, second_far))
    second_pair = jnp.stack([second, second_far])
    attn = lax.all_to_all(tie(attn, second_pair), "ctx", 0, 0, tiled=False)
    attn, *joined_near = lax.optimization_barrier((attn,) + joined_near)
    second_pair = (second_pair, depth_swap(second_pair, 1))
    joined = gather_pairs(joined, joined_near)
    resid, m, proj_full, attn_low = call(
        mix_kernel,
        "mix",
        [(token, F32), (token, BF16), ((model_dim, model_dim), BF16), (token, BF16)],
        [SMEM] + [VMEM] * 3 + [ANY] * 8,
        [pltpu.SemaphoreType.DMA((32,))],
    )(spots, x, vec, attn, *joined)
    m_near = gather_near(m)
    m_parts = gather_far(m, m_near)
    m_parts[6] = tie(m_parts[6], second_pair[1])

    kept, sent, y_kept, y_sent, w_kept, w_sent, d_ubias = call(
        feed_fast_kernel,
        "feed",
        [half] * 4 + [((2, 2 * part, hidden), BF16)] * 2 + [((1, hidden), F32)],
        [SMEM] + [ANY] * 16 + [VMEM] * 3,
        [
            pltpu.VMEM((hidden, model_dim), BF16),
            pltpu.VMEM((model_dim, hidden), BF16),
            pltpu.VMEM((length, model_dim), BF16),
            pltpu.VMEM((length, model_dim), BF16),
            pltpu.VMEM((8,) + token, BF16),
            pltpu.VMEM((length, hidden), BF16),
            pltpu.VMEM((length, hidden), BF16),
            pltpu.SemaphoreType.DMA((16,)),
            pltpu.SemaphoreType.DMA((8,)),
        ],
        [ANY] * 2 + [VMEM] * 5,
        limit=40,
        cost=20,
    )(spots, *m_parts, *joined, *second_pair, ubias)
    w_swapped = depth_swap(w_sent, 1)
    mine, pairs = scatter_pairs(kept, sent)
    d_m_parts = scatter_rest(mine, pairs)
    y_mine, y_pairs = scatter_pairs(y_kept, y_sent)

    proj_half = ((4, part // 2, model_dim), BF16)
    w_pair = (w_kept.astype(F32) + w_swapped.astype(F32)).astype(BF16)
    w_far = depth_swap(w_pair[1], 2)
    d_resid, d_attn, sums, proj_kept, proj_sent = call(
        mix_back_kernel,
        "mix_back",
        [(token, F32), ((8, rows, width), BF16), ((8, model_dim), F32), proj_half, proj_half],
        [SMEM] + [VMEM] * 10,
        [pltpu.VMEM((model_dim, model_dim), BF16)],
        after=[w_pair, y_pairs[0]],
        cost=0,
    )(spots, dy, resid, vec, proj_full, attn_low, *d_m_parts)
    y_parts = scatter_rest(y_mine, y_pairs)
    proj_mine, proj_pairs = scatter_pairs(proj_kept, proj_sent)
    d_attn = lax.all_to_all(d_attn, "ctx", 0, 0, tiled=False)
    d_attn, w_far = lax.optimization_barrier((d_attn, w_far) + tuple(y_parts[2:]))[:2]
    d_feed = (w_pair[0].astype(F32) + w_far.astype(F32)).astype(BF16)
    feed_near = gather_direct(d_feed)
    proj_halves = scatter_half(proj_pairs)

    d_qkv, kept, sent, d_qkv_sum = attend_grad(
        spots[SPOT_CTX : SPOT_CTX + 8],
        qkv,
        d_attn,
        attn_trans,
        log_total,
        qkv_full,
    )
    sent, *travelled = lax.optimization_barrier((sent,) + proj_halves + feed_near)
    proj_parts = scatter_other(proj_mine, proj_pairs, *travelled[:2])
    feed_parts = gather_pairs(d_feed, travelled[2:])
    mine, pairs = scatter_pairs(kept, sent)
    d_x_halves = scatter_half(pairs)
    d_first = first_sums(x_parts, kept, tie(sent, *pairs))
    last = call(
        pack_last_kernel,
        "pack_last",
        [((2, part + 16, 4 * width), BF16)] * 2,
        [SMEM] + [VMEM] * 10,
        [
            pltpu.VMEM((8, model_dim), F32),
            pltpu.VMEM((1, units), F32),
            pltpu.VMEM((part // 2, model_dim), F32),
        ],
        cost=0,
    )(spots, normed, d_qkv, d_first, d_qkv_sum, sums, d_ubias, *proj_parts)
    last_swapped = depth_swap(last[1], 1)
    last = (last[0].astype(F32) + last_swapped.astype(F32)).astype(BF16)
    last_far = depth_swap(last[1], 2)
    last_far, *d_x_halves = lax.optimization_barrier((last_far,) + d_x_halves)
    d_x_parts = scatter_other(mine, pairs, *d_x_halves)
    last = (last[0].astype(F32) + last_far.astype(F32)).astype(BF16)
    (d_input,) = call(
        input_grad_kernel, "input_grad", [(token, F32)], [VMEM] * 7
    )(x, d_resid, vec, *d_x_parts)
    last = gather_pairs(last, gather_direct(last))
    final_sum = sum(item.astype(F32) for item in y_parts)
    block_out = (resid + final_sum + vec[7]).astype(BF16)
    d_up, d_down = place_feed(
        spots[SPOT_CTX : SPOT_CTX + 8],
        feed_parts,
        part,
        model_dim,
        units,
        4,
    )
    placed = call(
        place_last_kernel,
        "place_last",
        [((part, 3 * model_dim), F32), ((part, model_dim), F32)]
        + [((1, part), F32)] * 8
        + [((1, units), F32)],
        [SMEM] + [VMEM] * 8,
    )(spots, *last)
    d_weight_qkv, d_proj = placed[:2]
    d_vec = [item.reshape(-1) for item in placed[2:]]
    return (
        block_out.reshape(block_in.shape),
        d_input.reshape(block_in.shape),
        d_vec[0],
        d_vec[1],
        d_weight_qkv,
        d_vec[2],
        d_vec[3],
        d_proj,
        d_vec[4],
        d_vec[5],
        d_vec[6],
        d_up,
        d_vec[8],
        d_down,
        d_vec[7],
    )


def solution(mesh):
    rows, matrix, vector = P("fsdp", "ctx", None), P("fsdp", None), P("fsdp")
    in_specs = (
        rows,
        rows,
        vector,
        vector,
        matrix,
        vector,
        vector,
        matrix,
        vector,
        vector,
        vector,
        matrix,
        vector,
        matrix,
        vector,
    )
    out_specs = (rows, rows) + in_specs[2:]
    fast = mesh.shape["ctx"] == 8 and mesh.shape["fsdp"] == 4
    shards = shards_fast if fast else shards_any
    return jax.shard_map(shards, mesh=mesh, in_specs=in_specs, out_specs=out_specs, check_vma=False)
```

```python
import functools
import math

import jax
import jax.numpy as jnp
from jax import lax
from jax.experimental import pallas as pl
from jax.experimental.pallas import tpu as pltpu
from jax.sharding import PartitionSpec as P

HEADS = 16
HEAD_DIM = 64

EPSILON = 1e-05
GELU_COEF = 0.7978845608028654
MASKED = -1e30
SCORE_SCALE = HEAD_DIM ** (-0.5)
EXP2_SCALE = SCORE_SCALE / math.log(2.0)
F32 = jnp.float32
BF16 = jnp.bfloat16
SMEM = pl.BlockSpec(memory_space=pltpu.SMEM)
VMEM = pl.BlockSpec(memory_space=pltpu.VMEM)


def layer_norm(values, gain_vec, shift_vec):
    center = values - jnp.mean(values, -1, keepdims=True)
    spread = jnp.mean(center * center, -1, keepdims=True)
    return center * lax.rsqrt(spread + EPSILON) * gain_vec + shift_vec


def contract_rows(left, right):
    return lax.dot_general(left, right, (((0,), (0,)), ((), ())), preferred_element_type=F32)


def times_trans(left, right):
    return lax.dot_general(left, right, (((1,), (1,)), ((), ())), preferred_element_type=F32)


def times(left, right):
    return jnp.dot(left, right, preferred_element_type=F32)


def ctx_swap(value, bits):
    size = lax.axis_size("ctx")
    return lax.ppermute(value, "ctx", [(at, at ^ bits) for at in range(size)])


def ctx_places():
    size = lax.axis_size("ctx")
    order = jnp.arange(size, dtype=jnp.int32)
    return jnp.bitwise_xor(order, lax.axis_index("ctx")) if size == 8 else order


def ctx_gather(block):
    size = lax.axis_size("ctx")
    if size != 8:
        whole = lax.all_gather(block, "ctx", axis=0)
        return [whole[at] for at in range(size)]
    half = block.shape[0] // 2
    by_x = ctx_swap(block, 2)
    by_y = ctx_swap(block, 4)
    own_pair = ctx_swap(block, 1)
    diag = jnp.concatenate([ctx_swap(by_y[:half], 2), ctx_swap(by_x[half:], 4)])
    pair_x = ctx_swap(by_x, 1)
    pair_y = ctx_swap(by_y, 1)
    pair_diag = ctx_swap(diag, 1)
    return [block, own_pair, by_x, pair_x, by_y, pair_y, diag, pair_diag]


def ctx_scatter(kept, sent):
    if lax.axis_size("ctx") != 8:
        blocks = jnp.stack([kept, sent], 1).reshape((-1,) + kept.shape[1:])
        return lax.psum_scatter(blocks, "ctx", scatter_dimension=0, tiled=False).astype(F32)
    swapped = ctx_swap(sent, 1)
    total = kept[0].astype(F32) + swapped[0].astype(F32)
    for step in (1, 2, 3):
        pair = kept[step] + swapped[step]
        total = total + ctx_swap(pair, 2 * step).astype(F32)
    return total


def depth_shift(value, step):
    size = lax.axis_size("fsdp")
    return lax.ppermute(value, "fsdp", [(at, (at + step) % size) for at in range(size)])


def depth_swap(value, bits):
    size = lax.axis_size("fsdp")
    return lax.ppermute(value, "fsdp", [(at, at ^ bits) for at in range(size)])


def depth_places():
    size = lax.axis_size("fsdp")
    order = jnp.arange(size, dtype=jnp.int32)
    return lax.rem(lax.axis_index("fsdp") - order + size, size) if size == 4 else order


def depth_gather(block):
    size = lax.axis_size("fsdp")
    if size != 4:
        whole = lax.all_gather(block, "fsdp", axis=0)
        return [whole[at] for at in range(size)]
    return [block] + [depth_shift(block, step) for step in range(1, size)]


def depth_scatter(blocks):
    size = lax.axis_size("fsdp")
    if size != 4:
        return lax.psum_scatter(blocks, "fsdp", scatter_dimension=0, tiled=False).astype(F32)
    here = lax.axis_index("fsdp")
    total = lax.dynamic_index_in_dim(blocks, here, 0, False).astype(F32)
    for step in range(1, size):
        part = lax.dynamic_index_in_dim(blocks, lax.rem(here + step, size), 0, False)
        total = total + depth_shift(part, step).astype(F32)
    return total


def cost_of(microseconds):
    return pl.CostEstimate(flops=microseconds * 10**9, bytes_accessed=0, transcendentals=0)


def causal(rows, columns):
    keys = lax.broadcasted_iota(jnp.int32, (rows, columns), 0)
    queries = lax.broadcasted_iota(jnp.int32, (rows, columns), 1)
    return keys <= queries


def rows_at(place, rows):
    return pl.ds(pl.multiple_of(place * rows, rows), rows)


def normalize(values):
    center = values - jnp.mean(values, -1, keepdims=True)
    spread = jnp.mean(center * center, -1, keepdims=True)
    return center * lax.rsqrt(spread + EPSILON)


def attend_kernel(blocks, depth, tile, places_ref, depths_ref, *refs):
    x_refs, w_refs = refs[:blocks], refs[blocks : blocks + depth]
    (
        vec_ref,
        bias_ref,
        normed_ref,
        w_ref,
        qkv_ref,
        out_ref,
        out_t_ref,
        log_ref,
        q_ref,
        k_ref,
        v_t_ref,
    ) = refs[blocks + depth :]
    length, width = out_ref.shape
    heads = width // HEAD_DIM
    rows = length // blocks
    part = w_ref.shape[0] // depth
    for at in range(depth):
        place = rows_at(depths_ref[at], part)
        for column in range(3):
            w_ref[place, column * width : (column + 1) * width] = w_refs[at][
                column * part : (column + 1) * part, :
            ]
    for block in range(blocks):
        place = rows_at(places_ref[block], rows)
        normed = normalize(x_refs[block][...].astype(F32)) * vec_ref[0:1, :] + vec_ref[1:2, :]
        normed = normed.astype(BF16)
        normed_ref[place, :] = normed
        qkv = (times(normed, w_ref[...]) + bias_ref[...]).astype(BF16)
        qkv_ref[place, :] = qkv
        for head in range(heads):
            low, high = head * HEAD_DIM, (head + 1) * HEAD_DIM
            q_ref[head, place, :] = qkv[:, low:high]
            k_ref[head, place, :] = qkv[:, width + low : width + high]
        v_t_ref[:, place] = qkv[:, 2 * width :].T
    for q_tile in range(length // tile):
        columns = slice(q_tile * tile, (q_tile + 1) * tile)
        queries = [q_ref[head, columns, :] for head in range(heads)]

        def visit(k_tile, state, masked):
            start = k_tile * tile
            result = []
            for head in range(heads):
                run_max, run_sum, run_acc = state[head]
                scores = times_trans(k_ref[head, pl.ds(start, tile), :], queries[head])
                if masked:
                    scores = jnp.where(causal(tile, tile), scores, MASKED)
                new_max = jnp.maximum(run_max, jnp.max(scores, 0, keepdims=True))
                weights = jnp.exp2(scores * EXP2_SCALE - new_max * EXP2_SCALE)
                factor = jnp.exp2((run_max - new_max) * EXP2_SCALE)
                new_sum = run_sum * factor + jnp.sum(weights, 0, keepdims=True)
                low, high = head * HEAD_DIM, (head + 1) * HEAD_DIM
                values = v_t_ref[low:high, pl.ds(start, tile)]
                new_acc = run_acc * factor + times(values, weights.astype(BF16))
                result.append((new_max, new_sum, new_acc))
            return result

        state = [
            (
                jnp.full((1, tile), MASKED, F32),
                jnp.zeros((1, tile), F32),
                jnp.zeros((HEAD_DIM, tile), F32),
            )
        ] * heads
        for k_tile in range(q_tile):
            state = visit(k_tile, state, False)
        state = visit(q_tile, state, True)
        result = []
        for head in range(heads):
            run_max, run_sum, run_acc = state[head]
            result.append(run_acc / run_sum)
            log_ref[head : head + 1, columns] = run_max * EXP2_SCALE + jnp.log2(run_sum)
        result = jnp.concatenate(result, 0) if heads > 1 else result[0]
        out_t_ref[:, columns] = result
        out_ref[columns, :] = result.T.astype(BF16)


def attend_grad_kernel(
    blocks, tile, places_ref, qkv_ref, out_t_ref, log_ref, w_ref, d_out_ref, *refs
):
    d_qkv_ref, kept_ref, sent_ref, sum_ref = refs[:4]
    q_ref, k_ref, v_ref, k_t_ref, do_ref, delta_ref, dq_t_ref, dk_ref, dv_ref = refs[4:]
    width, length = out_t_ref.shape
    heads = width // HEAD_DIM
    rows = length // blocks
    for block in range(blocks):
        here = slice(block * rows, (block + 1) * rows)
        part = qkv_ref[here, :]
        for head in range(heads):
            low, high = head * HEAD_DIM, (head + 1) * HEAD_DIM
            q_ref[head, here, :] = part[:, low:high]
            k_ref[head, here, :] = part[:, width + low : width + high]
            v_ref[head, here, :] = part[:, 2 * width + low : 2 * width + high]
        k_t_ref[:, here] = part[:, width : 2 * width].T
        d_out = d_out_ref[block]
        product = d_out.astype(F32).T * out_t_ref[:, here]
        for head in range(heads):
            low, high = head * HEAD_DIM, (head + 1) * HEAD_DIM
            do_ref[head, here, :] = d_out[:, low:high]
            delta_ref[head : head + 1, here] = jnp.sum(product[low:high], 0, keepdims=True)
    dq_t_ref[...] = jnp.zeros_like(dq_t_ref)
    tiles = length // tile
    for k_tile in range(tiles):
        key_rows = slice(k_tile * tile, (k_tile + 1) * tile)

        def visit(q_tile, state, masked):
            query_rows = pl.ds(q_tile * tile, tile)
            result = []
            for head in range(heads):
                d_key, d_value = state[head]
                low, high = head * HEAD_DIM, (head + 1) * HEAD_DIM
                queries = q_ref[head, query_rows, :]
                d_out = do_ref[head, query_rows, :]
                scores = times_trans(k_ref[head, key_rows, :], queries)
                log_row = log_ref[head : head + 1, query_rows]
                probs = jnp.exp2(scores * EXP2_SCALE - log_row)
                if masked:
                    probs = jnp.where(causal(tile, tile), probs, 0.0)
                d_probs = times_trans(v_ref[head, key_rows, :], d_out)
                d_scores = (probs * (d_probs - delta_ref[head : head + 1, query_rows])).astype(BF16)
                d_value = d_value + times(probs.astype(BF16), d_out)
                d_key = d_key + times(d_scores, queries)
                dq_t_ref[low:high, query_rows] += times(k_t_ref[low:high, key_rows], d_scores)
                result.append((d_key, d_value))
            return result

        state = [(jnp.zeros((tile, HEAD_DIM), F32), jnp.zeros((tile, HEAD_DIM), F32))] * heads
        state = visit(k_tile, state, True)
        for q_tile in range(k_tile + 1, tiles):
            state = visit(q_tile, state, False)
        for head in range(heads):
            dk_ref[head, key_rows, :] = state[head][0]
            dv_ref[head, key_rows, :] = state[head][1]
    total = jnp.zeros((1, 3 * width), F32)
    for block in range(blocks):
        place = rows_at(places_ref[block], rows)
        d_key = [dk_ref[head, place, :] * SCORE_SCALE for head in range(heads)]
        d_value = [dv_ref[head, place, :] for head in range(heads)]
        parts = [dq_t_ref[:, place].T * SCORE_SCALE] + d_key + d_value
        d_qkv = jnp.concatenate(parts, 1).astype(BF16)
        d_qkv_ref[place, :] = d_qkv
        total = total + jnp.sum(d_qkv.astype(F32), 0, keepdims=True)
        out = sent_ref if block % 2 else kept_ref
        out[block // 2] = times_trans(d_qkv, w_ref[...]).astype(BF16)
    sum_ref[...] = total


def attend(places, depths, x_parts, w_parts, vectors, bias):
    blocks, depth = len(x_parts), len(w_parts)
    rows, model_dim = x_parts[0].shape
    width = bias.shape[1] // 3
    length = rows * blocks
    heads = width // HEAD_DIM
    tile = min(512, length)
    return pl.pallas_call(
        functools.partial(attend_kernel, blocks, depth, tile),
        out_shape=(
            jax.ShapeDtypeStruct((length, model_dim), BF16),
            jax.ShapeDtypeStruct((model_dim, 3 * width), BF16),
            jax.ShapeDtypeStruct((length, 3 * width), BF16),
            jax.ShapeDtypeStruct((length, width), BF16),
            jax.ShapeDtypeStruct((width, length), F32),
            jax.ShapeDtypeStruct((heads, length), F32),
        ),
        in_specs=[SMEM] * 2 + [VMEM] * (blocks + depth + 2),
        out_specs=(VMEM,) * 6,
        scratch_shapes=[
            pltpu.VMEM((heads, length, HEAD_DIM), BF16),
            pltpu.VMEM((heads, length, HEAD_DIM), BF16),
            pltpu.VMEM((width, length), BF16),
        ],
        compiler_params=pltpu.CompilerParams(vmem_limit_bytes=32 << 20),
        cost_estimate=cost_of(10),
        name="attend",
    )(places, depths, *x_parts, *w_parts, vectors, bias)


def attend_grad(places, qkv, d_out, out_t, log_total, w_full):
    length, width = qkv.shape[0], qkv.shape[1] // 3
    model_dim = w_full.shape[0]
    blocks = places.shape[0]
    heads = width // HEAD_DIM
    tile = min(512, length)
    per_head = pltpu.VMEM((heads, length, HEAD_DIM), BF16)
    half = jax.ShapeDtypeStruct((blocks // 2, length // blocks, model_dim), BF16)
    return pl.pallas_call(
        functools.partial(attend_grad_kernel, blocks, tile),
        out_shape=(
            jax.ShapeDtypeStruct((length, 3 * width), BF16),
            half,
            half,
            jax.ShapeDtypeStruct((1, 3 * width), F32),
        ),
        in_specs=[SMEM] + [VMEM] * 5,
        out_specs=(VMEM,) * 4,
        scratch_shapes=[
            per_head,
            per_head,
            per_head,
            pltpu.VMEM((width, length), BF16),
            per_head,
            pltpu.VMEM((heads, length), F32),
            pltpu.VMEM((width, length), F32),
            pltpu.VMEM((heads, length, HEAD_DIM), F32),
            pltpu.VMEM((heads, length, HEAD_DIM), F32),
        ],
        compiler_params=pltpu.CompilerParams(vmem_limit_bytes=32 << 20),
        cost_estimate=cost_of(20),
        name="attend_grad",
    )(places, qkv, out_t, log_total, w_full, d_out)


def feed_kernel(blocks, depth, depths_ref, *refs):
    m_refs, dy_refs = refs[:blocks], refs[blocks : 2 * blocks]
    w_refs = refs[2 * blocks : 2 * blocks + depth]
    (
        bias_ref,
        kept_ref,
        sent_ref,
        m_ref,
        dy_ref,
        hidden_ref,
        d_pre_ref,
        sum_ref,
        down_ref,
        up_ref,
    ) = refs[2 * blocks + depth :]
    rows = m_refs[0].shape[0]
    model_dim, hidden = up_ref.shape
    part, share = model_dim // depth, hidden // depth
    for at in range(depth):
        up_ref[rows_at(depths_ref[at], part), :] = w_refs[at][:part, :]
        place = rows_at(depths_ref[at], share)
        for cut in range(model_dim // hidden):
            first = part + cut * share
            down_ref[place, cut * hidden : (cut + 1) * hidden] = w_refs[at][
                first : first + share, :
            ]
    total = jnp.zeros((1, hidden), F32)
    for block in range(blocks):
        here = slice(block * rows, (block + 1) * rows)
        m_ref[here, :] = m_refs[block][...]
        dy_ref[here, :] = dy_refs[block][...]
        pre_act = times(m_refs[block][...], up_ref[...]) + bias_ref[...]
        d_hidden = times_trans(dy_refs[block][...], down_ref[...])
        square = pre_act * pre_act
        bent = jnp.tanh(GELU_COEF * (pre_act + 0.044715 * (square * pre_act)))
        half_one = 0.5 + 0.5 * bent
        hidden_ref[here, :] = (pre_act * half_one).astype(BF16)
        slope = half_one + (0.5 * pre_act) * (1.0 - bent * bent) * (
            GELU_COEF + (3.0 * 0.044715 * GELU_COEF) * square
        )
        d_pre = (d_hidden * slope).astype(BF16)
        d_pre_ref[here, :] = d_pre
        total = total + jnp.sum(d_pre.astype(F32), 0, keepdims=True)
        out = sent_ref if block % 2 else kept_ref
        out[block // 2] = times_trans(d_pre, up_ref[...]).astype(BF16)
    sum_ref[...] = total


def feed(depths, m_parts, dy_parts, w_parts, bias):
    blocks, depth = len(m_parts), len(w_parts)
    rows, model_dim = m_parts[0].shape
    hidden = bias.shape[1]
    length = rows * blocks
    half = jax.ShapeDtypeStruct((blocks // 2, rows, model_dim), BF16)
    whole = jax.ShapeDtypeStruct((length, model_dim), BF16)
    units = jax.ShapeDtypeStruct((length, hidden), BF16)
    return pl.pallas_call(
        functools.partial(feed_kernel, blocks, depth),
        out_shape=(
            half,
            half,
            whole,
            whole,
            units,
            units,
            jax.ShapeDtypeStruct((1, hidden), F32),
            jax.ShapeDtypeStruct((hidden, model_dim), BF16),
        ),
        in_specs=[SMEM] + [VMEM] * (2 * blocks + depth + 1),
        out_specs=(VMEM,) * 8,
        scratch_shapes=[pltpu.VMEM((model_dim, hidden), BF16)],
        compiler_params=pltpu.CompilerParams(vmem_limit_bytes=32 << 20),
        cost_estimate=cost_of(10),
        name="feed",
    )(depths, *m_parts, *dy_parts, *w_parts, bias)


def first_sums_kernel(blocks, *refs):
    x_refs = refs[:blocks]
    kept_ref, sent_ref, out_ref = refs[blocks:]
    gain = jnp.zeros((1, out_ref.shape[1]), F32)
    shift = gain
    for block in range(blocks):
        grad = (sent_ref if block % 2 else kept_ref)[block // 2].astype(F32)
        values = normalize(x_refs[block][...].astype(F32))
        gain = gain + jnp.sum(grad * values, 0, keepdims=True)
        shift = shift + jnp.sum(grad, 0, keepdims=True)
    out_ref[...] = jnp.concatenate([gain, shift], 0)


def first_sums(x_parts, kept, sent):
    blocks = len(x_parts)
    rows, model_dim = x_parts[0].shape
    return pl.pallas_call(
        functools.partial(first_sums_kernel, blocks),
        out_shape=jax.ShapeDtypeStruct((2, model_dim), F32),
        in_specs=[VMEM] * (blocks + 2),
        out_specs=VMEM,
        compiler_params=pltpu.CompilerParams(vmem_limit_bytes=32 << 20),
        cost_estimate=cost_of(0),
        name="first_sums",
    )(*x_parts, kept, sent)


def place_feed_kernel(blocks, depth, places_ref, *refs):
    piece_refs, (up_ref, down_ref) = refs[:blocks], refs[blocks:]
    part, share = up_ref.shape[0], up_ref.shape[1] // depth // blocks
    hidden = share * depth
    for at in range(blocks):
        place = places_ref[at]
        for cut in range(depth):
            start = pl.multiple_of(cut * share * blocks + place * share, share)
            up_ref[:, pl.ds(start, share)] = piece_refs[at][
                :part, cut * share : (cut + 1) * share
            ].astype(F32)
        for cut in range(down_ref.shape[1] // hidden):
            first = part + cut * share
            down_ref[rows_at(place, share), cut * hidden : (cut + 1) * hidden] = piece_refs[at][
                first : first + share, :
            ].astype(F32)


def place_feed(places, pieces, part, model_dim, units, depth):
    blocks = len(pieces)
    share = units // blocks
    if share % 128 == 0:
        return pl.pallas_call(
            functools.partial(place_feed_kernel, blocks, depth),
            out_shape=(
                jax.ShapeDtypeStruct((part, units * depth), F32),
                jax.ShapeDtypeStruct((units, model_dim), F32),
            ),
            in_specs=[SMEM] + [VMEM] * blocks,
            out_specs=(VMEM,) * 2,
            compiler_params=pltpu.CompilerParams(vmem_limit_bytes=32 << 20),
            name="place_feed",
        )(places, *pieces)
    pieces = jnp.stack(pieces).astype(F32)
    up = pieces[:, :part].reshape(blocks, part, depth, share).transpose(1, 2, 0, 3)
    down = pieces[:, part:].reshape(blocks, -1, share, share * depth).transpose(0, 2, 1, 3)
    return up.reshape(part, -1), down.reshape(units, model_dim)


def place_heads_kernel(blocks, places_ref, *refs):
    piece_refs, (qkv_ref, proj_ref, vec_ref) = refs[:blocks], refs[blocks:]
    part, width = qkv_ref.shape[0], qkv_ref.shape[1] // 3 // blocks
    share = part // blocks
    for at in range(blocks):
        place = places_ref[at]
        for cut in range(3):
            start = pl.multiple_of(cut * width * blocks + place * width, width)
            qkv_ref[:, pl.ds(start, width)] = piece_refs[at][
                :part, cut * width : (cut + 1) * width
            ].astype(F32)
        for cut in range(blocks):
            proj_ref[rows_at(place, share), cut * width : (cut + 1) * width] = piece_refs[at][
                cut * share : (cut + 1) * share, 3 * width :
            ].astype(F32)
    vec = piece_refs[0][part:, :].astype(F32)
    for at in range(1, blocks):
        vec = vec + piece_refs[at][part:, :].astype(F32)
    vec_ref[...] = vec


def place_heads(places, pieces, part, model_dim):
    blocks = len(pieces)
    width, extra = model_dim // blocks, pieces[0].shape[0] - part
    if width % 128 == 0:
        return pl.pallas_call(
            functools.partial(place_heads_kernel, blocks),
            out_shape=(
                jax.ShapeDtypeStruct((part, 3 * model_dim), F32),
                jax.ShapeDtypeStruct((part, model_dim), F32),
                jax.ShapeDtypeStruct((extra, 4 * width), F32),
            ),
            in_specs=[SMEM] + [VMEM] * blocks,
            out_specs=(VMEM,) * 3,
            compiler_params=pltpu.CompilerParams(vmem_limit_bytes=32 << 20),
            name="place_heads",
        )(places, *pieces)
    pieces = jnp.stack(pieces).astype(F32)
    qkv = pieces[:, :part, : 3 * width].reshape(blocks, part, 3, width).transpose(1, 2, 0, 3)
    proj = pieces[:, :part, 3 * width :].reshape(blocks, blocks, part // blocks, width)
    proj = proj.transpose(0, 2, 1, 3).reshape(part, model_dim)
    return qkv.reshape(part, -1), proj, jnp.sum(pieces[:, part:], 0)


def shards_any(
    block_in,
    out_grad,
    ln1_gain,
    ln1_shift,
    qkv_weight,
    query_bias,
    value_bias,
    proj_weight,
    proj_bias,
    ln2_gain,
    ln2_shift,
    up_weight,
    up_bias,
    down_weight,
    down_bias,
):
    seq_count, blk_len, model_dim = block_in.shape
    ctx_size, depth = lax.axis_size("ctx"), lax.axis_size("fsdp")
    ctx_index, depth_index = lax.axis_index("ctx"), lax.axis_index("fsdp")
    places, depths = ctx_places(), depth_places()
    seq_len = ctx_size * blk_len
    width = model_dim // ctx_size
    part = model_dim // depth
    units = up_bias.shape[0]
    share = units // ctx_size
    hidden = share * depth
    cuts = model_dim // hidden

    own_in = block_in.reshape(blk_len, model_dim)
    own_dy = out_grad.reshape(blk_len, model_dim)

    def ctx_columns(value, columns, axis):
        return lax.dynamic_slice_in_dim(value, ctx_index * columns, columns, axis)

    x_parts = ctx_gather(own_in)
    vectors = jnp.concatenate(
        [
            ln1_gain,
            ln1_shift,
            query_bias,
            value_bias,
            proj_bias,
            ln2_gain,
            ln2_shift,
            down_bias,
            up_bias,
        ]
    )
    slices = [
        lax.dynamic_slice_in_dim(qkv_weight, at * model_dim + ctx_index * width, width, 1)
        for at in range(3)
    ]
    first = depth_gather(jnp.concatenate(slices + [vectors.reshape(-1, width)]))
    vec = jnp.stack([piece[3 * part :] for piece in first]).reshape(depth, -1)
    vec = jnp.take(vec, depths, axis=0).astype(F32)
    ubias = ctx_columns(vec[:, 8 * part :], share, 1).reshape(1, hidden)
    vec = vec[:, : 8 * part].reshape(depth, 8, part).transpose(1, 0, 2).reshape(8, model_dim)
    gain_two, shift_two = vec[5], vec[6]
    qkv_bias = jnp.concatenate(
        [ctx_columns(vec[2], width, 0), jnp.zeros((width,), F32), ctx_columns(vec[3], width, 0)]
    ).reshape(1, 3 * width)

    normed, qkv_full, qkv, attn_heads, attn_trans, log_total = attend(
        places, depths, x_parts, first, vec, qkv_bias
    )
    attn_low = lax.all_to_all(
        attn_heads.reshape(ctx_size, blk_len, width), "ctx", 0, 0, tiled=False
    )
    attn_low = attn_low.transpose(1, 0, 2).reshape(blk_len, model_dim)

    up_slice = lax.dynamic_index_in_dim(
        up_weight.reshape(part, depth, ctx_size, share), ctx_index, 2, False
    ).reshape(part, hidden)
    down_slice = ctx_columns(down_weight, share, 0)
    down_cuts = [down_slice[:, at * hidden : (at + 1) * hidden] for at in range(cuts)]
    second = depth_gather(jnp.concatenate([up_slice] + down_cuts))
    proj_rows = part // ctx_size
    proj_full = lax.all_gather(
        ctx_columns(proj_weight, proj_rows, 0), ("fsdp", "ctx"), axis=0, tiled=True
    )
    dy_parts = ctx_gather(own_dy)

    own_f = own_in.astype(F32)
    resid_one = own_f + times(attn_low, proj_full) + vec[4]
    normed_two = layer_norm(resid_one, gain_two, shift_two).astype(BF16)

    m_parts = ctx_gather(normed_two)
    kept, sent, all_two, all_dy, hidden_low, d_pre, d_ubias, down_full = feed(
        depths, m_parts, dy_parts, second, ubias
    )
    d_normed_two = ctx_scatter(kept, sent)
    final_part = times(hidden_low, down_full).astype(BF16)
    final_part = final_part.reshape(ctx_size // 2, 2, blk_len, model_dim)
    final_sum = ctx_scatter(final_part[:, 0], final_part[:, 1])
    block_out = (resid_one + final_sum + vec[7]).astype(BF16).reshape(block_in.shape)
    d_up = contract_rows(all_two, d_pre).astype(BF16).reshape(depth, part, hidden)
    d_down = contract_rows(hidden_low, all_dy).astype(BF16).reshape(depth, share, cuts, hidden)
    d_down = d_down.transpose(0, 2, 1, 3).reshape(depth, cuts * share, hidden)
    d_feed = depth_scatter(jnp.concatenate([d_up, d_down], 1)).astype(BF16)
    d_up, d_down = place_feed(places, ctx_gather(d_feed), part, model_dim, units, depth)

    norm_two_out, norm_two_pull = jax.vjp(layer_norm, resid_one, gain_two, shift_two)
    d_resid_part, d_gain_two, d_shift_two = norm_two_pull(d_normed_two)
    grad_f = own_dy.astype(F32)
    d_resid = grad_f + d_resid_part
    d_branch = d_resid.astype(BF16)
    d_attn = times_trans(d_branch, proj_full).astype(BF16)
    d_attn = d_attn.reshape(blk_len, ctx_size, width).transpose(1, 0, 2)
    d_attn = lax.all_to_all(d_attn, "ctx", 0, 0, tiled=False)
    d_proj = contract_rows(attn_low, d_branch).astype(BF16)
    d_proj = d_proj.reshape(depth, ctx_size, proj_rows, model_dim)
    d_proj = jnp.take(d_proj, places, axis=1).transpose(1, 0, 2, 3)
    d_proj = d_proj.reshape(ctx_size // 2, 2, part // ctx_size * depth, model_dim)
    d_proj = ctx_scatter(d_proj[:, 0], d_proj[:, 1]).astype(BF16)
    d_proj = d_proj.reshape(depth, proj_rows, ctx_size, width).transpose(0, 2, 1, 3)
    d_proj = d_proj.reshape(depth, part, width)

    d_qkv, kept, sent, d_qkv_sum = attend_grad(
        places, qkv, d_attn, attn_trans, log_total, qkv_full
    )
    d_normed_own = ctx_scatter(kept, sent)
    d_weight_qkv = contract_rows(normed, d_qkv).astype(BF16).reshape(depth, part, 3 * width)
    d_first = first_sums(x_parts, kept, sent)
    norm_one, norm_one_pull = jax.vjp(lambda value: layer_norm(value, vec[0], vec[1]), own_f)
    d_input = (d_resid + norm_one_pull(d_normed_own)[0]).reshape(block_in.shape)

    def widen(value, total):
        start = jnp.zeros(value.shape[:-1] + (total,), F32)
        return lax.dynamic_update_slice_in_dim(
            start, value, ctx_index * value.shape[-1], value.ndim - 1
        )

    small = [
        d_first[0],
        d_first[1],
        widen(d_qkv_sum[0, :width], model_dim),
        widen(d_qkv_sum[0, 2 * width :], model_dim),
        jnp.sum(d_branch.astype(F32), 0),
        d_gain_two,
        d_shift_two,
        jnp.sum(grad_f, 0),
    ]
    small = jnp.stack(small).reshape(8, depth, part).transpose(1, 0, 2).reshape(depth, 8 * part)
    small = jnp.concatenate([small, widen(d_ubias.reshape(depth, share), units)], 1)
    count = small.shape[1]
    small = small.astype(BF16).reshape(depth, -1, 4 * width)
    small = jnp.pad(small, ((0, 0), (0, -small.shape[1] % 16), (0, 0)))
    last = jnp.concatenate([jnp.concatenate([d_weight_qkv, d_proj], 2), small], 1)
    last = ctx_gather(depth_scatter(last).astype(BF16))
    d_weight_qkv, d_proj, small = place_heads(places, last, part, model_dim)
    small = small.reshape(-1)[:count]
    d_vec = small[: 8 * part].reshape(8, part)
    return (
        block_out,
        d_input,
        d_vec[0],
        d_vec[1],
        d_weight_qkv,
        d_vec[2],
        d_vec[3],
        d_proj,
        d_vec[4],
        d_vec[5],
        d_vec[6],
        d_up,
        small[8 * part :],
        d_down,
        d_vec[7],
    )


ANY = pl.BlockSpec(memory_space=pl.ANY)
HBM = pl.BlockSpec(memory_space=pltpu.HBM)


SPOT_OWN, SPOT_CTX, SPOT_FROM, SPOT_SWAP = 0, 1, 9, 13


def tie(value, *others):
    return lax.optimization_barrier((value,) + others)[0]


def call(kernel, name, outs, in_specs, scratch=(), out_specs=None, limit=16, after=(), cost=3):
    count = len(in_specs)

    def body(*refs):
        return kernel(*refs[:count], *refs[count + len(after) :])

    run = pl.pallas_call(
        body if after else kernel,
        out_shape=tuple(jax.ShapeDtypeStruct(shape, kind) for shape, kind in outs),
        in_specs=list(in_specs) + [ANY] * len(after),
        out_specs=tuple(out_specs or [VMEM] * len(outs)),
        scratch_shapes=list(scratch),
        compiler_params=pltpu.CompilerParams(vmem_limit_bytes=limit << 20),
        cost_estimate=cost_of(cost),
        name=name,
    )
    return lambda *args: run(*args, *after)


def lanes_at(place, size):
    return pl.ds(pl.multiple_of(place * size, size), size)


def run_copies(copies):
    for copy in copies:
        copy.start()
    for copy in copies:
        copy.wait()


def pack_first_kernel(spots_ref, qkv_ref, proj_ref, vec_ref, out_ref, proj_buf, sems):
    own = spots_ref[SPOT_OWN]
    part, model_dim = proj_ref.shape
    width = out_ref.shape[1]
    blocks = model_dim // width
    share = part // blocks
    copies = [
        pltpu.make_async_copy(
            qkv_ref.at[:, lanes_at(at * blocks + own, width)],
            out_ref.at[at * part : (at + 1) * part, :],
            sems.at[at],
        )
        for at in range(3)
    ]
    copies.append(pltpu.make_async_copy(proj_ref.at[rows_at(own, share), :], proj_buf, sems.at[3]))
    run_copies(copies)
    vec = vec_ref[...].reshape(1, 16 * part)
    vec = [vec[:, at * part : (at + 1) * part] for at in range(16)]
    vec = jnp.concatenate(vec, 0).astype(BF16)
    first = 3 * part
    out_ref[first : first + 16, :] = vec[:, :width]
    out_ref[first + 16 : first + 32, :] = vec[:, width:]
    first = first + 32
    for at in range(blocks):
        out_ref[first + at * share : first + (at + 1) * share, :] = proj_buf[
            :, at * width : (at + 1) * width
        ]


def pack_second_kernel(spots_ref, up_ref, down_ref, out_ref, sems):
    own = spots_ref[SPOT_OWN]
    part, hidden = up_ref.shape[0], out_ref.shape[1]
    share = hidden // 4
    blocks = up_ref.shape[1] // hidden
    copies = []
    for at in range(4):
        copies.append(
            pltpu.make_async_copy(
                up_ref.at[:, lanes_at(at * blocks + own, share)],
                out_ref.at[:part, at * share : (at + 1) * share],
                sems.at[at],
            )
        )
    for at in range(down_ref.shape[1] // hidden):
        first = part + at * share
        copies.append(
            pltpu.make_async_copy(
                down_ref.at[rows_at(own, share), at * hidden : (at + 1) * hidden],
                out_ref.at[first : first + share, :],
                sems.at[4 + at],
            )
        )
    run_copies(copies)


def attend_fast_kernel(tile, spots_ref, *refs):
    x_refs, w_refs = refs[:8], refs[8:10]
    (
        normed_ref,
        w_ref,
        qkv_ref,
        out_ref,
        out_t_ref,
        log_ref,
        vec_ref,
        ubias_ref,
        q_ref,
        k_ref,
        v_t_ref,
        normed_buf,
        sems,
    ) = refs[10:]
    blocks, rows, width = out_ref.shape
    length = blocks * rows
    heads = width // HEAD_DIM
    part = w_ref.shape[0] // 4
    own = spots_ref[SPOT_OWN]
    for at in range(4):
        source = spots_ref[SPOT_SWAP + at]
        piece = w_refs[at % 2].at[at // 2]
        place = rows_at(source, part)
        for column in range(3):
            w_ref[place, column * width : (column + 1) * width] = piece[
                column * part : (column + 1) * part, :
            ]
        for half in range(2):
            first = 3 * part + 16 * half
            vec_ref[:, lanes_at(source * 2 + half, width)] = piece[
                first : first + 16, :
            ].astype(F32)
    for at in range(4):
        rows_here = vec_ref[8:16, lanes_at(at * 2 + lax.rem(own, 2), width)]
        chosen = lax.broadcasted_iota(jnp.int32, (8, width), 0) == own // 2
        ubias_ref[:, at * width : (at + 1) * width] = jnp.sum(
            jnp.where(chosen, rows_here, 0.0), 0, keepdims=True
        )
    qbias, vbias = (vec_ref[at : at + 1, lanes_at(own, width)] for at in (2, 3))
    bias = jnp.concatenate([qbias, jnp.zeros((1, width), F32), vbias], 1)
    gain, shift = vec_ref[0:1, :], vec_ref[1:2, :]
    copies = []
    for block in range(blocks):
        place = rows_at(spots_ref[SPOT_CTX + block], rows)
        normed = (normalize(x_refs[block][...].astype(F32)) * gain + shift).astype(BF16)
        normed_buf[block] = normed
        copies.append(
            pltpu.make_async_copy(normed_buf.at[block], normed_ref.at[place, :], sems.at[block])
        )
        copies[-1].start()
        qkv = (times(normed, w_ref[...]) + bias).astype(BF16)
        qkv_ref[place, :] = qkv
        for head in range(heads):
            low, high = head * HEAD_DIM, (head + 1) * HEAD_DIM
            q_ref[head, place, :] = qkv[:, low:high]
            k_ref[head, place, :] = qkv[:, width + low : width + high]
        v_t_ref[:, place] = qkv[:, 2 * width :].T
    for q_tile in range(length // tile):
        columns = slice(q_tile * tile, (q_tile + 1) * tile)
        queries = [q_ref[head, columns, :] for head in range(heads)]

        def visit(k_tile, state, masked):
            start = k_tile * tile
            result = []
            for head in range(heads):
                run_max, run_sum, run_acc = state[head]
                scores = times_trans(k_ref[head, pl.ds(start, tile), :], queries[head])
                if masked:
                    scores = jnp.where(causal(tile, tile), scores, MASKED)
                new_max = jnp.maximum(run_max, jnp.max(scores, 0, keepdims=True))
                weights = jnp.exp2(scores * EXP2_SCALE - new_max * EXP2_SCALE)
                factor = jnp.exp2((run_max - new_max) * EXP2_SCALE)
                new_sum = run_sum * factor + jnp.sum(weights, 0, keepdims=True)
                low, high = head * HEAD_DIM, (head + 1) * HEAD_DIM
                values = v_t_ref[low:high, pl.ds(start, tile)]
                new_acc = run_acc * factor + times(values, weights.astype(BF16))
                result.append((new_max, new_sum, new_acc))
            return result

        state = [
            (
                jnp.full((1, tile), MASKED, F32),
                jnp.zeros((1, tile), F32),
                jnp.zeros((HEAD_DIM, tile), F32),
            )
        ] * heads
        for k_tile in range(q_tile):
            state = visit(k_tile, state, False)
        state = visit(q_tile, state, True)
        result = []
        for head in range(heads):
            run_max, run_sum, run_acc = state[head]
            result.append(run_acc / run_sum)
            log_ref[head : head + 1, columns] = run_max * EXP2_SCALE + jnp.log2(run_sum)
        result = jnp.concatenate(result, 0)
        out_t_ref[:, columns] = result
        result = result.T.astype(BF16)
        for at in range(tile // rows):
            out_ref[q_tile * (tile // rows) + at] = result[at * rows : (at + 1) * rows]
    for copy in copies:
        copy.wait()


def mix_kernel(spots_ref, x_ref, vec_ref, attn_ref, *refs):
    joined_refs, (resid_ref, m_ref, proj_ref, attn_low_ref, sems) = refs[:8], refs[8:]
    blocks, rows, width = attn_ref.shape
    share = proj_ref.shape[0] // 4 // blocks
    copies = []
    for at in range(blocks):
        for source in range(4):
            place = spots_ref[SPOT_SWAP + source] * blocks + spots_ref[SPOT_CTX + at]
            first = rows + source * share
            copies.append(
                pltpu.make_async_copy(
                    joined_refs[at].at[first : first + share, :],
                    proj_ref.at[rows_at(place, share), :],
                    sems.at[at * 4 + source],
                )
            )
            copies[-1].start()
        attn_low_ref[:, at * width : (at + 1) * width] = attn_ref[at]
    for copy in copies:
        copy.wait()
    resid = x_ref[...].astype(F32) + times(attn_low_ref[...], proj_ref[...]) + vec_ref[4:5, :]
    resid_ref[...] = resid
    m_ref[...] = (normalize(resid) * vec_ref[5:6, :] + vec_ref[6:7, :]).astype(BF16)


def norm_back(values, grad, gain):
    center = values - jnp.mean(values, -1, keepdims=True)
    scale = lax.rsqrt(jnp.mean(center * center, -1, keepdims=True) + EPSILON)
    unit = center * scale
    grad_unit = grad * gain
    inner = jnp.mean(grad_unit * unit, -1, keepdims=True)
    return unit, scale * (grad_unit - jnp.mean(grad_unit, -1, keepdims=True) - unit * inner)


def add_parts(refs):
    total = refs[0][...].astype(F32)
    for ref in refs[1:]:
        total = total + ref[...].astype(F32)
    return total


def mix_back_kernel(spots_ref, dy_ref, resid_ref, vec_ref, proj_ref, attn_ref, *refs):
    part_refs, (d_resid_ref, d_attn_ref, sum_ref, kept_ref, sent_ref, full_ref) = refs[:5], refs[5:]
    blocks, rows, width = d_attn_ref.shape
    grad = add_parts(part_refs)
    dy = dy_ref[...].astype(F32)
    unit, d_values = norm_back(resid_ref[...], grad, vec_ref[5:6, :])
    d_resid = dy + d_values
    d_resid_ref[...] = d_resid
    d_branch = d_resid.astype(BF16)
    for at in range(blocks):
        d_attn_ref[at] = times_trans(
            d_branch, proj_ref[at * width : (at + 1) * width, :]
        ).astype(BF16)
    sums = [d_branch.astype(F32), grad * unit, grad, dy]
    sums = [jnp.sum(item, 0, keepdims=True) for item in sums]
    sum_ref[...] = jnp.concatenate(sums + [jnp.zeros((4, sum_ref.shape[1]), F32)], 0)
    full_ref[...] = contract_rows(attn_ref[...], d_branch).astype(BF16)
    share = full_ref.shape[0] // 4 // blocks
    for block in range(blocks):
        out = sent_ref if block % 2 else kept_ref
        for at in range(4):
            place = at * blocks + spots_ref[SPOT_CTX + block]
            out[block // 2, at * share : (at + 1) * share, :] = full_ref[rows_at(place, share), :]


def feed_fast_kernel(spots_ref, *refs):
    m_refs, dy_refs, w_refs, bias_ref = refs[:8], refs[8:16], refs[16:18], refs[18]
    kept_ref, sent_ref, y_kept_ref, y_sent_ref, w_kept_ref, w_sent_ref, sum_ref = refs[19:26]
    (
        down_ref,
        up_ref,
        m_buf,
        dy_buf,
        out_buf,
        hidden_ref,
        d_pre_ref,
        in_sems,
        out_sems,
    ) = refs[26:]
    length, model_dim = m_buf.shape
    rows = length // 8
    hidden = up_ref.shape[1]
    part, share = model_dim // 4, hidden // 4
    for block in range(8):
        here = slice(block * rows, (block + 1) * rows)
        pltpu.make_async_copy(m_refs[block], m_buf.at[here, :], in_sems.at[2 * block]).start()
        pltpu.make_async_copy(
            dy_refs[block].at[:rows, :], dy_buf.at[here, :], in_sems.at[2 * block + 1]
        ).start()
    for at in range(4):
        source = spots_ref[SPOT_SWAP + at]
        piece = w_refs[at % 2].at[at // 2]
        up_ref[rows_at(source, part), :] = piece[:part, :]
        for cut in range(model_dim // hidden):
            first = part + cut * share
            down_ref[rows_at(source, share), cut * hidden : (cut + 1) * hidden] = piece[
                first : first + share, :
            ]
    sum_ref[...] = jnp.zeros_like(sum_ref)
    outs = ((kept_ref, y_kept_ref), (sent_ref, y_sent_ref))

    def send(pair, side):
        block = 2 * pair + side
        return pltpu.make_async_copy(out_buf.at[block], outs[side][0].at[pair], out_sems.at[block])

    @pl.loop(0, 4)
    def _(pair):
        for side in range(2):
            block = 2 * pair + side
            here = rows_at(block, rows)
            for at, buf in enumerate((m_buf, dy_buf)):
                pltpu.make_async_copy(
                    buf.at[here, :], buf.at[here, :], in_sems.at[2 * block + at]
                ).wait()
            pre_act = times(m_buf[here, :], up_ref[...]) + bias_ref[...]
            d_hidden = times_trans(dy_buf[here, :], down_ref[...])
            square = pre_act * pre_act
            bent = jnp.tanh(GELU_COEF * (pre_act + 0.044715 * (square * pre_act)))
            half_one = 0.5 + 0.5 * bent
            hidden_low = (pre_act * half_one).astype(BF16)
            hidden_ref[here, :] = hidden_low
            slope = half_one + (0.5 * pre_act) * (1.0 - bent * bent) * (
                GELU_COEF + (3.0 * 0.044715 * GELU_COEF) * square
            )
            d_pre = (d_hidden * slope).astype(BF16)
            d_pre_ref[here, :] = d_pre
            sum_ref[...] += jnp.sum(d_pre.astype(F32), 0, keepdims=True)
            out_buf[block] = times_trans(d_pre, up_ref[...]).astype(BF16)
            send(pair, side).start()
            outs[side][1][pair] = times(hidden_low, down_ref[...]).astype(BF16)

    @pl.loop(0, 2)
    def _(pair):
        for side, out in enumerate((w_kept_ref, w_sent_ref)):
            place = spots_ref[SPOT_SWAP + 2 * pair + side]
            columns = lanes_at(place, part)
            out[pair, :part, :] = contract_rows(m_buf[:, columns], d_pre_ref[...]).astype(BF16)
            d_down = contract_rows(hidden_ref[:, lanes_at(place, share)], dy_buf[...]).astype(BF16)
            for cut in range(model_dim // hidden):
                first = part + cut * share
                out[pair, first : first + share, :] = d_down[:, cut * hidden : (cut + 1) * hidden]

    for pair in range(4):
        for side in range(2):
            send(pair, side).wait()


def pack_last_kernel(
    spots_ref,
    normed_ref,
    d_qkv_ref,
    d_first_ref,
    d_qkv_sum_ref,
    sum_ref,
    d_ubias_ref,
    *refs,
):
    part_refs, out_refs, (vec_ref, units_ref, proj_ref) = refs[:4], refs[4:6], refs[6:]
    own = spots_ref[SPOT_OWN]
    width = d_qkv_ref.shape[1] // 3
    model_dim = normed_ref.shape[1]
    part = model_dim // 4
    blocks = model_dim // width
    share = part // blocks
    proj_ref[...] = add_parts(part_refs)
    vec_ref[...] = jnp.zeros_like(vec_ref)
    vec_ref[0:2, :] = d_first_ref[...]
    vec_ref[2:3, lanes_at(own, width)] = d_qkv_sum_ref[:, :width]
    vec_ref[3:4, lanes_at(own, width)] = d_qkv_sum_ref[:, 2 * width :]
    vec_ref[4:8, :] = sum_ref[0:4, :]
    for at in range(4):
        place = spots_ref[SPOT_SWAP + at]
        out = out_refs[at % 2].at[at // 2]
        columns = lanes_at(place, part)
        out[:part, : 3 * width] = contract_rows(normed_ref[:, columns], d_qkv_ref[...]).astype(BF16)
        for cut in range(blocks):
            out[cut * share : (cut + 1) * share, 3 * width :] = proj_ref[
                rows_at(place, share), cut * width : (cut + 1) * width
            ].astype(BF16)
        units_ref[...] = jnp.zeros_like(units_ref)
        units_ref[:, lanes_at(own, width)] = d_ubias_ref[:, lanes_at(place, width)]
        vec = [
            jnp.concatenate([vec_ref[2 * row : 2 * row + 1, columns], vec_ref[2 * row + 1 : 2 * row + 2, columns]], 1)
            for row in range(4)
        ]
        vec = vec + [units_ref[:, : 2 * part], units_ref[:, 2 * part :]]
        vec = jnp.concatenate(vec + [jnp.zeros((10, 4 * width), F32)], 0)
        out[part:, :] = vec.astype(BF16)


def place_last_kernel(spots_ref, *refs):
    piece_refs, (qkv_ref, proj_ref), vec_refs = refs[:8], refs[8:10], refs[10:]
    part, width = qkv_ref.shape[0], qkv_ref.shape[1] // 24
    share = part // 8
    for at in range(8):
        place = spots_ref[SPOT_CTX + at]
        for cut in range(3):
            qkv_ref[:, lanes_at(cut * 8 + place, width)] = piece_refs[at][
                :part, cut * width : (cut + 1) * width
            ].astype(F32)
        for cut in range(8):
            proj_ref[rows_at(place, share), cut * width : (cut + 1) * width] = piece_refs[at][
                cut * share : (cut + 1) * share, 3 * width :
            ].astype(F32)
    vec = piece_refs[0][part:, :].astype(F32)
    for at in range(1, 8):
        vec = vec + piece_refs[at][part:, :].astype(F32)
    for at in range(8):
        vec_refs[at][...] = vec[at // 2 : at // 2 + 1, (at % 2) * part : (at % 2 + 1) * part]
    vec_refs[8][...] = jnp.concatenate([vec[4:5], vec[5:6]], 1)


def input_grad_kernel(x_ref, d_resid_ref, vec_ref, *refs):
    unit, d_values = norm_back(x_ref[...].astype(F32), add_parts(refs[:-1]), vec_ref[0:1, :])
    refs[-1][...] = d_resid_ref[...] + d_values


def scatter_pairs(kept, sent):
    swapped = ctx_swap(sent, 1)
    return [kept[0], swapped[0]], [kept[step] + swapped[step] for step in (1, 2, 3)]


def scatter_half(pairs):
    by_x, by_y, diag = pairs
    half = by_x.shape[0] // 2
    sent_x = ctx_swap(jnp.concatenate([by_x[:half], diag[:half]]), 2)
    return sent_x, ctx_swap(jnp.concatenate([by_y[half:], diag[half:]]), 4)


def scatter_other(own, pairs, from_x, from_y):
    by_x, by_y, _ = pairs
    half = by_x.shape[0] // 2
    rest = ctx_swap(by_y[:half] + from_x[half:], 4), ctx_swap(by_x[half:] + from_y[half:], 2)
    return own + [jnp.concatenate([from_x[:half], from_y[:half]]), jnp.concatenate(rest)]


def scatter_rest(own, pairs):
    return own + [ctx_swap(pair, 2 * (at + 1)) for at, pair in enumerate(pairs)]


def gather_direct(block):
    return ctx_swap(block, 2), ctx_swap(block, 4), ctx_swap(block, 6)


def gather_pairs(block, near):
    parts = [block] + list(near)
    return [item for part in parts for item in (part, ctx_swap(part, 1))]


def gather_near(block):
    return ctx_swap(block, 2), ctx_swap(block, 4), ctx_swap(block, 1)


def gather_far(block, near, ready=()):
    by_x, by_y, own_pair = near
    half = block.shape[0] // 2
    diag = jnp.concatenate([ctx_swap(by_y[:half], 2), ctx_swap(by_x[half:], 4)])
    pair_x = ctx_swap(by_x, 1)
    pair_y = ctx_swap(by_y, 1)
    return [block, own_pair, by_x, pair_x, by_y, pair_y, diag, ctx_swap(tie(diag, *ready), 1)]


def shards_fast(
    block_in,
    out_grad,
    ln1_gain,
    ln1_shift,
    qkv_weight,
    query_bias,
    value_bias,
    proj_weight,
    proj_bias,
    ln2_gain,
    ln2_shift,
    up_weight,
    up_bias,
    down_weight,
    down_bias,
):
    seq_count, rows, model_dim = block_in.shape
    length = 8 * rows
    width, part = model_dim // 8, model_dim // 4
    units = up_bias.shape[0]
    hidden = units // 2
    heads = width // HEAD_DIM
    own, here = lax.axis_index("ctx"), lax.axis_index("fsdp")
    eight, four = jnp.arange(8, dtype=jnp.int32), jnp.arange(4, dtype=jnp.int32)
    spots = jnp.concatenate(
        [own[None], eight ^ own, lax.rem(here - four + 4, 4), four ^ here]
    ).astype(jnp.int32)
    x = block_in.reshape(rows, model_dim)
    dy = out_grad.reshape(rows, model_dim)
    token = (rows, model_dim)
    half = ((4,) + token, BF16)

    x_near = gather_direct(x)
    vectors = [ln1_gain, ln1_shift, query_bias, value_bias, proj_bias, ln2_gain, ln2_shift]
    vectors = sum(
        jnp.pad(item.astype(F32), (at * part, 16 * part - at * part - item.shape[0]))
        for at, item in enumerate(vectors + [down_bias, up_bias])
    )
    (first,) = call(
        pack_first_kernel,
        "pack_first",
        [((4 * part + 32, width), BF16)],
        [SMEM] + [ANY] * 2 + [VMEM],
        [pltpu.VMEM((part // 8, model_dim), BF16), pltpu.SemaphoreType.DMA((4,))],
        cost=1,
    )(spots, qkv_weight, proj_weight, vectors)
    (second,) = call(
        pack_second_kernel,
        "pack_second",
        [((2 * part, hidden), BF16)],
        [SMEM] + [ANY] * 2,
        [pltpu.SemaphoreType.DMA((6,))],
        cost=1,
    )(spots, up_weight, tie(down_weight, first))
    first = jnp.stack([first, depth_swap(first, 2)])
    first = (first, depth_swap(first, 1))
    x_parts = gather_pairs(x, x_near)
    proj_slices = [first[at % 2][at // 2, 3 * part + 32 :] for at in range(4)]
    proj_slices = jnp.stack(proj_slices).reshape(4, 8, part // 8, width).transpose(0, 2, 1, 3)
    joined = jnp.concatenate([dy, proj_slices.reshape(part // 2, model_dim)])
    joined_near = gather_direct(joined)
    second_far = depth_swap(tie(second, first[1]), 2)

    normed, qkv_full, qkv, attn, attn_trans, log_total, vec, ubias = call(
        functools.partial(attend_fast_kernel, 512),
        "attend",
        [
            ((length, model_dim), BF16),
            ((model_dim, 3 * width), BF16),
            ((length, 3 * width), BF16),
            ((8, rows, width), BF16),
            ((width, length), F32),
            ((heads, length), F32),
            ((16, model_dim), F32),
            ((1, hidden), F32),
        ],
        [SMEM] + [VMEM] * 10,
        [
            pltpu.VMEM((heads, length, HEAD_DIM), BF16),
            pltpu.VMEM((heads, length, HEAD_DIM), BF16),
            pltpu.VMEM((width, length), BF16),
            pltpu.VMEM((8,) + token, BF16),
            pltpu.SemaphoreType.DMA((8,)),
        ],
        [ANY] + [VMEM] * 7,
        limit=58,
        cost=20,
    )(spots, *x_parts, *first)
    attn, second_far = lax.optimization_barrier((attn, second_far))
    second_pair = jnp.stack([second, second_far])
    attn = lax.all_to_all(tie(attn, second_pair), "ctx", 0, 0, tiled=False)
    attn, *joined_near = lax.optimization_barrier((attn,) + joined_near)
    second_pair = (second_pair, depth_swap(second_pair, 1))
    joined = gather_pairs(joined, joined_near)
    resid, m, proj_full, attn_low = call(
        mix_kernel,
        "mix",
        [(token, F32), (token, BF16), ((model_dim, model_dim), BF16), (token, BF16)],
        [SMEM] + [VMEM] * 3 + [ANY] * 8,
        [pltpu.SemaphoreType.DMA((32,))],
    )(spots, x, vec, attn, *joined)
    m_near = gather_near(m)
    *m_near, second_rest = lax.optimization_barrier(m_near + second_pair[1:])
    second_pair = (second_pair[0], second_rest)
    m_parts = gather_far(m, m_near)

    kept, sent, y_kept, y_sent, w_kept, w_sent, d_ubias = call(
        feed_fast_kernel,
        "feed",
        [half] * 4 + [((2, 2 * part, hidden), BF16)] * 2 + [((1, hidden), F32)],
        [SMEM] + [ANY] * 16 + [VMEM] * 3,
        [
            pltpu.VMEM((hidden, model_dim), BF16),
            pltpu.VMEM((model_dim, hidden), BF16),
            pltpu.VMEM((length, model_dim), BF16),
            pltpu.VMEM((length, model_dim), BF16),
            pltpu.VMEM((8,) + token, BF16),
            pltpu.VMEM((length, hidden), BF16),
            pltpu.VMEM((length, hidden), BF16),
            pltpu.SemaphoreType.DMA((16,)),
            pltpu.SemaphoreType.DMA((8,)),
        ],
        [ANY] * 2 + [VMEM] * 5,
        limit=40,
        cost=20,
    )(spots, *m_parts, *joined, *second_pair, ubias)
    w_swapped = depth_swap(w_sent, 1)
    mine, pairs = scatter_pairs(kept, sent)
    d_m_parts = scatter_rest(mine, pairs)
    y_mine, y_pairs = scatter_pairs(y_kept, y_sent)

    proj_half = ((4, part // 2, model_dim), BF16)
    w_pair = (w_kept.astype(F32) + w_swapped.astype(F32)).astype(BF16)
    w_far = depth_swap(w_pair[1], 2)
    d_resid, d_attn, sums, proj_kept, proj_sent = call(
        mix_back_kernel,
        "mix_back",
        [(token, F32), ((8, rows, width), BF16), ((8, model_dim), F32), proj_half, proj_half],
        [SMEM] + [VMEM] * 10,
        [pltpu.VMEM((model_dim, model_dim), BF16)],
        after=[w_pair, y_pairs[0]],
        cost=0,
    )(spots, dy, resid, vec, proj_full, attn_low, *d_m_parts)
    y_parts = scatter_other(y_mine, y_pairs, *scatter_half(y_pairs))
    proj_mine, proj_pairs = scatter_pairs(proj_kept, proj_sent)
    d_attn = lax.all_to_all(d_attn, "ctx", 0, 0, tiled=False)
    d_attn = lax.optimization_barrier((d_attn,) + tuple(y_parts[2:]))[0]
    proj_halves = scatter_half(proj_pairs)

    d_qkv, kept, sent, d_qkv_sum = attend_grad(
        spots[SPOT_CTX : SPOT_CTX + 8],
        qkv,
        d_attn,
        attn_trans,
        log_total,
        qkv_full,
    )
    sent, w_far, *travelled = lax.optimization_barrier((sent, w_far) + proj_halves)
    proj_parts = scatter_other(proj_mine, proj_pairs, *travelled)
    d_feed = (w_pair[0].astype(F32) + w_far.astype(F32)).astype(BF16)
    feed_near = gather_near(d_feed)
    mine, pairs = scatter_pairs(kept, sent)
    d_x_halves = scatter_half(pairs)
    d_first = first_sums(x_parts, kept, sent)
    last = call(
        pack_last_kernel,
        "pack_last",
        [((2, part + 16, 4 * width), BF16)] * 2,
        [SMEM] + [VMEM] * 10,
        [
            pltpu.VMEM((8, model_dim), F32),
            pltpu.VMEM((1, units), F32),
            pltpu.VMEM((part // 2, model_dim), F32),
        ],
        cost=0,
    )(spots, normed, d_qkv, d_first, d_qkv_sum, sums, d_ubias, *proj_parts)
    last_swapped = depth_swap(last[1], 1)
    last_swapped, *travelled = lax.optimization_barrier(
        (last_swapped,) + d_x_halves + feed_near[:2]
    )
    last = (last[0].astype(F32) + last_swapped.astype(F32)).astype(BF16)
    last_far = depth_swap(last[1], 2)
    d_x_parts = scatter_other(mine, pairs, *travelled[:2])
    last_far = lax.optimization_barrier((last_far,) + tuple(d_x_parts[3:]))[0]
    feed_parts = gather_far(d_feed, (travelled[2], travelled[3], feed_near[2]), [last_far])
    final_sum = sum(item.astype(F32) for item in y_parts)
    block_out = (resid + final_sum + vec[7]).astype(BF16)
    d_up, d_down = place_feed(
        spots[SPOT_CTX : SPOT_CTX + 8], feed_parts, part, model_dim, units, 4
    )
    last = (last[0].astype(F32) + last_far.astype(F32)).astype(BF16)
    (d_input,) = call(
        input_grad_kernel, "input_grad", [(token, F32)], [VMEM] * 7, cost=1
    )(x, d_resid, vec, *d_x_parts)
    last_near = lax.optimization_barrier(gather_direct(last) + (d_input, block_out))[:3]
    last = gather_pairs(last, last_near)
    placed = call(
        place_last_kernel,
        "place_last",
        [((part, 3 * model_dim), F32), ((part, model_dim), F32)]
        + [((1, part), F32)] * 8
        + [((1, units), F32)],
        [SMEM] + [VMEM] * 8,
    )(spots, *last)
    d_weight_qkv, d_proj = placed[:2]
    d_vec = [item.reshape(-1) for item in placed[2:]]
    return (
        block_out.reshape(block_in.shape),
        d_input.reshape(block_in.shape),
        d_vec[0],
        d_vec[1],
        d_weight_qkv,
        d_vec[2],
        d_vec[3],
        d_proj,
        d_vec[4],
        d_vec[5],
        d_vec[6],
        d_up,
        d_vec[8],
        d_down,
        d_vec[7],
    )


def solution(mesh):
    rows, matrix, vector = P("fsdp", "ctx", None), P("fsdp", None), P("fsdp")
    in_specs = (
        rows,
        rows,
        vector,
        vector,
        matrix,
        vector,
        vector,
        matrix,
        vector,
        vector,
        vector,
        matrix,
        vector,
        matrix,
        vector,
    )
    out_specs = (rows, rows) + in_specs[2:]
    fast = mesh.shape["ctx"] == 8 and mesh.shape["fsdp"] == 4
    shards = shards_fast if fast else shards_any
    return jax.shard_map(shards, mesh=mesh, in_specs=in_specs, out_specs=out_specs, check_vma=False)
```

```python
import functools
import math

import jax
import jax.numpy as jnp
from jax import lax
from jax.experimental import pallas as pl
from jax.experimental.pallas import tpu as pltpu
from jax.sharding import PartitionSpec as P

HEADS = 16
HEAD_DIM = 64

EPSILON = 1e-05
GELU_COEF = 0.7978845608028654
MASKED = -1e30
SCORE_SCALE = HEAD_DIM ** (-0.5)
EXP2_SCALE = SCORE_SCALE / math.log(2.0)
F32 = jnp.float32
BF16 = jnp.bfloat16
SMEM = pl.BlockSpec(memory_space=pltpu.SMEM)
VMEM = pl.BlockSpec(memory_space=pltpu.VMEM)


def layer_norm(values, gain_vec, shift_vec):
    center = values - jnp.mean(values, -1, keepdims=True)
    spread = jnp.mean(center * center, -1, keepdims=True)
    return center * lax.rsqrt(spread + EPSILON) * gain_vec + shift_vec


def contract_rows(left, right):
    return lax.dot_general(left, right, (((0,), (0,)), ((), ())), preferred_element_type=F32)


def times_trans(left, right):
    return lax.dot_general(left, right, (((1,), (1,)), ((), ())), preferred_element_type=F32)


def times(left, right):
    return jnp.dot(left, right, preferred_element_type=F32)


def ctx_swap(value, bits):
    size = lax.axis_size("ctx")
    return lax.ppermute(value, "ctx", [(at, at ^ bits) for at in range(size)])


def ctx_places():
    size = lax.axis_size("ctx")
    order = jnp.arange(size, dtype=jnp.int32)
    return jnp.bitwise_xor(order, lax.axis_index("ctx")) if size == 8 else order


def ctx_gather(block):
    size = lax.axis_size("ctx")
    if size != 8:
        whole = lax.all_gather(block, "ctx", axis=0)
        return [whole[at] for at in range(size)]
    half = block.shape[0] // 2
    by_x = ctx_swap(block, 2)
    by_y = ctx_swap(block, 4)
    own_pair = ctx_swap(block, 1)
    diag = jnp.concatenate([ctx_swap(by_y[:half], 2), ctx_swap(by_x[half:], 4)])
    pair_x = ctx_swap(by_x, 1)
    pair_y = ctx_swap(by_y, 1)
    pair_diag = ctx_swap(diag, 1)
    return [block, own_pair, by_x, pair_x, by_y, pair_y, diag, pair_diag]


def ctx_scatter(kept, sent):
    if lax.axis_size("ctx") != 8:
        blocks = jnp.stack([kept, sent], 1).reshape((-1,) + kept.shape[1:])
        return lax.psum_scatter(blocks, "ctx", scatter_dimension=0, tiled=False).astype(F32)
    swapped = ctx_swap(sent, 1)
    total = kept[0].astype(F32) + swapped[0].astype(F32)
    for step in (1, 2, 3):
        pair = kept[step] + swapped[step]
        total = total + ctx_swap(pair, 2 * step).astype(F32)
    return total


def depth_shift(value, step):
    size = lax.axis_size("fsdp")
    return lax.ppermute(value, "fsdp", [(at, (at + step) % size) for at in range(size)])


def depth_swap(value, bits):
    size = lax.axis_size("fsdp")
    return lax.ppermute(value, "fsdp", [(at, at ^ bits) for at in range(size)])


def depth_places():
    size = lax.axis_size("fsdp")
    order = jnp.arange(size, dtype=jnp.int32)
    return lax.rem(lax.axis_index("fsdp") - order + size, size) if size == 4 else order


def depth_gather(block):
    size = lax.axis_size("fsdp")
    if size != 4:
        whole = lax.all_gather(block, "fsdp", axis=0)
        return [whole[at] for at in range(size)]
    return [block] + [depth_shift(block, step) for step in range(1, size)]


def depth_scatter(blocks):
    size = lax.axis_size("fsdp")
    if size != 4:
        return lax.psum_scatter(blocks, "fsdp", scatter_dimension=0, tiled=False).astype(F32)
    here = lax.axis_index("fsdp")
    total = lax.dynamic_index_in_dim(blocks, here, 0, False).astype(F32)
    for step in range(1, size):
        part = lax.dynamic_index_in_dim(blocks, lax.rem(here + step, size), 0, False)
        total = total + depth_shift(part, step).astype(F32)
    return total


def cost_of(microseconds):
    return pl.CostEstimate(flops=microseconds * 10**9, bytes_accessed=0, transcendentals=0)


def causal(rows, columns):
    keys = lax.broadcasted_iota(jnp.int32, (rows, columns), 0)
    queries = lax.broadcasted_iota(jnp.int32, (rows, columns), 1)
    return keys <= queries


def rows_at(place, rows):
    return pl.ds(pl.multiple_of(place * rows, rows), rows)


def normalize(values):
    center = values - jnp.mean(values, -1, keepdims=True)
    spread = jnp.mean(center * center, -1, keepdims=True)
    return center * lax.rsqrt(spread + EPSILON)


def attend_kernel(blocks, depth, tile, places_ref, depths_ref, *refs):
    x_refs, w_refs = refs[:blocks], refs[blocks : blocks + depth]
    (
        vec_ref,
        bias_ref,
        normed_ref,
        w_ref,
        qkv_ref,
        out_ref,
        out_t_ref,
        log_ref,
        q_ref,
        k_ref,
        v_t_ref,
    ) = refs[blocks + depth :]
    length, width = out_ref.shape
    heads = width // HEAD_DIM
    rows = length // blocks
    part = w_ref.shape[0] // depth
    for at in range(depth):
        place = rows_at(depths_ref[at], part)
        for column in range(3):
            w_ref[place, column * width : (column + 1) * width] = w_refs[at][
                column * part : (column + 1) * part, :
            ]
    for block in range(blocks):
        place = rows_at(places_ref[block], rows)
        normed = normalize(x_refs[block][...].astype(F32)) * vec_ref[0:1, :] + vec_ref[1:2, :]
        normed = normed.astype(BF16)
        normed_ref[place, :] = normed
        qkv = (times(normed, w_ref[...]) + bias_ref[...]).astype(BF16)
        qkv_ref[place, :] = qkv
        for head in range(heads):
            low, high = head * HEAD_DIM, (head + 1) * HEAD_DIM
            q_ref[head, place, :] = qkv[:, low:high]
            k_ref[head, place, :] = qkv[:, width + low : width + high]
        v_t_ref[:, place] = qkv[:, 2 * width :].T
    for q_tile in range(length // tile):
        columns = slice(q_tile * tile, (q_tile + 1) * tile)
        queries = [q_ref[head, columns, :] for head in range(heads)]

        def visit(k_tile, state, masked):
            start = k_tile * tile
            result = []
            for head in range(heads):
                run_max, run_sum, run_acc = state[head]
                scores = times_trans(k_ref[head, pl.ds(start, tile), :], queries[head])
                if masked:
                    scores = jnp.where(causal(tile, tile), scores, MASKED)
                new_max = jnp.maximum(run_max, jnp.max(scores, 0, keepdims=True))
                weights = jnp.exp2(scores * EXP2_SCALE - new_max * EXP2_SCALE)
                factor = jnp.exp2((run_max - new_max) * EXP2_SCALE)
                new_sum = run_sum * factor + jnp.sum(weights, 0, keepdims=True)
                low, high = head * HEAD_DIM, (head + 1) * HEAD_DIM
                values = v_t_ref[low:high, pl.ds(start, tile)]
                new_acc = run_acc * factor + times(values, weights.astype(BF16))
                result.append((new_max, new_sum, new_acc))
            return result

        state = [
            (
                jnp.full((1, tile), MASKED, F32),
                jnp.zeros((1, tile), F32),
                jnp.zeros((HEAD_DIM, tile), F32),
            )
        ] * heads
        for k_tile in range(q_tile):
            state = visit(k_tile, state, False)
        state = visit(q_tile, state, True)
        result = []
        for head in range(heads):
            run_max, run_sum, run_acc = state[head]
            result.append(run_acc / run_sum)
            log_ref[head : head + 1, columns] = run_max * EXP2_SCALE + jnp.log2(run_sum)
        result = jnp.concatenate(result, 0) if heads > 1 else result[0]
        out_t_ref[:, columns] = result
        out_ref[columns, :] = result.T.astype(BF16)


def attend_grad_kernel(
    blocks, tile, places_ref, qkv_ref, out_t_ref, log_ref, w_ref, d_out_ref, *refs
):
    d_qkv_ref, kept_ref, sent_ref, sum_ref = refs[:4]
    q_ref, k_ref, v_ref, k_t_ref, do_ref, delta_ref, dq_t_ref, dk_ref, dv_ref = refs[4:]
    width, length = out_t_ref.shape
    heads = width // HEAD_DIM
    rows = length // blocks
    for block in range(blocks):
        here = slice(block * rows, (block + 1) * rows)
        part = qkv_ref[here, :]
        for head in range(heads):
            low, high = head * HEAD_DIM, (head + 1) * HEAD_DIM
            q_ref[head, here, :] = part[:, low:high]
            k_ref[head, here, :] = part[:, width + low : width + high]
            v_ref[head, here, :] = part[:, 2 * width + low : 2 * width + high]
        k_t_ref[:, here] = part[:, width : 2 * width].T
        d_out = d_out_ref[block]
        product = d_out.astype(F32).T * out_t_ref[:, here]
        for head in range(heads):
            low, high = head * HEAD_DIM, (head + 1) * HEAD_DIM
            do_ref[head, here, :] = d_out[:, low:high]
            delta_ref[head : head + 1, here] = jnp.sum(product[low:high], 0, keepdims=True)
    dq_t_ref[...] = jnp.zeros_like(dq_t_ref)
    tiles = length // tile
    for k_tile in range(tiles):
        all_keys = slice(k_tile * tile, (k_tile + 1) * tile)

        def visit(key_rows, query_rows, state, masked):
            result = []
            for head in range(heads):
                d_key, d_value = state[head]
                low, high = head * HEAD_DIM, (head + 1) * HEAD_DIM
                queries = q_ref[head, query_rows, :]
                d_out = do_ref[head, query_rows, :]
                scores = times_trans(k_ref[head, key_rows, :], queries)
                log_row = log_ref[head : head + 1, query_rows]
                probs = jnp.exp2(scores * EXP2_SCALE - log_row)
                if masked:
                    probs = jnp.where(causal(*probs.shape), probs, 0.0)
                d_probs = times_trans(v_ref[head, key_rows, :], d_out)
                d_scores = (probs * (d_probs - delta_ref[head : head + 1, query_rows])).astype(BF16)
                d_value = d_value + times(probs.astype(BF16), d_out)
                d_key = d_key + times(d_scores, queries)
                dq_t_ref[low:high, query_rows] += times(k_t_ref[low:high, key_rows], d_scores)
                result.append((d_key, d_value))
            return result

        half = tile // 2
        middle = k_tile * tile + half
        zero = [(jnp.zeros((half, HEAD_DIM), F32), jnp.zeros((half, HEAD_DIM), F32))] * heads
        first = visit(slice(k_tile * tile, middle), all_keys, zero, True)
        second = slice(middle, (k_tile + 1) * tile)
        second = visit(second, second, zero, True)
        state = [
            tuple(jnp.concatenate(pair, 0) for pair in zip(one, other))
            for one, other in zip(first, second)
        ]
        for q_tile in range(k_tile + 1, tiles):
            state = visit(all_keys, slice(q_tile * tile, (q_tile + 1) * tile), state, False)
        for head in range(heads):
            dk_ref[head, all_keys, :] = state[head][0]
            dv_ref[head, all_keys, :] = state[head][1]
    total = jnp.zeros((1, 3 * width), F32)
    for block in range(blocks):
        place = rows_at(places_ref[block], rows)
        d_key = [dk_ref[head, place, :] * SCORE_SCALE for head in range(heads)]
        d_value = [dv_ref[head, place, :] for head in range(heads)]
        parts = [dq_t_ref[:, place].T * SCORE_SCALE] + d_key + d_value
        d_qkv = jnp.concatenate(parts, 1).astype(BF16)
        d_qkv_ref[place, :] = d_qkv
        total = total + jnp.sum(d_qkv.astype(F32), 0, keepdims=True)
        out = sent_ref if block % 2 else kept_ref
        out[block // 2] = times_trans(d_qkv, w_ref[...]).astype(BF16)
    sum_ref[...] = total


def attend(places, depths, x_parts, w_parts, vectors, bias):
    blocks, depth = len(x_parts), len(w_parts)
    rows, model_dim = x_parts[0].shape
    width = bias.shape[1] // 3
    length = rows * blocks
    heads = width // HEAD_DIM
    tile = min(512, length)
    return pl.pallas_call(
        functools.partial(attend_kernel, blocks, depth, tile),
        out_shape=(
            jax.ShapeDtypeStruct((length, model_dim), BF16),
            jax.ShapeDtypeStruct((model_dim, 3 * width), BF16),
            jax.ShapeDtypeStruct((length, 3 * width), BF16),
            jax.ShapeDtypeStruct((length, width), BF16),
            jax.ShapeDtypeStruct((width, length), F32),
            jax.ShapeDtypeStruct((heads, length), F32),
        ),
        in_specs=[SMEM] * 2 + [VMEM] * (blocks + depth + 2),
        out_specs=(VMEM,) * 6,
        scratch_shapes=[
            pltpu.VMEM((heads, length, HEAD_DIM), BF16),
            pltpu.VMEM((heads, length, HEAD_DIM), BF16),
            pltpu.VMEM((width, length), BF16),
        ],
        compiler_params=pltpu.CompilerParams(vmem_limit_bytes=32 << 20),
        cost_estimate=cost_of(10),
        name="attend",
    )(places, depths, *x_parts, *w_parts, vectors, bias)


def attend_grad(places, qkv, d_out, out_t, log_total, w_full):
    length, width = qkv.shape[0], qkv.shape[1] // 3
    model_dim = w_full.shape[0]
    blocks = places.shape[0]
    heads = width // HEAD_DIM
    tile = min(512, length)
    per_head = pltpu.VMEM((heads, length, HEAD_DIM), BF16)
    half = jax.ShapeDtypeStruct((blocks // 2, length // blocks, model_dim), BF16)
    return pl.pallas_call(
        functools.partial(attend_grad_kernel, blocks, tile),
        out_shape=(
            jax.ShapeDtypeStruct((length, 3 * width), BF16),
            half,
            half,
            jax.ShapeDtypeStruct((1, 3 * width), F32),
        ),
        in_specs=[SMEM] + [VMEM] * 5,
        out_specs=(VMEM,) * 4,
        scratch_shapes=[
            per_head,
            per_head,
            per_head,
            pltpu.VMEM((width, length), BF16),
            per_head,
            pltpu.VMEM((heads, length), F32),
            pltpu.VMEM((width, length), F32),
            pltpu.VMEM((heads, length, HEAD_DIM), F32),
            pltpu.VMEM((heads, length, HEAD_DIM), F32),
        ],
        compiler_params=pltpu.CompilerParams(vmem_limit_bytes=32 << 20),
        cost_estimate=cost_of(20),
        name="attend_grad",
    )(places, qkv, out_t, log_total, w_full, d_out)


def feed_kernel(blocks, depth, depths_ref, *refs):
    m_refs, dy_refs = refs[:blocks], refs[blocks : 2 * blocks]
    w_refs = refs[2 * blocks : 2 * blocks + depth]
    (
        bias_ref,
        kept_ref,
        sent_ref,
        m_ref,
        dy_ref,
        hidden_ref,
        d_pre_ref,
        sum_ref,
        down_ref,
        up_ref,
    ) = refs[2 * blocks + depth :]
    rows = m_refs[0].shape[0]
    model_dim, hidden = up_ref.shape
    part, share = model_dim // depth, hidden // depth
    for at in range(depth):
        up_ref[rows_at(depths_ref[at], part), :] = w_refs[at][:part, :]
        place = rows_at(depths_ref[at], share)
        for cut in range(model_dim // hidden):
            first = part + cut * share
            down_ref[place, cut * hidden : (cut + 1) * hidden] = w_refs[at][
                first : first + share, :
            ]
    total = jnp.zeros((1, hidden), F32)
    for block in range(blocks):
        here = slice(block * rows, (block + 1) * rows)
        m_ref[here, :] = m_refs[block][...]
        dy_ref[here, :] = dy_refs[block][...]
        pre_act = times(m_refs[block][...], up_ref[...]) + bias_ref[...]
        d_hidden = times_trans(dy_refs[block][...], down_ref[...])
        square = pre_act * pre_act
        bent = jnp.tanh(GELU_COEF * (pre_act + 0.044715 * (square * pre_act)))
        half_one = 0.5 + 0.5 * bent
        hidden_ref[here, :] = (pre_act * half_one).astype(BF16)
        slope = half_one + (0.5 * pre_act) * (1.0 - bent * bent) * (
            GELU_COEF + (3.0 * 0.044715 * GELU_COEF) * square
        )
        d_pre = (d_hidden * slope).astype(BF16)
        d_pre_ref[here, :] = d_pre
        total = total + jnp.sum(d_pre.astype(F32), 0, keepdims=True)
        out = sent_ref if block % 2 else kept_ref
        out[block // 2] = times_trans(d_pre, up_ref[...]).astype(BF16)
    sum_ref[...] = total


def feed(depths, m_parts, dy_parts, w_parts, bias):
    blocks, depth = len(m_parts), len(w_parts)
    rows, model_dim = m_parts[0].shape
    hidden = bias.shape[1]
    length = rows * blocks
    half = jax.ShapeDtypeStruct((blocks // 2, rows, model_dim), BF16)
    whole = jax.ShapeDtypeStruct((length, model_dim), BF16)
    units = jax.ShapeDtypeStruct((length, hidden), BF16)
    return pl.pallas_call(
        functools.partial(feed_kernel, blocks, depth),
        out_shape=(
            half,
            half,
            whole,
            whole,
            units,
            units,
            jax.ShapeDtypeStruct((1, hidden), F32),
            jax.ShapeDtypeStruct((hidden, model_dim), BF16),
        ),
        in_specs=[SMEM] + [VMEM] * (2 * blocks + depth + 1),
        out_specs=(VMEM,) * 8,
        scratch_shapes=[pltpu.VMEM((model_dim, hidden), BF16)],
        compiler_params=pltpu.CompilerParams(vmem_limit_bytes=32 << 20),
        cost_estimate=cost_of(10),
        name="feed",
    )(depths, *m_parts, *dy_parts, *w_parts, bias)


def first_sums_kernel(blocks, *refs):
    x_refs = refs[:blocks]
    kept_ref, sent_ref, out_ref = refs[blocks:]
    gain = jnp.zeros((1, out_ref.shape[1]), F32)
    shift = gain
    for block in range(blocks):
        grad = (sent_ref if block % 2 else kept_ref)[block // 2].astype(F32)
        values = normalize(x_refs[block][...].astype(F32))
        gain = gain + jnp.sum(grad * values, 0, keepdims=True)
        shift = shift + jnp.sum(grad, 0, keepdims=True)
    out_ref[...] = jnp.concatenate([gain, shift], 0)


def first_sums(x_parts, kept, sent):
    blocks = len(x_parts)
    rows, model_dim = x_parts[0].shape
    return pl.pallas_call(
        functools.partial(first_sums_kernel, blocks),
        out_shape=jax.ShapeDtypeStruct((2, model_dim), F32),
        in_specs=[VMEM] * (blocks + 2),
        out_specs=VMEM,
        compiler_params=pltpu.CompilerParams(vmem_limit_bytes=32 << 20),
        cost_estimate=cost_of(0),
        name="first_sums",
    )(*x_parts, kept, sent)


def place_feed_kernel(blocks, depth, places_ref, *refs):
    piece_refs, (up_ref, down_ref) = refs[:blocks], refs[blocks:]
    part, share = up_ref.shape[0], up_ref.shape[1] // depth // blocks
    hidden = share * depth
    for at in range(blocks):
        place = places_ref[at]
        for cut in range(depth):
            start = pl.multiple_of(cut * share * blocks + place * share, share)
            up_ref[:, pl.ds(start, share)] = piece_refs[at][
                :part, cut * share : (cut + 1) * share
            ].astype(F32)
        for cut in range(down_ref.shape[1] // hidden):
            first = part + cut * share
            down_ref[rows_at(place, share), cut * hidden : (cut + 1) * hidden] = piece_refs[at][
                first : first + share, :
            ].astype(F32)


def place_feed(places, pieces, part, model_dim, units, depth):
    blocks = len(pieces)
    share = units // blocks
    if share % 128 == 0:
        return pl.pallas_call(
            functools.partial(place_feed_kernel, blocks, depth),
            out_shape=(
                jax.ShapeDtypeStruct((part, units * depth), F32),
                jax.ShapeDtypeStruct((units, model_dim), F32),
            ),
            in_specs=[SMEM] + [VMEM] * blocks,
            out_specs=(VMEM,) * 2,
            compiler_params=pltpu.CompilerParams(vmem_limit_bytes=32 << 20),
            name="place_feed",
        )(places, *pieces)
    pieces = jnp.stack(pieces).astype(F32)
    up = pieces[:, :part].reshape(blocks, part, depth, share).transpose(1, 2, 0, 3)
    down = pieces[:, part:].reshape(blocks, -1, share, share * depth).transpose(0, 2, 1, 3)
    return up.reshape(part, -1), down.reshape(units, model_dim)


def place_heads_kernel(blocks, places_ref, *refs):
    piece_refs, (qkv_ref, proj_ref, vec_ref) = refs[:blocks], refs[blocks:]
    part, width = qkv_ref.shape[0], qkv_ref.shape[1] // 3 // blocks
    share = part // blocks
    for at in range(blocks):
        place = places_ref[at]
        for cut in range(3):
            start = pl.multiple_of(cut * width * blocks + place * width, width)
            qkv_ref[:, pl.ds(start, width)] = piece_refs[at][
                :part, cut * width : (cut + 1) * width
            ].astype(F32)
        for cut in range(blocks):
            proj_ref[rows_at(place, share), cut * width : (cut + 1) * width] = piece_refs[at][
                cut * share : (cut + 1) * share, 3 * width :
            ].astype(F32)
    vec = piece_refs[0][part:, :].astype(F32)
    for at in range(1, blocks):
        vec = vec + piece_refs[at][part:, :].astype(F32)
    vec_ref[...] = vec


def place_heads(places, pieces, part, model_dim):
    blocks = len(pieces)
    width, extra = model_dim // blocks, pieces[0].shape[0] - part
    if width % 128 == 0:
        return pl.pallas_call(
            functools.partial(place_heads_kernel, blocks),
            out_shape=(
                jax.ShapeDtypeStruct((part, 3 * model_dim), F32),
                jax.ShapeDtypeStruct((part, model_dim), F32),
                jax.ShapeDtypeStruct((extra, 4 * width), F32),
            ),
            in_specs=[SMEM] + [VMEM] * blocks,
            out_specs=(VMEM,) * 3,
            compiler_params=pltpu.CompilerParams(vmem_limit_bytes=32 << 20),
            name="place_heads",
        )(places, *pieces)
    pieces = jnp.stack(pieces).astype(F32)
    qkv = pieces[:, :part, : 3 * width].reshape(blocks, part, 3, width).transpose(1, 2, 0, 3)
    proj = pieces[:, :part, 3 * width :].reshape(blocks, blocks, part // blocks, width)
    proj = proj.transpose(0, 2, 1, 3).reshape(part, model_dim)
    return qkv.reshape(part, -1), proj, jnp.sum(pieces[:, part:], 0)


def shards_any(
    block_in,
    out_grad,
    ln1_gain,
    ln1_shift,
    qkv_weight,
    query_bias,
    value_bias,
    proj_weight,
    proj_bias,
    ln2_gain,
    ln2_shift,
    up_weight,
    up_bias,
    down_weight,
    down_bias,
):
    seq_count, blk_len, model_dim = block_in.shape
    ctx_size, depth = lax.axis_size("ctx"), lax.axis_size("fsdp")
    ctx_index, depth_index = lax.axis_index("ctx"), lax.axis_index("fsdp")
    places, depths = ctx_places(), depth_places()
    seq_len = ctx_size * blk_len
    width = model_dim // ctx_size
    part = model_dim // depth
    units = up_bias.shape[0]
    share = units // ctx_size
    hidden = share * depth
    cuts = model_dim // hidden

    own_in = block_in.reshape(blk_len, model_dim)
    own_dy = out_grad.reshape(blk_len, model_dim)

    def ctx_columns(value, columns, axis):
        return lax.dynamic_slice_in_dim(value, ctx_index * columns, columns, axis)

    x_parts = ctx_gather(own_in)
    vectors = jnp.concatenate(
        [
            ln1_gain,
            ln1_shift,
            query_bias,
            value_bias,
            proj_bias,
            ln2_gain,
            ln2_shift,
            down_bias,
            up_bias,
        ]
    )
    slices = [
        lax.dynamic_slice_in_dim(qkv_weight, at * model_dim + ctx_index * width, width, 1)
        for at in range(3)
    ]
    first = depth_gather(jnp.concatenate(slices + [vectors.reshape(-1, width)]))
    vec = jnp.stack([piece[3 * part :] for piece in first]).reshape(depth, -1)
    vec = jnp.take(vec, depths, axis=0).astype(F32)
    ubias = ctx_columns(vec[:, 8 * part :], share, 1).reshape(1, hidden)
    vec = vec[:, : 8 * part].reshape(depth, 8, part).transpose(1, 0, 2).reshape(8, model_dim)
    gain_two, shift_two = vec[5], vec[6]
    qkv_bias = jnp.concatenate(
        [ctx_columns(vec[2], width, 0), jnp.zeros((width,), F32), ctx_columns(vec[3], width, 0)]
    ).reshape(1, 3 * width)

    normed, qkv_full, qkv, attn_heads, attn_trans, log_total = attend(
        places, depths, x_parts, first, vec, qkv_bias
    )
    attn_low = lax.all_to_all(
        attn_heads.reshape(ctx_size, blk_len, width), "ctx", 0, 0, tiled=False
    )
    attn_low = attn_low.transpose(1, 0, 2).reshape(blk_len, model_dim)

    up_slice = lax.dynamic_index_in_dim(
        up_weight.reshape(part, depth, ctx_size, share), ctx_index, 2, False
    ).reshape(part, hidden)
    down_slice = ctx_columns(down_weight, share, 0)
    down_cuts = [down_slice[:, at * hidden : (at + 1) * hidden] for at in range(cuts)]
    second = depth_gather(jnp.concatenate([up_slice] + down_cuts))
    proj_rows = part // ctx_size
    proj_full = lax.all_gather(
        ctx_columns(proj_weight, proj_rows, 0), ("fsdp", "ctx"), axis=0, tiled=True
    )
    dy_parts = ctx_gather(own_dy)

    own_f = own_in.astype(F32)
    resid_one = own_f + times(attn_low, proj_full) + vec[4]
    normed_two = layer_norm(resid_one, gain_two, shift_two).astype(BF16)

    m_parts = ctx_gather(normed_two)
    kept, sent, all_two, all_dy, hidden_low, d_pre, d_ubias, down_full = feed(
        depths, m_parts, dy_parts, second, ubias
    )
    d_normed_two = ctx_scatter(kept, sent)
    final_part = times(hidden_low, down_full).astype(BF16)
    final_part = final_part.reshape(ctx_size // 2, 2, blk_len, model_dim)
    final_sum = ctx_scatter(final_part[:, 0], final_part[:, 1])
    block_out = (resid_one + final_sum + vec[7]).astype(BF16).reshape(block_in.shape)
    d_up = contract_rows(all_two, d_pre).astype(BF16).reshape(depth, part, hidden)
    d_down = contract_rows(hidden_low, all_dy).astype(BF16).reshape(depth, share, cuts, hidden)
    d_down = d_down.transpose(0, 2, 1, 3).reshape(depth, cuts * share, hidden)
    d_feed = depth_scatter(jnp.concatenate([d_up, d_down], 1)).astype(BF16)
    d_up, d_down = place_feed(places, ctx_gather(d_feed), part, model_dim, units, depth)

    norm_two_out, norm_two_pull = jax.vjp(layer_norm, resid_one, gain_two, shift_two)
    d_resid_part, d_gain_two, d_shift_two = norm_two_pull(d_normed_two)
    grad_f = own_dy.astype(F32)
    d_resid = grad_f + d_resid_part
    d_branch = d_resid.astype(BF16)
    d_attn = times_trans(d_branch, proj_full).astype(BF16)
    d_attn = d_attn.reshape(blk_len, ctx_size, width).transpose(1, 0, 2)
    d_attn = lax.all_to_all(d_attn, "ctx", 0, 0, tiled=False)
    d_proj = contract_rows(attn_low, d_branch).astype(BF16)
    d_proj = d_proj.reshape(depth, ctx_size, proj_rows, model_dim)
    d_proj = jnp.take(d_proj, places, axis=1).transpose(1, 0, 2, 3)
    d_proj = d_proj.reshape(ctx_size // 2, 2, part // ctx_size * depth, model_dim)
    d_proj = ctx_scatter(d_proj[:, 0], d_proj[:, 1]).astype(BF16)
    d_proj = d_proj.reshape(depth, proj_rows, ctx_size, width).transpose(0, 2, 1, 3)
    d_proj = d_proj.reshape(depth, part, width)

    d_qkv, kept, sent, d_qkv_sum = attend_grad(
        places, qkv, d_attn, attn_trans, log_total, qkv_full
    )
    d_normed_own = ctx_scatter(kept, sent)
    d_weight_qkv = contract_rows(normed, d_qkv).astype(BF16).reshape(depth, part, 3 * width)
    d_first = first_sums(x_parts, kept, sent)
    norm_one, norm_one_pull = jax.vjp(lambda value: layer_norm(value, vec[0], vec[1]), own_f)
    d_input = (d_resid + norm_one_pull(d_normed_own)[0]).reshape(block_in.shape)

    def widen(value, total):
        start = jnp.zeros(value.shape[:-1] + (total,), F32)
        return lax.dynamic_update_slice_in_dim(
            start, value, ctx_index * value.shape[-1], value.ndim - 1
        )

    small = [
        d_first[0],
        d_first[1],
        widen(d_qkv_sum[0, :width], model_dim),
        widen(d_qkv_sum[0, 2 * width :], model_dim),
        jnp.sum(d_branch.astype(F32), 0),
        d_gain_two,
        d_shift_two,
        jnp.sum(grad_f, 0),
    ]
    small = jnp.stack(small).reshape(8, depth, part).transpose(1, 0, 2).reshape(depth, 8 * part)
    small = jnp.concatenate([small, widen(d_ubias.reshape(depth, share), units)], 1)
    count = small.shape[1]
    small = small.astype(BF16).reshape(depth, -1, 4 * width)
    small = jnp.pad(small, ((0, 0), (0, -small.shape[1] % 16), (0, 0)))
    last = jnp.concatenate([jnp.concatenate([d_weight_qkv, d_proj], 2), small], 1)
    last = ctx_gather(depth_scatter(last).astype(BF16))
    d_weight_qkv, d_proj, small = place_heads(places, last, part, model_dim)
    small = small.reshape(-1)[:count]
    d_vec = small[: 8 * part].reshape(8, part)
    return (
        block_out,
        d_input,
        d_vec[0],
        d_vec[1],
        d_weight_qkv,
        d_vec[2],
        d_vec[3],
        d_proj,
        d_vec[4],
        d_vec[5],
        d_vec[6],
        d_up,
        small[8 * part :],
        d_down,
        d_vec[7],
    )


ANY = pl.BlockSpec(memory_space=pl.ANY)
HBM = pl.BlockSpec(memory_space=pltpu.HBM)


SPOT_OWN, SPOT_CTX, SPOT_FROM, SPOT_SWAP = 0, 1, 9, 13


def tie(value, *others):
    return lax.optimization_barrier((value,) + others)[0]


def call(kernel, name, outs, in_specs, scratch=(), out_specs=None, limit=16, after=(), cost=3):
    count = len(in_specs)

    def body(*refs):
        return kernel(*refs[:count], *refs[count + len(after) :])

    run = pl.pallas_call(
        body if after else kernel,
        out_shape=tuple(jax.ShapeDtypeStruct(shape, kind) for shape, kind in outs),
        in_specs=list(in_specs) + [ANY] * len(after),
        out_specs=tuple(out_specs or [VMEM] * len(outs)),
        scratch_shapes=list(scratch),
        compiler_params=pltpu.CompilerParams(vmem_limit_bytes=limit << 20),
        cost_estimate=cost_of(cost),
        name=name,
    )
    return lambda *args: run(*args, *after)


def lanes_at(place, size):
    return pl.ds(pl.multiple_of(place * size, size), size)


def run_copies(copies):
    for copy in copies:
        copy.start()
    for copy in copies:
        copy.wait()


def pack_first_kernel(spots_ref, qkv_ref, proj_ref, vec_ref, out_ref, proj_buf, sems):
    own = spots_ref[SPOT_OWN]
    part, model_dim = proj_ref.shape
    width = out_ref.shape[1]
    blocks = model_dim // width
    share = part // blocks
    copies = [
        pltpu.make_async_copy(
            qkv_ref.at[:, lanes_at(at * blocks + own, width)],
            out_ref.at[at * part : (at + 1) * part, :],
            sems.at[at],
        )
        for at in range(3)
    ]
    copies.append(pltpu.make_async_copy(proj_ref.at[rows_at(own, share), :], proj_buf, sems.at[3]))
    run_copies(copies)
    vec = vec_ref[...].reshape(1, 16 * part)
    vec = [vec[:, at * part : (at + 1) * part] for at in range(16)]
    vec = jnp.concatenate(vec, 0).astype(BF16)
    first = 3 * part
    out_ref[first : first + 16, :] = vec[:, :width]
    out_ref[first + 16 : first + 32, :] = vec[:, width:]
    first = first + 32
    for at in range(blocks):
        out_ref[first + at * share : first + (at + 1) * share, :] = proj_buf[
            :, at * width : (at + 1) * width
        ]


def pack_second_kernel(spots_ref, up_ref, down_ref, out_ref, sems):
    own = spots_ref[SPOT_OWN]
    part, hidden = up_ref.shape[0], out_ref.shape[1]
    share = hidden // 4
    blocks = up_ref.shape[1] // hidden
    copies = []
    for at in range(4):
        copies.append(
            pltpu.make_async_copy(
                up_ref.at[:, lanes_at(at * blocks + own, share)],
                out_ref.at[:part, at * share : (at + 1) * share],
                sems.at[at],
            )
        )
    for at in range(down_ref.shape[1] // hidden):
        first = part + at * share
        copies.append(
            pltpu.make_async_copy(
                down_ref.at[rows_at(own, share), at * hidden : (at + 1) * hidden],
                out_ref.at[first : first + share, :],
                sems.at[4 + at],
            )
        )
    run_copies(copies)


def attend_fast_kernel(tile, spots_ref, *refs):
    x_refs, w_refs = refs[:8], refs[8:10]
    (
        normed_ref,
        w_ref,
        qkv_ref,
        out_ref,
        out_t_ref,
        log_ref,
        vec_ref,
        ubias_ref,
        q_ref,
        k_ref,
        v_t_ref,
        normed_buf,
        sems,
    ) = refs[10:]
    blocks, rows, width = out_ref.shape
    length = blocks * rows
    heads = width // HEAD_DIM
    part = w_ref.shape[0] // 4
    own = spots_ref[SPOT_OWN]
    for at in range(4):
        source = spots_ref[SPOT_SWAP + at]
        piece = w_refs[at % 2].at[at // 2]
        place = rows_at(source, part)
        for column in range(3):
            w_ref[place, column * width : (column + 1) * width] = piece[
                column * part : (column + 1) * part, :
            ]
        for half in range(2):
            first = 3 * part + 16 * half
            vec_ref[:, lanes_at(source * 2 + half, width)] = piece[
                first : first + 16, :
            ].astype(F32)
    for at in range(4):
        rows_here = vec_ref[8:16, lanes_at(at * 2 + lax.rem(own, 2), width)]
        chosen = lax.broadcasted_iota(jnp.int32, (8, width), 0) == own // 2
        ubias_ref[:, at * width : (at + 1) * width] = jnp.sum(
            jnp.where(chosen, rows_here, 0.0), 0, keepdims=True
        )
    qbias, vbias = (vec_ref[at : at + 1, lanes_at(own, width)] for at in (2, 3))
    bias = jnp.concatenate([qbias, jnp.zeros((1, width), F32), vbias], 1)
    gain, shift = vec_ref[0:1, :], vec_ref[1:2, :]
    copies = []
    for block in range(blocks):
        place = rows_at(spots_ref[SPOT_CTX + block], rows)
        normed = (normalize(x_refs[block][...].astype(F32)) * gain + shift).astype(BF16)
        normed_buf[block] = normed
        copies.append(
            pltpu.make_async_copy(normed_buf.at[block], normed_ref.at[place, :], sems.at[block])
        )
        copies[-1].start()
        qkv = (times(normed, w_ref[...]) + bias).astype(BF16)
        qkv_ref[place, :] = qkv
        for head in range(heads):
            low, high = head * HEAD_DIM, (head + 1) * HEAD_DIM
            q_ref[head, place, :] = qkv[:, low:high]
            k_ref[head, place, :] = qkv[:, width + low : width + high]
        v_t_ref[:, place] = qkv[:, 2 * width :].T
    for q_tile in range(length // tile):
        columns = slice(q_tile * tile, (q_tile + 1) * tile)
        queries = [q_ref[head, columns, :] for head in range(heads)]

        def visit(k_tile, state, masked):
            start = k_tile * tile
            result = []
            for head in range(heads):
                run_max, run_sum, run_acc = state[head]
                scores = times_trans(k_ref[head, pl.ds(start, tile), :], queries[head])
                if masked:
                    scores = jnp.where(causal(tile, tile), scores, MASKED)
                new_max = jnp.maximum(run_max, jnp.max(scores, 0, keepdims=True))
                weights = jnp.exp2(scores * EXP2_SCALE - new_max * EXP2_SCALE)
                factor = jnp.exp2((run_max - new_max) * EXP2_SCALE)
                new_sum = run_sum * factor + jnp.sum(weights, 0, keepdims=True)
                low, high = head * HEAD_DIM, (head + 1) * HEAD_DIM
                values = v_t_ref[low:high, pl.ds(start, tile)]
                new_acc = run_acc * factor + times(values, weights.astype(BF16))
                result.append((new_max, new_sum, new_acc))
            return result

        state = [
            (
                jnp.full((1, tile), MASKED, F32),
                jnp.zeros((1, tile), F32),
                jnp.zeros((HEAD_DIM, tile), F32),
            )
        ] * heads
        for k_tile in range(q_tile):
            state = visit(k_tile, state, False)
        state = visit(q_tile, state, True)
        result = []
        for head in range(heads):
            run_max, run_sum, run_acc = state[head]
            result.append(run_acc / run_sum)
            log_ref[head : head + 1, columns] = run_max * EXP2_SCALE + jnp.log2(run_sum)
        result = jnp.concatenate(result, 0)
        out_t_ref[:, columns] = result
        result = result.T.astype(BF16)
        for at in range(tile // rows):
            out_ref[q_tile * (tile // rows) + at] = result[at * rows : (at + 1) * rows]
    for copy in copies:
        copy.wait()


def mix_kernel(spots_ref, x_ref, vec_ref, attn_ref, *refs):
    joined_refs, (resid_ref, m_ref, proj_ref, attn_low_ref, sems) = refs[:8], refs[8:]
    blocks, rows, width = attn_ref.shape
    share = proj_ref.shape[0] // 4 // blocks
    copies = []
    for at in range(blocks):
        for source in range(4):
            place = spots_ref[SPOT_SWAP + source] * blocks + spots_ref[SPOT_CTX + at]
            first = rows + source * share
            copies.append(
                pltpu.make_async_copy(
                    joined_refs[at].at[first : first + share, :],
                    proj_ref.at[rows_at(place, share), :],
                    sems.at[at * 4 + source],
                )
            )
            copies[-1].start()
        attn_low_ref[:, at * width : (at + 1) * width] = attn_ref[at]
    for copy in copies:
        copy.wait()
    resid = x_ref[...].astype(F32) + times(attn_low_ref[...], proj_ref[...]) + vec_ref[4:5, :]
    resid_ref[...] = resid
    m_ref[...] = (normalize(resid) * vec_ref[5:6, :] + vec_ref[6:7, :]).astype(BF16)


def norm_back(values, grad, gain):
    center = values - jnp.mean(values, -1, keepdims=True)
    scale = lax.rsqrt(jnp.mean(center * center, -1, keepdims=True) + EPSILON)
    unit = center * scale
    grad_unit = grad * gain
    inner = jnp.mean(grad_unit * unit, -1, keepdims=True)
    return unit, scale * (grad_unit - jnp.mean(grad_unit, -1, keepdims=True) - unit * inner)


def add_parts(refs):
    total = refs[0][...].astype(F32)
    for ref in refs[1:]:
        total = total + ref[...].astype(F32)
    return total


def mix_back_kernel(spots_ref, dy_ref, resid_ref, vec_ref, proj_ref, attn_ref, *refs):
    part_refs, (d_resid_ref, d_attn_ref, sum_ref, kept_ref, sent_ref, full_ref) = refs[:5], refs[5:]
    blocks, rows, width = d_attn_ref.shape
    grad = add_parts(part_refs)
    dy = dy_ref[...].astype(F32)
    unit, d_values = norm_back(resid_ref[...], grad, vec_ref[5:6, :])
    d_resid = dy + d_values
    d_resid_ref[...] = d_resid
    d_branch = d_resid.astype(BF16)
    for at in range(blocks):
        d_attn_ref[at] = times_trans(
            d_branch, proj_ref[at * width : (at + 1) * width, :]
        ).astype(BF16)
    sums = [d_branch.astype(F32), grad * unit, grad, dy]
    sums = [jnp.sum(item, 0, keepdims=True) for item in sums]
    sum_ref[...] = jnp.concatenate(sums + [jnp.zeros((4, sum_ref.shape[1]), F32)], 0)
    full_ref[...] = contract_rows(attn_ref[...], d_branch).astype(BF16)
    share = full_ref.shape[0] // 4 // blocks
    for block in range(blocks):
        out = sent_ref if block % 2 else kept_ref
        for at in range(4):
            place = at * blocks + spots_ref[SPOT_CTX + block]
            out[block // 2, at * share : (at + 1) * share, :] = full_ref[rows_at(place, share), :]


def feed_fast_kernel(spots_ref, *refs):
    m_refs, dy_refs, w_refs, bias_ref = refs[:8], refs[8:16], refs[16:18], refs[18]
    kept_ref, sent_ref, y_kept_ref, y_sent_ref, w_kept_ref, w_sent_ref, sum_ref = refs[19:26]
    (
        down_ref,
        up_ref,
        m_buf,
        dy_buf,
        out_buf,
        hidden_ref,
        d_pre_ref,
        in_sems,
        out_sems,
    ) = refs[26:]
    length, model_dim = m_buf.shape
    rows = length // 8
    hidden = up_ref.shape[1]
    part, share = model_dim // 4, hidden // 4
    for block in range(8):
        here = slice(block * rows, (block + 1) * rows)
        pltpu.make_async_copy(m_refs[block], m_buf.at[here, :], in_sems.at[2 * block]).start()
        pltpu.make_async_copy(
            dy_refs[block].at[:rows, :], dy_buf.at[here, :], in_sems.at[2 * block + 1]
        ).start()
    for at in range(4):
        source = spots_ref[SPOT_SWAP + at]
        piece = w_refs[at % 2].at[at // 2]
        up_ref[rows_at(source, part), :] = piece[:part, :]
        for cut in range(model_dim // hidden):
            first = part + cut * share
            down_ref[rows_at(source, share), cut * hidden : (cut + 1) * hidden] = piece[
                first : first + share, :
            ]
    sum_ref[...] = jnp.zeros_like(sum_ref)
    outs = ((kept_ref, y_kept_ref), (sent_ref, y_sent_ref))

    def send(pair, side):
        block = 2 * pair + side
        return pltpu.make_async_copy(out_buf.at[block], outs[side][0].at[pair], out_sems.at[block])

    @pl.loop(0, 4)
    def _(pair):
        for side in range(2):
            block = 2 * pair + side
            here = rows_at(block, rows)
            for at, buf in enumerate((m_buf, dy_buf)):
                pltpu.make_async_copy(
                    buf.at[here, :], buf.at[here, :], in_sems.at[2 * block + at]
                ).wait()
            pre_act = times(m_buf[here, :], up_ref[...]) + bias_ref[...]
            d_hidden = times_trans(dy_buf[here, :], down_ref[...])
            square = pre_act * pre_act
            bent = jnp.tanh(GELU_COEF * (pre_act + 0.044715 * (square * pre_act)))
            half_one = 0.5 + 0.5 * bent
            hidden_low = (pre_act * half_one).astype(BF16)
            hidden_ref[here, :] = hidden_low
            slope = half_one + (0.5 * pre_act) * (1.0 - bent * bent) * (
                GELU_COEF + (3.0 * 0.044715 * GELU_COEF) * square
            )
            d_pre = (d_hidden * slope).astype(BF16)
            d_pre_ref[here, :] = d_pre
            sum_ref[...] += jnp.sum(d_pre.astype(F32), 0, keepdims=True)
            out_buf[block] = times_trans(d_pre, up_ref[...]).astype(BF16)
            send(pair, side).start()
            outs[side][1][pair] = times(hidden_low, down_ref[...]).astype(BF16)

    @pl.loop(0, 2)
    def _(pair):
        for side, out in enumerate((w_kept_ref, w_sent_ref)):
            place = spots_ref[SPOT_SWAP + 2 * pair + side]
            columns = lanes_at(place, part)
            out[pair, :part, :] = contract_rows(m_buf[:, columns], d_pre_ref[...]).astype(BF16)
            d_down = contract_rows(hidden_ref[:, lanes_at(place, share)], dy_buf[...]).astype(BF16)
            for cut in range(model_dim // hidden):
                first = part + cut * share
                out[pair, first : first + share, :] = d_down[:, cut * hidden : (cut + 1) * hidden]

    for pair in range(4):
        for side in range(2):
            send(pair, side).wait()


def pack_last_kernel(
    spots_ref,
    normed_ref,
    d_qkv_ref,
    d_first_ref,
    d_qkv_sum_ref,
    sum_ref,
    d_ubias_ref,
    *refs,
):
    part_refs, out_refs, (vec_ref, units_ref, proj_ref) = refs[:4], refs[4:6], refs[6:]
    own = spots_ref[SPOT_OWN]
    width = d_qkv_ref.shape[1] // 3
    model_dim = normed_ref.shape[1]
    part = model_dim // 4
    blocks = model_dim // width
    share = part // blocks
    proj_ref[...] = add_parts(part_refs)
    vec_ref[...] = jnp.zeros_like(vec_ref)
    vec_ref[0:2, :] = d_first_ref[...]
    vec_ref[2:3, lanes_at(own, width)] = d_qkv_sum_ref[:, :width]
    vec_ref[3:4, lanes_at(own, width)] = d_qkv_sum_ref[:, 2 * width :]
    vec_ref[4:8, :] = sum_ref[0:4, :]
    for at in range(4):
        place = spots_ref[SPOT_SWAP + at]
        out = out_refs[at % 2].at[at // 2]
        columns = lanes_at(place, part)
        out[:part, : 3 * width] = contract_rows(normed_ref[:, columns], d_qkv_ref[...]).astype(BF16)
        for cut in range(blocks):
            out[cut * share : (cut + 1) * share, 3 * width :] = proj_ref[
                rows_at(place, share), cut * width : (cut + 1) * width
            ].astype(BF16)
        units_ref[...] = jnp.zeros_like(units_ref)
        units_ref[:, lanes_at(own, width)] = d_ubias_ref[:, lanes_at(place, width)]
        vec = [
            jnp.concatenate([vec_ref[2 * row : 2 * row + 1, columns], vec_ref[2 * row + 1 : 2 * row + 2, columns]], 1)
            for row in range(4)
        ]
        vec = vec + [units_ref[:, : 2 * part], units_ref[:, 2 * part :]]
        vec = jnp.concatenate(vec + [jnp.zeros((10, 4 * width), F32)], 0)
        out[part:, :] = vec.astype(BF16)


def place_last_kernel(spots_ref, *refs):
    piece_refs, (qkv_ref, proj_ref), vec_refs = refs[:8], refs[8:10], refs[10:]
    part, width = qkv_ref.shape[0], qkv_ref.shape[1] // 24
    share = part // 8
    for at in range(8):
        place = spots_ref[SPOT_CTX + at]
        for cut in range(3):
            qkv_ref[:, lanes_at(cut * 8 + place, width)] = piece_refs[at][
                :part, cut * width : (cut + 1) * width
            ].astype(F32)
        for cut in range(8):
            proj_ref[rows_at(place, share), cut * width : (cut + 1) * width] = piece_refs[at][
                cut * share : (cut + 1) * share, 3 * width :
            ].astype(F32)
    vec = piece_refs[0][part:, :].astype(F32)
    for at in range(1, 8):
        vec = vec + piece_refs[at][part:, :].astype(F32)
    for at in range(8):
        vec_refs[at][...] = vec[at // 2 : at // 2 + 1, (at % 2) * part : (at % 2 + 1) * part]
    vec_refs[8][...] = jnp.concatenate([vec[4:5], vec[5:6]], 1)


def input_grad_kernel(x_ref, d_resid_ref, vec_ref, *refs):
    unit, d_values = norm_back(x_ref[...].astype(F32), add_parts(refs[:-1]), vec_ref[0:1, :])
    refs[-1][...] = d_resid_ref[...] + d_values


def scatter_pairs(kept, sent):
    swapped = ctx_swap(sent, 1)
    return [kept[0], swapped[0]], [kept[step] + swapped[step] for step in (1, 2, 3)]


def scatter_half(pairs):
    by_x, by_y, diag = pairs
    half = by_x.shape[0] // 2
    sent_x = ctx_swap(jnp.concatenate([by_x[:half], diag[:half]]), 2)
    return sent_x, ctx_swap(jnp.concatenate([by_y[half:], diag[half:]]), 4)


def scatter_other(own, pairs, from_x, from_y):
    by_x, by_y, _ = pairs
    half = by_x.shape[0] // 2
    rest = ctx_swap(by_y[:half] + from_x[half:], 4), ctx_swap(by_x[half:] + from_y[half:], 2)
    return own + [jnp.concatenate([from_x[:half], from_y[:half]]), jnp.concatenate(rest)]


def scatter_rest(own, pairs):
    return own + [ctx_swap(pair, 2 * (at + 1)) for at, pair in enumerate(pairs)]


def gather_direct(block):
    return ctx_swap(block, 2), ctx_swap(block, 4), ctx_swap(block, 6)


def gather_pairs(block, near):
    parts = [block] + list(near)
    return [item for part in parts for item in (part, ctx_swap(part, 1))]


def gather_near(block):
    return ctx_swap(block, 2), ctx_swap(block, 4), ctx_swap(block, 1)


def gather_far(block, near, ready=()):
    by_x, by_y, own_pair = near
    half = block.shape[0] // 2
    diag = jnp.concatenate([ctx_swap(by_y[:half], 2), ctx_swap(by_x[half:], 4)])
    pair_x = ctx_swap(by_x, 1)
    pair_y = ctx_swap(by_y, 1)
    return [block, own_pair, by_x, pair_x, by_y, pair_y, diag, ctx_swap(tie(diag, *ready), 1)]


def shards_fast(
    block_in,
    out_grad,
    ln1_gain,
    ln1_shift,
    qkv_weight,
    query_bias,
    value_bias,
    proj_weight,
    proj_bias,
    ln2_gain,
    ln2_shift,
    up_weight,
    up_bias,
    down_weight,
    down_bias,
):
    seq_count, rows, model_dim = block_in.shape
    length = 8 * rows
    width, part = model_dim // 8, model_dim // 4
    units = up_bias.shape[0]
    hidden = units // 2
    heads = width // HEAD_DIM
    own, here = lax.axis_index("ctx"), lax.axis_index("fsdp")
    eight, four = jnp.arange(8, dtype=jnp.int32), jnp.arange(4, dtype=jnp.int32)
    spots = jnp.concatenate(
        [own[None], eight ^ own, lax.rem(here - four + 4, 4), four ^ here]
    ).astype(jnp.int32)
    x = block_in.reshape(rows, model_dim)
    dy = out_grad.reshape(rows, model_dim)
    token = (rows, model_dim)
    half = ((4,) + token, BF16)

    x_near = gather_direct(x)
    vectors = [ln1_gain, ln1_shift, query_bias, value_bias, proj_bias, ln2_gain, ln2_shift]
    vectors = sum(
        jnp.pad(item.astype(F32), (at * part, 16 * part - at * part - item.shape[0]))
        for at, item in enumerate(vectors + [down_bias, up_bias])
    )
    (first,) = call(
        pack_first_kernel,
        "pack_first",
        [((4 * part + 32, width), BF16)],
        [SMEM] + [ANY] * 2 + [VMEM],
        [pltpu.VMEM((part // 8, model_dim), BF16), pltpu.SemaphoreType.DMA((4,))],
        cost=1,
    )(spots, qkv_weight, proj_weight, vectors)
    (second,) = call(
        pack_second_kernel,
        "pack_second",
        [((2 * part, hidden), BF16)],
        [SMEM] + [ANY] * 2,
        [pltpu.SemaphoreType.DMA((6,))],
        cost=1,
    )(spots, up_weight, tie(down_weight, first))
    first = jnp.stack([first, depth_swap(first, 2)])
    first = (first, depth_swap(first, 1))
    x_parts = gather_pairs(x, x_near)
    proj_slices = [first[at % 2][at // 2, 3 * part + 32 :] for at in range(4)]
    proj_slices = jnp.stack(proj_slices).reshape(4, 8, part // 8, width).transpose(0, 2, 1, 3)
    joined = jnp.concatenate([dy, proj_slices.reshape(part // 2, model_dim)])
    joined_near = gather_direct(joined)
    second_far = depth_swap(tie(second, first[1]), 2)

    normed, qkv_full, qkv, attn, attn_trans, log_total, vec, ubias = call(
        functools.partial(attend_fast_kernel, 512),
        "attend",
        [
            ((length, model_dim), BF16),
            ((model_dim, 3 * width), BF16),
            ((length, 3 * width), BF16),
            ((8, rows, width), BF16),
            ((width, length), F32),
            ((heads, length), F32),
            ((16, model_dim), F32),
            ((1, hidden), F32),
        ],
        [SMEM] + [VMEM] * 10,
        [
            pltpu.VMEM((heads, length, HEAD_DIM), BF16),
            pltpu.VMEM((heads, length, HEAD_DIM), BF16),
            pltpu.VMEM((width, length), BF16),
            pltpu.VMEM((8,) + token, BF16),
            pltpu.SemaphoreType.DMA((8,)),
        ],
        [ANY] + [VMEM] * 7,
        limit=58,
        cost=20,
    )(spots, *x_parts, *first)
    attn, second_far = lax.optimization_barrier((attn, second_far))
    second_pair = jnp.stack([second, second_far])
    attn = lax.all_to_all(tie(attn, second_pair), "ctx", 0, 0, tiled=False)
    attn, *joined_near = lax.optimization_barrier((attn,) + joined_near)
    second_pair = (second_pair, depth_swap(second_pair, 1))
    joined = gather_pairs(joined, joined_near)
    resid, m, proj_full, attn_low = call(
        mix_kernel,
        "mix",
        [(token, F32), (token, BF16), ((model_dim, model_dim), BF16), (token, BF16)],
        [SMEM] + [VMEM] * 3 + [ANY] * 8,
        [pltpu.SemaphoreType.DMA((32,))],
    )(spots, x, vec, attn, *joined)
    m_near = gather_near(m)
    *m_near, second_rest = lax.optimization_barrier(m_near + second_pair[1:])
    second_pair = (second_pair[0], second_rest)
    m_parts = gather_far(m, m_near)

    kept, sent, y_kept, y_sent, w_kept, w_sent, d_ubias = call(
        feed_fast_kernel,
        "feed",
        [half] * 4 + [((2, 2 * part, hidden), BF16)] * 2 + [((1, hidden), F32)],
        [SMEM] + [ANY] * 16 + [VMEM] * 3,
        [
            pltpu.VMEM((hidden, model_dim), BF16),
            pltpu.VMEM((model_dim, hidden), BF16),
            pltpu.VMEM((length, model_dim), BF16),
            pltpu.VMEM((length, model_dim), BF16),
            pltpu.VMEM((8,) + token, BF16),
            pltpu.VMEM((length, hidden), BF16),
            pltpu.VMEM((length, hidden), BF16),
            pltpu.SemaphoreType.DMA((16,)),
            pltpu.SemaphoreType.DMA((8,)),
        ],
        [ANY] * 2 + [VMEM] * 5,
        limit=40,
        cost=20,
    )(spots, *m_parts, *joined, *second_pair, ubias)
    w_swapped = depth_swap(w_sent, 1)
    mine, pairs = scatter_pairs(kept, sent)
    d_m_parts = scatter_rest(mine, pairs)
    y_mine, y_pairs = scatter_pairs(y_kept, y_sent)

    proj_half = ((4, part // 2, model_dim), BF16)
    w_pair = (w_kept.astype(F32) + w_swapped.astype(F32)).astype(BF16)
    w_far = depth_swap(w_pair[1], 2)
    d_resid, d_attn, sums, proj_kept, proj_sent = call(
        mix_back_kernel,
        "mix_back",
        [(token, F32), ((8, rows, width), BF16), ((8, model_dim), F32), proj_half, proj_half],
        [SMEM] + [VMEM] * 10,
        [pltpu.VMEM((model_dim, model_dim), BF16)],
        after=[w_pair, y_pairs[0]],
        cost=0,
    )(spots, dy, resid, vec, proj_full, attn_low, *d_m_parts)
    y_parts = scatter_other(y_mine, y_pairs, *scatter_half(y_pairs))
    proj_mine, proj_pairs = scatter_pairs(proj_kept, proj_sent)
    d_attn = lax.all_to_all(d_attn, "ctx", 0, 0, tiled=False)
    d_attn = lax.optimization_barrier((d_attn,) + tuple(y_parts[2:]))[0]
    proj_halves = scatter_half(proj_pairs)

    d_qkv, kept, sent, d_qkv_sum = attend_grad(
        spots[SPOT_CTX : SPOT_CTX + 8],
        qkv,
        d_attn,
        attn_trans,
        log_total,
        qkv_full,
    )
    sent, w_far, *travelled = lax.optimization_barrier((sent, w_far) + proj_halves)
    proj_parts = scatter_other(proj_mine, proj_pairs, *travelled)
    d_feed = (w_pair[0].astype(F32) + w_far.astype(F32)).astype(BF16)
    feed_near = gather_near(d_feed)
    mine, pairs = scatter_pairs(kept, sent)
    d_x_halves = scatter_half(pairs)
    d_first = first_sums(x_parts, kept, sent)
    last = call(
        pack_last_kernel,
        "pack_last",
        [((2, part + 16, 4 * width), BF16)] * 2,
        [SMEM] + [VMEM] * 10,
        [
            pltpu.VMEM((8, model_dim), F32),
            pltpu.VMEM((1, units), F32),
            pltpu.VMEM((part // 2, model_dim), F32),
        ],
        cost=0,
    )(spots, normed, d_qkv, d_first, d_qkv_sum, sums, d_ubias, *proj_parts)
    last_swapped = depth_swap(last[1], 1)
    last_swapped, *travelled = lax.optimization_barrier(
        (last_swapped,) + d_x_halves + feed_near[:2]
    )
    last = (last[0].astype(F32) + last_swapped.astype(F32)).astype(BF16)
    last_far = depth_swap(last[1], 2)
    d_x_parts = scatter_other(mine, pairs, *travelled[:2])
    last_far = lax.optimization_barrier((last_far,) + tuple(d_x_parts[3:]))[0]
    feed_parts = gather_far(d_feed, (travelled[2], travelled[3], feed_near[2]), [last_far])
    final_sum = sum(item.astype(F32) for item in y_parts)
    block_out = (resid + final_sum + vec[7]).astype(BF16)
    d_up, d_down = place_feed(
        spots[SPOT_CTX : SPOT_CTX + 8], feed_parts, part, model_dim, units, 4
    )
    last = (last[0].astype(F32) + last_far.astype(F32)).astype(BF16)
    (d_input,) = call(
        input_grad_kernel, "input_grad", [(token, F32)], [VMEM] * 7, cost=1
    )(x, d_resid, vec, *d_x_parts)
    last_near = lax.optimization_barrier(gather_direct(last) + (d_input, block_out))[:3]
    last = gather_pairs(last, last_near)
    placed = call(
        place_last_kernel,
        "place_last",
        [((part, 3 * model_dim), F32), ((part, model_dim), F32)]
        + [((1, part), F32)] * 8
        + [((1, units), F32)],
        [SMEM] + [VMEM] * 8,
    )(spots, *last)
    d_weight_qkv, d_proj = placed[:2]
    d_vec = [item.reshape(-1) for item in placed[2:]]
    return (
        block_out.reshape(block_in.shape),
        d_input.reshape(block_in.shape),
        d_vec[0],
        d_vec[1],
        d_weight_qkv,
        d_vec[2],
        d_vec[3],
        d_proj,
        d_vec[4],
        d_vec[5],
        d_vec[6],
        d_up,
        d_vec[8],
        d_down,
        d_vec[7],
    )


def solution(mesh):
    rows, matrix, vector = P("fsdp", "ctx", None), P("fsdp", None), P("fsdp")
    in_specs = (
        rows,
        rows,
        vector,
        vector,
        matrix,
        vector,
        vector,
        matrix,
        vector,
        vector,
        vector,
        matrix,
        vector,
        matrix,
        vector,
    )
    out_specs = (rows, rows) + in_specs[2:]
    fast = mesh.shape["ctx"] == 8 and mesh.shape["fsdp"] == 4
    shards = shards_fast if fast else shards_any
    return jax.shard_map(shards, mesh=mesh, in_specs=in_specs, out_specs=out_specs, check_vma=False)
```
